32 devices in a mesh: dir: 2 (over x), dp: 16 (over z, y, core).
Axes of the slice: x: 2, y: 2, z: 4, core: 2. Of those that a mesh axis runs over, the one named last changes fastest.
Arguments:
- tokens: bfloat16 [2048, 1536], P('dp'), may hold values from -6 to 6
- item_grids: int32 [32, 2], P('dp'), may hold values from 0 to 16, as said below
- norm_gain: bfloat16 [1536], P('dp'), may hold values from 0.099609375 to 1.8984375
- proj_in_x: bfloat16 [1536, 3072], P(None, 'dp'), may hold values from -0.15625 to 0.15625
- proj_in_z: bfloat16 [1536, 3072], P(None, 'dp'), may hold values from -0.15625 to 0.15625
- proj_out: bfloat16 [3072, 1536], P(None, 'dp'), may hold values from -0.109375 to 0.109375
- conv_weight: bfloat16 [2, 4, 3072], P('dir', None, 'dp'), may hold values from -3 to 3
- conv_bias: bfloat16 [2, 3072], P('dir', 'dp'), may hold values from -0.5 to 0.5
- proj_state: bfloat16 [2, 3072, 128], P('dir', 'dp'), may hold values from -0.109375 to 0.109375
- proj_step: bfloat16 [2, 96, 3072], P('dir', None, 'dp'), may hold values from -0.625 to 0.625
- step_bias: bfloat16 [2, 3072], P('dir', 'dp'), may hold values from -4 to -1
- decay_log: bfloat16 [2, 16, 3072], P('dir', None, 'dp'), may hold values from 0 to 2.796875
- skip_gain: bfloat16 [2, 3072], P('dir', 'dp'), may hold values from 0.5 to 1.5
- grad_out: bfloat16 [16, 2, 64, 1536], P('dp', 'dir'), may hold values from -6 to 6
Outputs:
- mixed: bfloat16 [16, 2, 64, 1536], P('dp', 'dir')
- grad_tokens: float32 [16, 2, 64, 1536], P('dp', 'dir')
- grad_norm_gain: float32 [1536], P(('dir', 'dp'))
- grad_proj_in_x: float32 [1536, 3072], P('dir', 'dp')
- grad_proj_in_z: float32 [1536, 3072], P('dir', 'dp')
- grad_proj_out: float32 [3072, 1536], P('dir', 'dp')
- grad_conv_weight: float32 [2, 4, 3072], P('dir', None, 'dp')
- grad_conv_bias: float32 [2, 3072], P('dir', 'dp')
- grad_proj_state: float32 [2, 3072, 128], P('dir', 'dp')
- grad_proj_step: float32 [2, 96, 3072], P('dir', None, 'dp')
- grad_step_bias: float32 [2, 3072], P('dir', 'dp')
- grad_decay_log: float32 [2, 16, 3072], P('dir', None, 'dp')
- grad_skip_gain: float32 [2, 3072], P('dir', 'dp')
The draws below stay inside these ranges and needn't reach their ends.
Inputs may be any that keep to these rules, and one draw needn't show every extreme that they name: `item_grids`: rows 2p and 2p + 1 are the height and width of the items packed in order into the 128 token slots of index p of dp; an unused row is (0, 0); the lengths of a pack add up to at most 128, and some pack is filled completely.
All inputs are finite; a program needn't handle non-finite values.
Results may differ from the reference program's by a relative error of at most 0.013.
Values may be sent and summed in bfloat16 or wider, within the bound.
A program may use at most 320 MiB of HBM per device.

```python
from functools import partial
import jax
import jax.numpy as jnp
from jax import lax

D = 1536
E = 3072
STATE = 16
DT_RANK = 96
CONV = 4
TOK_DEV = 128
BLOCK = 32
HALF = 64
PROJ = 128
TOKENS = 2048
N_DP = 16


def draw_item_grids(key, part):
    key = jax.random.fold_in(key, 7)
    keys = jax.random.split(key, 3)
    devices = TOKENS // TOK_DEV
    pattern = jax.random.randint(keys[0], (devices,), 0, 3)
    pattern = jnp.where(jnp.arange(devices) == 0, 0, pattern)
    full_rows = TOK_DEV // 16
    first_rows = jax.random.randint(keys[1], (devices,), 1, full_rows + 1)
    second_top = jnp.minimum(full_rows, (TOK_DEV - 8 * first_rows) // 8)
    second_rows = jax.random.randint(keys[2], (devices,), 1, second_top + 1)
    first_height = jnp.where(pattern == 0, full_rows, jnp.where(pattern == 1, 16, first_rows))
    first_width = jnp.where(pattern == 0, 16, jnp.where(pattern == 1, full_rows, 8))
    second_height = jnp.where(pattern == 2, second_rows, 0)
    second_width = jnp.where(pattern == 2, 8, 0)
    first_item = jnp.stack([first_height, first_width], 1)
    second_item = jnp.stack([second_height, second_width], 1)
    return jnp.stack([first_item, second_item], 1).reshape(devices * 2, 2).astype(jnp.int32)


def steps_of(rng, dims, cuts, smallest, top_value):
    level = 1.0
    for dim, blocks in cuts:
        heights = jax.random.uniform(jax.random.fold_in(jax.random.fold_in(rng, 6), dim), (blocks,), jnp.float32, smallest / len(cuts), top_value / len(cuts))
        level = level * jnp.repeat(jnp.exp(heights), dims[dim] // blocks).reshape((-1,) + (1,) * (len(dims) - 1 - dim))
    return level


def bell_draw(key, shape, width, reach, shards=(), kind=jnp.bfloat16):
    level = steps_of(key, shape, shards, -0.22, 0.18) if shards else 1.0
    drawn = jax.random.normal(key, shape, jnp.float32) * width * level
    return jnp.minimum(jnp.maximum(drawn, -reach), reach).astype(kind)


def setup_inputs(seed: int = 0) -> dict:
    splits = jax.random.split(jax.random.key(seed), 15)
    tokens = bell_draw(splits[0], (TOKENS, D), 1.0, 6.0, ((0, 16),))
    item_grids = draw_item_grids(jax.random.fold_in(splits[14], 71), 0)
    norm_gain = jnp.clip(1.0 + 0.18 * jax.random.normal(splits[2], (D,), jnp.float32), 0.099609375, 1.8984375).astype(jnp.bfloat16)
    proj_in_x = bell_draw(splits[3], (D, E), D ** -0.5, 0.15625, ((1, 16),))
    proj_in_z = bell_draw(splits[4], (D, E), D ** -0.5, 0.15625, ((1, 16),))
    proj_out = bell_draw(splits[5], (E, D), E ** -0.5, 0.109375, ((1, 16),))
    conv_weight = bell_draw(splits[6], (2, CONV, E), CONV ** -0.5, 3.0, ((0, 2), (2, 16)))
    conv_bias = jnp.clip(jax.random.uniform(splits[7], (2, E), jnp.float32, -0.5, 0.5) * steps_of(splits[7], (2, E), ((0, 2), (1, 16)), -0.4, 0.0), -0.5, 0.5).astype(jnp.bfloat16)
    proj_state = bell_draw(splits[8], (2, E, PROJ), E ** -0.5, 0.109375, ((0, 2), (1, 16)))
    proj_step = bell_draw(splits[9], (2, DT_RANK, E), DT_RANK ** -0.5, 0.625, ((0, 2), (2, 16)))
    step_bias = jnp.clip(-4.0 + 3.0 * jax.random.uniform(splits[10], (2, E), jnp.float32) ** steps_of(splits[10], (2, E), ((0, 2), (1, 16)), -0.2, 0.2), -4.0, -1.0).astype(jnp.bfloat16)
    decay_log = jnp.clip(2.796875 * jax.random.uniform(splits[11], (2, STATE, E), jnp.float32) ** steps_of(splits[11], (2, STATE, E), ((0, 2), (2, 16)), -0.2, 0.2), 0.0, 2.796875).astype(jnp.bfloat16)
    skip_gain = jnp.clip(0.5 + 1.0 * jax.random.uniform(splits[12], (2, E), jnp.float32) ** steps_of(splits[12], (2, E), ((0, 2), (1, 16)), -0.2, 0.2), 0.5, 1.5).astype(jnp.bfloat16)
    grad_out = bell_draw(splits[13], (N_DP, 2, HALF, D), 1.0, 6.0, ((0, 16), (1, 2)))
    return dict(tokens=tokens, item_grids=item_grids, norm_gain=norm_gain, proj_in_x=proj_in_x, proj_in_z=proj_in_z, proj_out=proj_out, conv_weight=conv_weight, conv_bias=conv_bias, proj_state=proj_state, proj_step=proj_step, step_bias=step_bias, decay_log=decay_log, skip_gain=skip_gain, grad_out=grad_out)


@jax.custom_vjp
def low(v):
    return lax.optimization_barrier(v.astype(jnp.bfloat16)).astype(jnp.float32)

@jax.custom_vjp
def low_back(v):
    return v

def low_keep(v):
    return (low(v), None)

def low_pass(kept, grad):
    return (grad,)

def back_keep(v):
    return (v, None)

def back_low(kept, grad):
    return (low(grad),)
low.defvjp(low_keep, low_pass)
low_back.defvjp(back_keep, back_low)

def matmul(left, right):
    return jnp.dot(left, right, precision=lax.Precision.HIGHEST, preferred_element_type=jnp.float32)

def segments(grid_rows, length):
    first_end = grid_rows[0, 0] * grid_rows[0, 1]
    second = first_end + grid_rows[1, 0] * grid_rows[1, 1]
    position = jnp.arange(length, dtype=jnp.int32)
    return (position >= first_end).astype(jnp.int32) + (position >= second).astype(jnp.int32)

def carry_mask(segment_ids, dtype):
    matching = (segment_ids[1:] == segment_ids[:-1]).astype(dtype)
    return jnp.concatenate([jnp.zeros((1,), dtype), matching], 0)

def conv_act(conv_in, kernel_rows, kernel_offset, segment_ids):
    kernel_len = kernel_rows.shape[0]
    length = conv_in.shape[0]
    summed = kernel_offset[None, :] + kernel_rows[kernel_len - 1][None, :] * conv_in
    for offset in range(1, kernel_len):
        shifted = jnp.concatenate([jnp.zeros((offset, conv_in.shape[1]), conv_in.dtype), conv_in[:length - offset]], 0)
        earlier_ids = jnp.concatenate([jnp.full((offset,), -1, jnp.int32), segment_ids[:length - offset]], 0)
        matching = (earlier_ids == segment_ids).astype(conv_in.dtype)
        summed = summed + kernel_rows[kernel_len - 1 - offset][None, :] * shifted * matching[:, None]
    return jax.nn.silu(summed)

def combine(earlier, latter):
    return (earlier[0] * latter[0], latter[0] * earlier[1] + latter[1])

def scan_block(decay_rate, state_in, block_data):
    step_size, values, state_io, keep_mask = block_data
    states = decay_rate.shape[0]
    factor = jnp.exp(step_size[:, None, :] * decay_rate[None]) * keep_mask[:, None, None]
    inject = (step_size * values)[:, None, :] * state_io[:, :states, None]
    total_a, total_b = lax.associative_scan(combine, (factor, inject), axis=0)
    hidden = total_a * state_in[None] + total_b
    readout = lax.optimization_barrier(jnp.sum(hidden * state_io[:, states:, None], axis=1))
    return (hidden[-1], readout)

def mixer_scan(values, step_input, state_io, bias_row, log_rate, skip_row, keep_mask, block_len):
    step_size = jax.nn.softplus(step_input + bias_row[None, :])
    decay_rate = -jnp.exp(log_rate)
    length, channels = values.shape
    blocks = length // block_len
    shaped = (step_size.reshape(blocks, block_len, channels), values.reshape(blocks, block_len, channels), state_io.reshape(blocks, block_len, state_io.shape[1]), keep_mask.reshape(blocks, block_len))
    initial = jnp.zeros(decay_rate.shape, values.dtype)
    _, readout = lax.scan(jax.checkpoint(partial(scan_block, decay_rate)), initial, shaped)
    return readout.reshape(length, channels) + skip_row[None, :] * values

def pack_forward(params, inputs, grid_rows):
    gain, weight_x, weight_z, weight_out, kernel, kernel_bias, weight_state, weight_step, bias_step, log_decay, skip_all = params
    length = inputs.shape[0]
    inv_rms = lax.rsqrt(lax.optimization_barrier(jnp.mean(inputs * inputs, axis=1, keepdims=True)) + 1e-05)
    normed = low(inputs * inv_rms * gain[None, :])
    base_ids = segments(grid_rows, length)
    summed = jnp.zeros((length, weight_x.shape[1]), jnp.float32)
    for course in range(2):
        if course == 1:
            normed_dir = jnp.flip(normed, 0)
            segment_ids = jnp.flip(base_ids, 0)
        else:
            normed_dir = normed
            segment_ids = base_ids
        keep_mask = carry_mask(segment_ids, inputs.dtype)
        conv_input = low_back(matmul(normed_dir, weight_x))
        conv_out = low(conv_act(conv_input, kernel[course], kernel_bias[course], segment_ids))
        projected = low_back(matmul(conv_out, weight_state[course]))
        rank_input = low(projected[:, :DT_RANK])
        step_input = low_back(matmul(rank_input, weight_step[course]))
        scan_out = mixer_scan(conv_out, step_input, projected[:, DT_RANK:], bias_step[course], log_decay[course], skip_all[course], keep_mask, BLOCK)
        if course == 1:
            scan_out = jnp.flip(scan_out, 0)
        summed = summed + scan_out
    gate_input = low_back(matmul(normed, weight_z))
    gated = low(summed * jax.nn.silu(gate_input))
    return matmul(gated, weight_out) + inputs

def reference(tokens, item_grids, norm_gain, proj_in_x, proj_in_z, proj_out, conv_weight, conv_bias, proj_state, proj_step, step_bias, decay_log, skip_gain, grad_out):
    params = tuple((item.astype(jnp.float32) for item in (norm_gain, proj_in_x, proj_in_z, proj_out, conv_weight, conv_bias, proj_state, proj_step, step_bias, decay_log, skip_gain)))
    packs = tokens.astype(jnp.float32).reshape(-1, TOK_DEV, D)
    grids = item_grids.reshape(-1, 2, 2)

    def whole(pack_inputs, weights):

        def one_pack(pair):
            return pack_forward(weights, pair[0], pair[1])
        return lax.map(jax.checkpoint(one_pack), (pack_inputs, grids))
    result, backward = jax.vjp(whole, packs, params)
    cotangent = grad_out.astype(jnp.float32).reshape(result.shape)
    grad_inputs, grads = backward(cotangent)
    mixed = result.astype(jnp.bfloat16).reshape(-1, 2, TOK_DEV // 2, D)
    grad_tokens = grad_inputs.reshape(-1, 2, TOK_DEV // 2, D)
    return (mixed, grad_tokens, grads[0], grads[1], grads[2], grads[3], grads[4], grads[5], grads[6], grads[7], grads[8], grads[9], grads[10])
```

```python
from functools import partial

import jax
import jax.numpy as jnp
from jax import lax
from jax.experimental import pallas as pl
from jax.experimental.pallas import tpu as pltpu
from jax.sharding import PartitionSpec as P

f32 = jnp.float32
bf16 = jnp.bfloat16
EPS = 1e-05
DT_RANK = 96
STATE = 16
TAPS = 4
TP = 8
PACK = 128
CHUNK = 16
NSTEP = 4
LOG2E = 1.4426950408889634
LN2 = 0.6931471805599453
BIG = 1e9
PAD = 24


def mm(left, right):
    return jnp.dot(left, right, preferred_element_type=f32)


def mm_nt(left, right):
    return lax.dot_general(left, right, (((1,), (1,)), ((), ())), preferred_element_type=f32)


def mm_tn(left, right):
    return lax.dot_general(left, right, (((0,), (0,)), ((), ())), preferred_element_type=f32)


def segment_of(t, ends):
    return (t >= ends[0]).astype(jnp.int32) + (t >= ends[1]).astype(jnp.int32)


def rows8(t):
    return pl.ds(pl.multiple_of(t * 8, 8), 8)


def sigmoid(v):
    return 1.0 / (1.0 + jnp.exp(-v))


def call(kernel, outs, args, **kw):
    params = dict(vmem_limit_bytes=60 << 20)
    return pl.pallas_call(
        kernel,
        out_shape=outs,
        compiler_params=pltpu.CompilerParams(**params),
        **kw,
    )(*args)


def spaces(args, scalars):
    return [
        pl.BlockSpec(memory_space=pltpu.SMEM if n in scalars else pltpu.VMEM)
        for n in range(len(args))
    ]


def front_kernel(
    dir_ref, ends_ref, tokens, gain, wx, wz, wstate, taps,
    normed, conv_in, conv_pre, conv_out, gate_in, proj,
):
    s = dir_ref[0]
    half = PACK // 2
    sgn = 1 - 2 * s
    conv_in[0:PAD, :] = jnp.zeros((PAD, conv_in.shape[1]), f32)
    conv_in[PAD + 8 * PACK :, :] = jnp.zeros((PAD, conv_in.shape[1]), f32)

    def norm_pack(p, carry):
        rows = pl.ds(pl.multiple_of(p * PACK, PACK), PACK)
        x = tokens[rows, :].astype(f32)
        inv = lax.rsqrt(jnp.mean(x * x, axis=1, keepdims=True) + EPS)
        normed[rows, :] = (x * inv * gain[...]).astype(bf16)
        mine = pl.ds(pl.multiple_of(p * PACK + s * half, half), half)
        gate_in[pl.ds(pl.multiple_of(p * half, half), half), :] = mm(normed[mine, :], wz[...])
        return carry

    lax.fori_loop(0, 8, norm_pack, 0)

    def in_rows(b, carry):
        span = 32
        parts = [normed[pl.ds(pl.multiple_of(p * PACK + b * span, span), span), :] for p in range(8)]
        x = mm(jnp.concatenate(parts, axis=0), wx[...])
        x = jnp.swapaxes(x.reshape(8, span, x.shape[1]), 0, 1).reshape(8 * span, x.shape[1])
        conv_in[pl.ds(pl.multiple_of(PAD + b * span * 8, 8), 8 * span), :] = x
        return carry

    lax.fori_loop(0, PACK // 32, in_rows, 0)
    ends = (ends_ref[0], ends_ref[1])

    def conv_step(t, carry):
        seg = segment_of(t, ends)
        total = taps[4:5, :] + taps[3:4, :] * conv_in[rows8(t + 3), :]
        for j in range(1, TAPS):
            there = t - j * sgn
            same = (segment_of(there, ends) == seg).astype(f32)[:, 0:1]
            total = total + taps[3 - j : 4 - j, :] * (conv_in[rows8(there + 3), :] * same)
        conv_pre[rows8(t), :] = total
        act = total * sigmoid(total)
        conv_out[rows8(t), :] = act.astype(bf16).astype(f32)
        return carry

    lax.fori_loop(0, PACK, conv_step, 0, unroll=2)
    proj[...] = mm(conv_out[...].astype(bf16), wstate[...])


def front(s, ends, tokens, gain, wx, wz, wstate, taps):
    rows, width = tokens.shape
    ch = wx.shape[1]
    args = (s, ends, tokens, gain, wx, wz, wstate, taps)
    outs = (
        jax.ShapeDtypeStruct((rows, width), bf16),
        jax.ShapeDtypeStruct((rows + 2 * PAD, ch), f32),
        jax.ShapeDtypeStruct((rows, ch), f32),
        jax.ShapeDtypeStruct((rows, ch), f32),
        jax.ShapeDtypeStruct((rows // 2, ch), f32),
        jax.ShapeDtypeStruct((rows, 128), f32),
    )
    return call(front_kernel, outs, args, in_specs=spaces(args, (0,)))


def softplus(v):
    return jnp.maximum(v, 0.0) + jnp.log1p(jnp.exp(-jnp.abs(v)))


def scan_kernel(dir_ref, ends_ref, proj, conv_out, wstep, small, decay, y, hprev, step, decay_step, u, state):
    c = pl.program_id(0)
    s = dir_ref[0]
    sgn = 1 - 2 * s
    block = c + s * (pl.num_programs(0) - 1 - 2 * c)
    ch = conv_out.shape[1]
    pre = mm(proj[...].astype(bf16), wstep[...])
    step_all = softplus(pre + small[0:1, :])
    step[...] = step_all
    u[...] = step_all * conv_out[...]
    y[...] = small[1:2, :] * conv_out[...]
    ends = (ends_ref[0], ends_ref[1])

    @pl.when(c == 0)
    def _():
        state[...] = jnp.zeros_like(state)

    for k in range(CHUNK):
        t = block * CHUNK + k
        fresh = (segment_of(t, ends) != segment_of(t - sgn, ends))[:, 0:1]
        decay_step[8 * k : 8 * k + 8, :] = jnp.where(fresh, BIG, step_all[8 * k : 8 * k + 8, :])

    for n0 in range(0, STATE, NSTEP):
        rate = [jnp.broadcast_to(decay[n : n + 1, :], (8, ch)) for n in range(n0, n0 + NSTEP)]

        def body(k, hs):
            r = s * (CHUNK - 1 - k) + (1 - s) * k
            rows = rows8(r)
            pv = proj[rows, :]
            st = decay_step[rows, :]
            uv = u[rows, :]
            acc = y[rows, :]
            new = []
            for m in range(NSTEP):
                n = n0 + m
                hprev[r, n] = hs[m]
                a = jnp.exp2(st * rate[m])
                h = a * hs[m] + uv * pv[:, DT_RANK + n : DT_RANK + n + 1]
                acc = acc + h * pv[:, DT_RANK + STATE + n : DT_RANK + STATE + n + 1]
                new.append(h)
            y[rows, :] = acc
            return tuple(new)

        hs = tuple(state[n] for n in range(n0, n0 + NSTEP))
        hs = lax.fori_loop(0, CHUNK, body, hs, unroll=2)
        for m in range(NSTEP):
            state[n0 + m] = hs[m]


def scan_forward(s, ends, proj, conv_out, wstep, small, decay):
    rows, ch = conv_out.shape
    span = CHUNK * 8
    blocks = rows // span

    def at(c, d):
        return c + d[0] * (blocks - 1 - 2 * c)

    def rowspec(width):
        return pl.BlockSpec((span, width), lambda c, d: (at(c, d), 0))

    def whole(shape):
        return pl.BlockSpec(shape, lambda c, d: (0,) * len(shape))

    return pl.pallas_call(
        scan_kernel,
        grid_spec=pltpu.PrefetchScalarGridSpec(
            num_scalar_prefetch=1,
            grid=(blocks,),
            in_specs=[
                whole(ends.shape), rowspec(128), rowspec(ch), whole(wstep.shape), whole(small.shape), whole(decay.shape),
            ],
            out_specs=(
                rowspec(ch),
                pl.BlockSpec((CHUNK, STATE, 8, ch), lambda c, d: (at(c, d), 0, 0, 0)),
            ),
            scratch_shapes=[
                pltpu.VMEM((span, ch), f32),
                pltpu.VMEM((span, ch), f32),
                pltpu.VMEM((span, ch), f32),
                pltpu.VMEM((STATE, 8, ch), f32),
            ],
        ),
        out_shape=(
            jax.ShapeDtypeStruct((rows, ch), f32),
            jax.ShapeDtypeStruct((rows // 8, STATE, 8, ch), f32),
        ),
        compiler_params=pltpu.CompilerParams(vmem_limit_bytes=60 << 20),
    )(s, ends, proj, conv_out, wstep, small, decay)


def gate_kernel(dir_ref, y, y_other, gate_in, wout, cot, gated, mixed, grad_sum, grad_gate, both, other):
    s = dir_ref[0]
    half = y_other.shape[0]
    steps = half // 8
    ch = y.shape[1]
    both[...] = y[pl.ds(pl.multiple_of(s * half, half), half), :] + y_other[...].astype(f32)
    summed = jnp.swapaxes(both[...].reshape(steps, 8, ch), 0, 1).reshape(half, ch)
    gate = gate_in[...]
    sig = sigmoid(gate)
    act = gate * sig
    g = (summed * act).astype(bf16)
    gated[...] = g
    mixed[...] = mm(g, wout[...]).astype(bf16)
    grad_gated = mm_nt(cot[...], wout[...])
    grad_gate[...] = (grad_gated * summed * sig * (1.0 + gate * (1.0 - sig))).astype(bf16)
    back = grad_gated * act
    other[...] = jnp.swapaxes(back.reshape(8, steps, ch), 0, 1).reshape(half, ch)
    grad_sum[...] = other[...].astype(bf16)


def gate(s, y, y_other, gate_in, wout, cot):
    half, ch = gate_in.shape
    args = (s, y, y_other, gate_in, wout, cot)
    outs = (
        jax.ShapeDtypeStruct((half, ch), bf16),
        jax.ShapeDtypeStruct((half, wout.shape[1]), bf16),
        jax.ShapeDtypeStruct((half, ch), bf16),
        jax.ShapeDtypeStruct((half, ch), bf16),
    )
    return call(
        gate_kernel, outs, args, in_specs=spaces(args, (0,)),
        scratch_shapes=[pltpu.VMEM((half, ch), f32), pltpu.VMEM((half, ch), f32)],
    )


def back_kernel(
    dir_ref, ends_ref, g_low, proj, conv_out, hprev, wstep, small, decay, ones,
    grad_values, grad_proj, grad_wstep, grad_rows, grad_decay,
    g, step, decay_step, u, s1, s2, pb, pc, carry_ref, acc_ref, bias_acc, skip_acc,
):
    c = pl.program_id(0)
    last = pl.num_programs(0) - 1
    s = dir_ref[0]
    sgn = 1 - 2 * s
    block = (last - c) + s * (2 * c - last)
    ch = conv_out.shape[1]
    rank = proj[...].astype(bf16)
    pre = mm(rank, wstep[...]) + small[0:1, :]
    step_all = softplus(pre)
    step[...] = step_all
    g[...] = g_low[...].astype(f32)
    u[...] = step_all * conv_out[...]
    ends = (ends_ref[0], ends_ref[1])

    @pl.when(c == 0)
    def _():
        carry_ref[...] = jnp.zeros_like(carry_ref)
        acc_ref[...] = jnp.zeros_like(acc_ref)
        bias_acc[...] = jnp.zeros_like(bias_acc)
        skip_acc[...] = jnp.zeros_like(skip_acc)
        grad_wstep[...] = jnp.zeros_like(grad_wstep)

    for k in range(CHUNK):
        t = block * CHUNK + k
        fresh = (segment_of(t, ends) != segment_of(t - sgn, ends))[:, 0:1]
        decay_step[8 * k : 8 * k + 8, :] = jnp.where(fresh, BIG, step_all[8 * k : 8 * k + 8, :])
    s1[...] = jnp.zeros_like(s1)
    s2[...] = jnp.zeros_like(s2)

    def tiles(v):
        total = v[:, 0:128]
        for w in range(128, ch, 128):
            total = total + v[:, w : w + 128]
        return total

    for n0 in range(0, STATE, NSTEP):
        rate = [jnp.broadcast_to(decay[n : n + 1, :], (8, ch)) for n in range(n0, n0 + NSTEP)]

        def body(k, state):
            carry, acc = state
            r = s * k + (1 - s) * (CHUNK - 1 - k)
            rows = rows8(r)
            pv = proj[rows, :]
            gv = g[rows, :]
            uv = u[rows, :]
            stv = step[rows, :]
            st = decay_step[rows, :]
            one = s1[rows, :]
            two = s2[rows, :]
            new_carry, new_acc = [], []
            for m in range(NSTEP):
                n = n0 + m
                a = jnp.exp2(st * rate[m])
                ah = a * hprev[r, n]
                lam = gv * pv[:, DT_RANK + STATE + n : DT_RANK + STATE + n + 1] + carry[m]
                w = lam * ah
                new_carry.append(a * lam)
                two = two + rate[m] * w
                new_acc.append(acc[m] + stv * w)
                one = one + lam * pv[:, DT_RANK + n : DT_RANK + n + 1]
                pb[rows, 128 * n : 128 * n + 128] = tiles(lam * uv)
                pc[rows, 128 * n : 128 * n + 128] = tiles(gv * ah)
            s1[rows, :] = one
            s2[rows, :] = two
            return tuple(new_carry), tuple(new_acc)

        first = (
            tuple(carry_ref[n] for n in range(n0, n0 + NSTEP)),
            tuple(acc_ref[n] for n in range(n0, n0 + NSTEP)),
        )
        carry, acc = lax.fori_loop(0, CHUNK, body, first, unroll=2)
        for m in range(NSTEP):
            carry_ref[n0 + m] = carry[m]
            acc_ref[n0 + m] = acc[m]

    values = conv_out[...]
    gv = g[...]
    one = s1[...]
    grad_values[...] = gv * small[1:2, :] + step[...] * one
    q = (LN2 * s2[...] + values * one) * sigmoid(pre)
    low = q.astype(bf16)
    bias_acc[...] += jnp.sum(q.reshape(CHUNK, 8, ch), axis=0)
    skip_acc[...] += jnp.sum((gv * values).reshape(CHUNK, 8, ch), axis=0)
    grad_wstep[...] += mm_tn(rank, low)
    gu = jnp.sum(gv * u[...], axis=1, keepdims=True)
    lane = lax.broadcasted_iota(jnp.int32, (CHUNK * 8, 128), 1)
    inject = jnp.where(lane >= DT_RANK + STATE, pltpu.roll(proj[...], STATE, 1), 0.0)
    grad_proj[...] = (
        mm_nt(low, wstep[...])
        + mm(pb[...].astype(bf16), ones[0])
        + mm(pc[...].astype(bf16), ones[1])
        + gu * inject
    )

    @pl.when(c == last)
    def _():
        grad_rows[0:1, :] = jnp.sum(bias_acc[...], axis=0, keepdims=True)
        grad_rows[1:2, :] = jnp.sum(skip_acc[...], axis=0, keepdims=True)
        for n in range(STATE):
            grad_decay[n : n + 1, :] = jnp.sum(acc_ref[n], axis=0, keepdims=True) * decay[n : n + 1, :] * LN2


def scan_backward(s, ends, g, proj, conv_out, hprev, wstep, small, decay):
    rows, ch = conv_out.shape
    span = CHUNK * 8
    blocks = rows // span

    def at(c, d):
        return (blocks - 1 - c) + d[0] * (2 * c - blocks + 1)

    def rowspec(width):
        return pl.BlockSpec((span, width), lambda c, d: (at(c, d), 0))

    def whole(shape):
        return pl.BlockSpec(shape, lambda c, d: (0,) * len(shape))

    source = lax.broadcasted_iota(jnp.int32, (2, STATE * 128, 128), 1) // 128
    which = lax.broadcasted_iota(jnp.int32, (2, STATE * 128, 128), 0)
    target = lax.broadcasted_iota(jnp.int32, (2, STATE * 128, 128), 2)
    ones = (target == DT_RANK + which * STATE + source).astype(bf16)
    big = pltpu.VMEM((span, ch), f32)
    return pl.pallas_call(
        back_kernel,
        grid_spec=pltpu.PrefetchScalarGridSpec(
            num_scalar_prefetch=1,
            grid=(blocks,),
            in_specs=[
                whole(ends.shape), rowspec(ch), rowspec(128), rowspec(ch),
                pl.BlockSpec((CHUNK, STATE, 8, ch), lambda c, d: (at(c, d), 0, 0, 0)),
                whole(wstep.shape), whole(small.shape), whole(decay.shape), whole(ones.shape),
            ],
            out_specs=(rowspec(ch), rowspec(128), whole((128, ch)), whole((2, ch)), whole((STATE, ch))),
            scratch_shapes=[big] * 6
            + [
                pltpu.VMEM((span, STATE * 128), f32),
                pltpu.VMEM((span, STATE * 128), f32),
                pltpu.VMEM((STATE, 8, ch), f32),
                pltpu.VMEM((STATE, 8, ch), f32),
                pltpu.VMEM((8, ch), f32),
                pltpu.VMEM((8, ch), f32),
            ],
        ),
        out_shape=(
            jax.ShapeDtypeStruct((rows, ch), f32),
            jax.ShapeDtypeStruct((rows, 128), f32),
            jax.ShapeDtypeStruct((128, ch), f32),
            jax.ShapeDtypeStruct((2, ch), f32),
            jax.ShapeDtypeStruct((STATE, ch), f32),
        ),
        compiler_params=pltpu.CompilerParams(vmem_limit_bytes=60 << 20),
    )(s, ends, g, proj, conv_out, hprev, wstep, small, decay, ones)


def conv_back_kernel(
    dir_ref, ends_ref, grad_values, grad_proj, conv_out, conv_pre, conv_in, wstate, taps,
    grad_in, grad_state, grad_taps, w, slots, sums,
):
    s = dir_ref[0]
    sgn = 1 - 2 * s
    ch = conv_out.shape[1]
    low = grad_proj[...].astype(bf16)
    w[0:PAD, :] = jnp.zeros((PAD, ch), f32)
    w[PAD + 8 * PACK :, :] = jnp.zeros((PAD, ch), f32)
    c = conv_pre[...]
    sig = sigmoid(c)
    w[PAD : PAD + 8 * PACK, :] = (grad_values[...] + mm_nt(low, wstate[...])) * (sig * (1.0 + c * (1.0 - sig)))
    grad_state[...] = mm_tn(conv_out[...].astype(bf16), low)
    sums[...] = jnp.zeros_like(sums)
    ends = (ends_ref[0], ends_ref[1])

    def step(t, carry):
        seg = segment_of(t, ends)
        here = w[rows8(t + 3), :]
        total = taps[3:4, :] * here
        sums[3] += here * conv_in[rows8(t + 3), :]
        sums[4] += here
        for j in range(1, TAPS):
            back = t - j * sgn
            ahead = t + j * sgn
            same_back = (segment_of(back, ends) == seg).astype(f32)[:, 0:1]
            same_ahead = (segment_of(ahead, ends) == seg).astype(f32)[:, 0:1]
            sums[3 - j] += here * (conv_in[rows8(back + 3), :] * same_back)
            total = total + taps[3 - j : 4 - j, :] * (w[rows8(ahead + 3), :] * same_ahead)
        slots[rows8(t), :] = total
        return carry

    lax.fori_loop(0, PACK, step, 0, unroll=2)
    for n in range(5):
        grad_taps[n : n + 1, :] = jnp.sum(sums[n], axis=0, keepdims=True)

    def out_rows(b, carry):
        span = 32
        x = slots[pl.ds(pl.multiple_of(b * span * 8, 8), 8 * span), :]
        x = jnp.swapaxes(x.reshape(span, 8, ch), 0, 1).astype(bf16)
        for p in range(8):
            grad_in[pl.ds(pl.multiple_of(p * PACK + b * span, span), span), :] = x[p]
        return carry

    lax.fori_loop(0, PACK // 32, out_rows, 0)


def conv_backward(s, ends, grad_values, grad_proj, conv_out, conv_pre, conv_in, wstate, taps):
    rows, ch = conv_out.shape
    args = (s, ends, grad_values, grad_proj, conv_out, conv_pre, conv_in, wstate, taps)
    outs = (
        jax.ShapeDtypeStruct((rows, ch), bf16),
        jax.ShapeDtypeStruct((ch, 128), f32),
        jax.ShapeDtypeStruct((5, ch), f32),
    )
    return call(
        conv_back_kernel, outs, args, in_specs=spaces(args, (0,)),
        scratch_shapes=[
            pltpu.VMEM((rows + 2 * PAD, ch), f32),
            pltpu.VMEM((rows, ch), f32),
            pltpu.VMEM((5, 8, ch), f32),
        ],
    )


def normed_grad_kernel(grad_x0, grad_x1, grad_z, wx, wz, out):
    rows = out.shape[0] // 4

    def body(b, carry):
        r = pl.ds(pl.multiple_of(b * rows, rows), rows)
        out[r, :] = (
            mm_nt(grad_x0[r, :], wx[...]) + mm_nt(grad_x1[r, :], wx[...]) + mm_nt(grad_z[r, :], wz[...])
        ).astype(bf16)
        return carry

    lax.fori_loop(0, 4, body, 0)


def tail_kernel(dir_ref, mixed_parts, grad_parts, tokens, cot, gain, mixed, grad_tokens, grad_gain):
    half = cot.shape[0]
    x = tokens[pl.ds(pl.multiple_of(dir_ref[0] * half, half), half), :].astype(f32)
    inv = lax.rsqrt(jnp.mean(x * x, axis=1, keepdims=True) + EPS)
    unit = x * inv
    total = x
    grad = jnp.zeros_like(x)
    for j in range(TP):
        total = total + mixed_parts[j].astype(f32)
        grad = grad + grad_parts[j].astype(f32)
    mixed[...] = total.astype(bf16)
    scaled = grad * gain[...]
    mean = jnp.mean(scaled * unit, axis=1, keepdims=True)
    grad_tokens[...] = inv * (scaled - unit * mean) + cot[...].astype(f32)
    grad_gain[...] = jnp.sum(grad * unit, axis=0, keepdims=True)


def local(
    reps, tokens, item_grids, norm_gain, proj_in_x, proj_in_z, proj_out, conv_weight, conv_bias,
    proj_state, proj_step, step_bias, decay_log, skip_gain, grad_out,
):
    share = [[(z * reps + y) * 2 + i for z in range(4) for i in range(2)] for y in range(reps)]
    same = [[(z * reps + y) * 2 + i for y in range(reps)] for z in range(4) for i in range(2)]
    direction = lax.axis_index("dir")
    s = direction.reshape(1).astype(jnp.int32)
    length, width = tokens.shape
    half = length // 2
    cols = proj_in_x.shape[1]
    ch = reps * cols
    outs_dev = proj_out.shape[1]

    def gather(x, groups, axis):
        return lax.all_gather(x, "dp", axis=axis, tiled=True, axis_index_groups=groups)

    def spread(x, groups):
        return lax.all_to_all(x, "dp", 0, 0, axis_index_groups=groups, tiled=False)

    tokens_all = gather(tokens, share, 0)
    grids = gather(item_grids.reshape(1, 2, 2), share, 0)
    gain = lax.all_gather(norm_gain, "dp", axis=0, tiled=True).astype(f32).reshape(1, width)
    lengths = grids[:, :, 0] * grids[:, :, 1]
    ends = jnp.stack([lengths[:, 0], lengths[:, 0] + lengths[:, 1]])
    ends = jnp.broadcast_to(ends[:, :, None], (2, TP, 128))
    wx = gather(proj_in_x, same, 1)
    wz = gather(proj_in_z, same, 1)
    small = jnp.concatenate(
        [conv_weight[0], conv_bias, step_bias, skip_gain, decay_log[0], proj_step[0]], axis=0
    )
    small = gather(small, same, 1)
    wstate = gather(proj_state[0], same, 0)
    taps = small[0:5].astype(f32)
    rows_small = small[5:7].astype(f32)
    decay = -LOG2E * jnp.exp(small[7 : 7 + STATE].astype(f32))
    wstep = jnp.concatenate([small[7 + STATE :], jnp.zeros((128 - DT_RANK, ch), bf16)], axis=0)
    wout = proj_out.reshape(4, reps, 2, cols, outs_dev).transpose(0, 2, 1, 3, 4).reshape(TP, ch, outs_dev)
    wout = spread(wout, share)
    wout = lax.all_gather(wout, "dp", axis=0, axis_index_groups=same)
    wout = wout.reshape(reps, 4, 2, ch, outs_dev).transpose(3, 1, 0, 2, 4).reshape(ch, width)
    cot_own = grad_out.reshape(half, width)
    cot = gather(cot_own, share, 0)

    normed, conv_in, conv_pre, conv_out, gate_in, proj_part = front(
        s, ends, tokens_all, gain, wx, wz, wstate, taps
    )
    proj = lax.psum(proj_part, "dp", axis_index_groups=share)
    y, hprev = scan_forward(s, ends, proj, conv_out, wstep, rows_small, decay)
    swap = [(0, 1), (1, 0)]
    rows_half = y.shape[0] // 2
    y_send = lax.dynamic_slice_in_dim(y, (1 - direction) * rows_half, rows_half, 0).astype(bf16)
    y_other = lax.ppermute(y_send, "dir", swap)
    gated, mixed_part, grad_sum, grad_gate = gate(s, y, y_other, gate_in, wout, cot)
    mixed_parts = spread(mixed_part.reshape(TP, half, width), share)
    grad_sum_other = lax.ppermute(grad_sum, "dir", swap)

    def in_order(own, other):
        first = jnp.where(direction == 0, own, other)
        second = jnp.where(direction == 0, other, own)
        return first, second

    g = jnp.concatenate(in_order(grad_sum, grad_sum_other), axis=0)
    grad_values, grad_proj_part, grad_wstep, grad_rows, grad_decay = scan_backward(
        s, ends, g, proj, conv_out, hprev, wstep, rows_small, decay
    )
    grad_proj = lax.psum(grad_proj_part, "dp", axis_index_groups=share)
    grad_in, grad_state, grad_taps = conv_backward(
        s, ends, grad_values, grad_proj, conv_out, conv_pre, conv_in, wstate, taps
    )
    grad_in_other = lax.ppermute(grad_in, "dir", swap)

    def own_half(x):
        x = x.reshape(TP, length, x.shape[1])
        return lax.dynamic_slice_in_dim(x, direction * half, half, 1).reshape(TP * half, x.shape[2])

    args = (own_half(grad_in), own_half(grad_in_other), grad_gate, wx, wz)
    grad_normed_part = call(
        normed_grad_kernel, jax.ShapeDtypeStruct((TP * half, width), bf16), args, in_specs=spaces(args, ())
    )
    grad_parts = spread(grad_normed_part.reshape(TP, half, width), share)

    grad_gate_other = lax.ppermute(grad_gate, "dir", swap)
    first, second = in_order(grad_gate.reshape(TP, half, ch), grad_gate_other.reshape(TP, half, ch))
    gate_all = jnp.concatenate([first, second], axis=1).reshape(TP * length, ch)
    own_cols = lax.dynamic_slice_in_dim(normed, direction * (width // 2), width // 2, 1)
    part_x = mm_tn(own_cols, grad_in) + mm_tn(own_cols, grad_in_other)
    part_z = mm_tn(own_cols, gate_all)

    def reduce_same(x, axis):
        x = jnp.moveaxis(x.reshape(x.shape[:axis] + (reps, cols) + x.shape[axis + 1 :]), axis, 0)
        return jnp.sum(spread(x, same).astype(f32), axis=0)

    grad_x = reduce_same(part_x.astype(bf16), 1)
    grad_z = reduce_same(part_z.astype(bf16), 1)
    part_out = mm_tn(gated, cot).astype(bf16)
    part_out = part_out.reshape(ch, 4, reps, 2, outs_dev).transpose(2, 1, 3, 0, 4)
    part_out = jnp.sum(spread(part_out, same).astype(f32), axis=0).astype(bf16)
    part_out = spread(part_out.reshape(TP, ch, outs_dev), share)
    part_out = lax.all_to_all(part_out.reshape(2, 4, ch, outs_dev), "dir", 0, 0, tiled=False)
    part_out = jnp.sum(part_out.astype(f32), axis=0)
    grad_out_w = (
        part_out.reshape(2, 2, reps, cols, outs_dev).transpose(0, 2, 1, 3, 4).reshape(4 * ch, outs_dev)
    )
    rows_grad = jnp.concatenate([grad_taps, grad_rows, grad_decay, grad_wstep[:DT_RANK]], axis=0)
    rows_grad = reduce_same(rows_grad, 1)
    state_grad = reduce_same(grad_state, 0)

    args = (s, mixed_parts, grad_parts, tokens, cot_own, gain)
    mixed, grad_tokens, grad_gain = call(
        tail_kernel,
        (
            jax.ShapeDtypeStruct((half, width), bf16),
            jax.ShapeDtypeStruct((half, width), f32),
            jax.ShapeDtypeStruct((1, width), f32),
        ),
        args,
        in_specs=spaces(args, (0,)),
    )
    gain_part = lax.psum_scatter(grad_gain[0], ("dir", "dp"), scatter_dimension=0, tiled=True)
    return (
        mixed.reshape(1, 1, half, width),
        grad_tokens.reshape(1, 1, half, width),
        gain_part,
        grad_x,
        grad_z,
        grad_out_w,
        rows_grad[None, 0:4],
        rows_grad[4:5],
        state_grad[None],
        rows_grad[None, 7 + STATE :],
        rows_grad[5:6],
        rows_grad[None, 7 : 7 + STATE],
        rows_grad[6:7],
    )


def solution(mesh):
    reps = mesh.shape["dp"] // TP
    return jax.shard_map(
        partial(local, reps),
        mesh=mesh,
        in_specs=(
            P("dp", None),
            P("dp", None),
            P("dp"),
            P(None, "dp"),
            P(None, "dp"),
            P(None, "dp"),
            P("dir", None, "dp"),
            P("dir", "dp"),
            P("dir", "dp", None),
            P("dir", None, "dp"),
            P("dir", "dp"),
            P("dir", None, "dp"),
            P("dir", "dp"),
            P("dp", "dir", None, None),
        ),
        out_specs=(
            P("dp", "dir", None, None),
            P("dp", "dir", None, None),
            P(("dir", "dp")),
            P("dir", "dp"),
            P("dir", "dp"),
            P("dir", "dp"),
            P("dir", None, "dp"),
            P("dir", "dp"),
            P("dir", "dp", None),
            P("dir", None, "dp"),
            P("dir", "dp"),
            P("dir", None, "dp"),
            P("dir", "dp"),
        ),
        check_vma=False,
    )
```

```python
from functools import partial

import jax
import jax.numpy as jnp
from jax import lax
from jax.experimental import pallas as pl
from jax.experimental.pallas import tpu as pltpu
from jax.sharding import PartitionSpec as P

f32 = jnp.float32
bf16 = jnp.bfloat16
EPS = 1e-05
DT_RANK = 96
STATE = 16
TAPS = 4
ZS = 4
TP = 8
PACK = 128
HALF = 64
CHUNK = 16
NSTEP = 4
LOG2E = 1.4426950408889634
LN2 = 0.6931471805599453
BIG = 1e9
PAD = 24
TAP_ROW, BIAS_ROW, STEP_ROW, SKIP_ROW, DECAY_ROW, SMALL_ROWS = 96, 100, 101, 102, 103, 128


def mm(left, right):
    return jnp.dot(left, right, preferred_element_type=f32)


def mm_nt(left, right):
    return lax.dot_general(left, right, (((1,), (1,)), ((), ())), preferred_element_type=f32)


def mm_tn(left, right):
    return lax.dot_general(left, right, (((0,), (0,)), ((), ())), preferred_element_type=f32)


def segment_of(t, ends):
    t = t.astype(f32) if hasattr(t, "astype") else float(t)
    return (t >= ends[0]).astype(f32) + (t >= ends[1]).astype(f32)


def rows8(t):
    return pl.ds(pl.multiple_of(t * 8, 8), 8)


def span(start, size):
    return pl.ds(pl.multiple_of(start * size, size), size)


def sigmoid(v):
    return 1.0 / (1.0 + jnp.exp(-v))


def softplus(v):
    return jnp.maximum(v, 0.0) + jnp.log1p(jnp.exp(-jnp.abs(v)))


def wide(mask, ch):
    return jnp.concatenate([mask] * (ch // 128), axis=1)


def tiles(v):
    total = v[:, 0:128]
    for at in range(128, v.shape[1], 128):
        total = total + v[:, at : at + 128]
    return total


class Net:
    def __init__(self, reps, send, recv, local):
        self.reps, self.send, self.recv, self.local = reps, send, recv, local
        self.s = lax.axis_index("dir")
        p = lax.axis_index("dp")
        self.i = lax.rem(p, 2)
        self.y = lax.rem(p // 2, reps)
        self.z = p // (2 * reps)
        self.used = 0
        self.moved = 0
        self.copies = []
        self.saves = []

    def place(self, s, z, y, i):
        return (s, (z * self.reps + y) * 2 + i)

    def flip(self, m):
        if m == 1:
            return self.z + 1 - 2 * lax.rem(self.z, 2)
        if m == 2:
            return lax.rem(self.z + 2, ZS)
        return ZS - 1 - self.z

    def over_x(self):
        return self.place(1 - self.s, self.z, self.y, self.i)

    def sibling(self):
        return self.place(self.s, self.z, self.y, 1 - self.i)

    def along_z(self, m):
        return self.place(self.s, self.flip(m), self.y, self.i)

    def shared(self, m):
        z = self.flip(m // 2) if m // 2 else self.z
        i = 1 - self.i if m % 2 else self.i
        return z, i

    def to_shared(self, m):
        z, i = self.shared(m)
        return self.place(self.s, z, self.y, i)

    def y_at(self, d):
        return lax.rem(self.y + d, self.reps)

    def along_y(self, d):
        return self.place(self.s, self.z, self.y_at(d), self.i)

    def greet(self):
        peers = [self.over_x()] + [self.to_shared(m) for m in range(1, TP)]
        peers += [self.along_y(d) for d in range(1, self.reps)]
        barrier = pltpu.get_barrier_semaphore()
        for peer in peers:
            pl.semaphore_signal(barrier, inc=1, device_id=peer, device_id_type=pl.DeviceIdType.MESH)
        pl.semaphore_wait(barrier, len(peers))

    def copy(self, source, target, peer):
        k = self.used
        self.used += 1
        c = pltpu.make_async_remote_copy(
            src_ref=source,
            dst_ref=target,
            send_sem=self.send.at[k],
            recv_sem=self.recv.at[k],
            device_id=peer,
            device_id_type=pl.DeviceIdType.MESH,
        )
        c.start()
        self.copies.append(c)
        return c

    def load(self, source, target):
        c = pltpu.make_async_copy(source, target, self.local.at[self.moved])
        self.moved += 1
        c.start()
        return c

    def save(self, source, target):
        self.saves.append(self.load(source, target))

    def finish(self):
        for c in self.copies:
            c.wait_send()
        for c in self.saves:
            c.wait()


class Reduce:
    def __init__(self, net, part, fold, out_low, in_low, total):
        self.net, self.part, self.fold, self.out_low, self.in_low, self.total = (
            net, part, fold, out_low, in_low, total,
        )
        self.rows = part.shape[0] // 2
        self.block = self.rows // ZS
        self.first = net.copy(part.at[span(1 - net.i, self.rows)], fold, net.sibling())

    def across_z(self):
        net, fold = self.net, self.fold
        self.first.wait_recv()
        fold[...] = self.part[span(net.i, self.rows), :] + fold[...]
        self.out_low[...] = fold[...].astype(bf16).reshape(ZS, self.block, 128)
        self.cs = [
            net.copy(self.out_low.at[net.flip(m)], self.in_low.at[m - 1], net.along_z(m))
            for m in range(1, ZS)
        ]

    def give(self):
        net, total = self.net, self.total
        mine = span(net.i * ZS + net.z, self.block)
        value = self.fold[span(net.z, self.block), :]
        for m in range(1, ZS):
            self.cs[m - 1].wait_recv()
            value = value + self.in_low[m - 1].astype(f32)
        total[mine, :] = value.astype(bf16)
        self.cs = [net.copy(total.at[mine], total.at[mine], net.along_z(m)) for m in range(1, ZS)]
        self.ds = [net.copy(total.at[mine], total.at[mine], net.sibling())]

    def end(self):
        net, total = self.net, self.total
        for m in range(1, ZS):
            self.cs[m - 1].wait_recv()
            there = span(net.i * ZS + net.flip(m), self.block)
            self.ds.append(net.copy(total.at[there], total.at[there], net.sibling()))
        for d in self.ds:
            d.wait_recv()


REDUCE_SCRATCH = (
    pltpu.VMEM((TP * PACK // 2, 128), f32),
    pltpu.VMEM((ZS, PACK, 128), bf16),
    pltpu.VMEM((ZS - 1, PACK, 128), bf16),
)


def fused(kernel, name_id, copies, moves, outs, args, scratch):
    return pl.pallas_call(
        kernel,
        out_shape=tuple(o for o, _ in outs),
        in_specs=[pl.BlockSpec(memory_space=m) for _, m in args],
        out_specs=tuple(pl.BlockSpec(memory_space=m) for _, m in outs),
        scratch_shapes=list(scratch)
        + [pltpu.SemaphoreType.DMA((n,)) for n in (copies, copies, moves)],
        compiler_params=pltpu.CompilerParams(
            collective_id=name_id, has_side_effects=True, vmem_limit_bytes=63 << 20
        ),
    )(*(a for a, _ in args))


def front_kernel(
    reps,
    grids, tokens, gain_own, wx_own, wz_own, wstep, taps_own, bias_own, step_own, skip_own, decay_own,
    wstate_own, wout_own, cot_own,
    normed_out, conv_in_out, conv_pre_out, conv_out_out, gate_out, tok_out, wx_out, wz_out,
    wout_out, cot_out, proj, gain, ends_out, small, wstate,
    tok_all, normed, wx_all, wz_all, wx, wz, small_all, wstate_all, wout_send, wout_in, meta_all, raw,
    conv_in, conv_pre, conv_out, gate_in, part,
    fold, out_low, in_low, send, recv, local,
):
    net = Net(reps, send, recv, local)
    s, z, y, i = net.s, net.z, net.y, net.i
    j = z * 2 + i
    cols, width = wx_own.shape
    ch = reps * cols
    piece = wout_own.shape[0]
    mine = span(j, PACK)
    mine_half = pl.ds(pl.multiple_of(j * PACK + s * HALF, HALF), HALF)
    tok_all[mine, :] = tokens[...]
    first_end = (grids[0, 0] * grids[0, 1]).astype(f32)
    second_end = first_end + (grids[1, 0] * grids[1, 1]).astype(f32)
    row = lax.broadcasted_iota(jnp.int32, (16, 128), 0)
    gain_row = jnp.concatenate([gain_own[...].astype(f32), jnp.zeros((1, 128 - piece), f32)], axis=1)
    meta = jnp.where(row == 0, gain_row, jnp.where(row == 1, first_end, second_end))
    meta_all[y, j] = meta.astype(bf16)
    wx_all[y] = wx_own[...]
    wz_all[y] = wz_own[...]
    small_rows = [wstep, taps_own, bias_own, step_own, skip_own, decay_own]
    small_rows = [ref[...].astype(f32) for ref in small_rows]
    small_rows.append(jnp.zeros((SMALL_ROWS - DECAY_ROW - STATE, cols), f32))
    small_all[y] = jnp.concatenate(small_rows, axis=0).astype(bf16)
    wstate_all[y] = wstate_own[...]
    net.greet()
    from_z = [net.copy(tok_all.at[mine_half], tok_all.at[mine_half], net.along_z(m)) for m in range(1, ZS)]
    from_core = [net.copy(tok_all.at[mine], tok_all.at[mine], net.sibling())]
    metas = [net.copy(meta_all.at[y, j], meta_all.at[y, j], net.to_shared(m)) for m in range(1, TP)]
    first_y = []
    for d in range(1, reps):
        for ref in (wx_all, small_all, wstate_all):
            first_y.append(net.copy(ref.at[y], ref.at[y], net.along_y(d)))
    cot_x = net.copy(cot_own, cot_out, net.over_x())
    for c in metas:
        c.wait_recv()
    meta_y = [net.copy(meta_all.at[y], meta_all.at[y], net.along_y(d)) for d in range(1, reps)]
    late_y = [net.copy(wz_all.at[y], wz_all.at[y], net.along_y(d)) for d in range(1, reps)]

    conv_in[0:PAD, :] = jnp.zeros((PAD, ch), f32)
    conv_in[PAD + 8 * PACK :, :] = jnp.zeros((PAD, ch), f32)
    for b in range(TP):
        both = meta_all[y, b].astype(f32)
        ends_out[0, b : b + 1, :] = both[1:2, :]
        ends_out[1, b : b + 1, :] = both[2:3, :]
    for p in range(TP * reps):
        zp, yp, ip = p // (2 * reps), (p // 2) % reps, p % 2
        wout_send[zp * 2 + ip, yp] = wout_own[:, p * cols : (p + 1) * cols]

    from_x = []
    for m in range(1, ZS):
        from_z[m - 1].wait_recv()
        rows = pl.ds(pl.multiple_of((net.flip(m) * 2 + i) * PACK + s * HALF, HALF), HALF)
        from_x.append(net.copy(tok_all.at[rows], tok_all.at[rows], net.over_x()))
        from_core.append(net.copy(tok_all.at[rows], tok_all.at[rows], net.sibling()))
    wout_in[j] = wout_send[j]
    wout_z = []
    for m in range(1, TP):
        zm, im = net.shared(m)
        wout_z.append(net.copy(wout_send.at[zm * 2 + im], wout_in.at[j], net.to_shared(m)))

    for c in meta_y + first_y:
        c.wait_recv()
    for p in range(TP * reps):
        zp, yp, ip = p // (2 * reps), (p // 2) % reps, p % 2
        gain[:, p * piece : (p + 1) * piece] = meta_all[yp, zp * 2 + ip].astype(f32)[0:1, 0:piece]
    for r in range(reps):
        wx[r * cols : (r + 1) * cols, :] = wx_all[r]
        small[:, r * cols : (r + 1) * cols] = small_all[r]
        wstate[r * cols : (r + 1) * cols, :] = wstate_all[r]
    net.save(wx, wx_out)

    def take(block):
        rows = span(block, PACK)
        x = tok_all[rows, :].astype(f32)
        inv = lax.rsqrt(jnp.mean(x * x, axis=1, keepdims=True) + EPS)
        low = (x * inv * gain[...]).astype(bf16)
        for h in range(2):
            normed[h, span(block, HALF), :] = low[h * HALF : (h + 1) * HALF]
        raw[rows, :] = mm_nt(low, wx[...])

    from_core[0].wait_recv()

    def take_pair(k, carry):
        take(z * 2 + k)
        return carry

    lax.fori_loop(0, 2, take_pair, 0)
    for m in range(1, ZS):
        from_x[m - 1].wait_recv()
        rows = pl.ds(pl.multiple_of((net.flip(m) * 2 + i) * PACK + (1 - s) * HALF, HALF), HALF)
        from_core.append(net.copy(tok_all.at[rows], tok_all.at[rows], net.sibling()))
    for m in range(1, ZS):
        from_core[m].wait_recv()
        from_core[m + ZS - 1].wait_recv()

        def take_far(k, carry, m=m):
            take(net.flip(m) * 2 + k)
            return carry

        lax.fori_loop(0, 2, take_far, 0)
    net.save(normed, normed_out)
    net.save(tok_all, tok_out)

    def in_order(b, carry):
        size = 32
        parts = [raw[pl.ds(pl.multiple_of(p * PACK + b * size, size), size), :] for p in range(8)]
        x = jnp.stack(parts, axis=1).reshape(8 * size, ch)
        conv_in[pl.ds(pl.multiple_of(PAD + b * size * 8, 8), 8 * size), :] = x
        return carry

    lax.fori_loop(0, PACK // 32, in_order, 0)
    ends = (ends_out[0], ends_out[1])
    sgn = 1 - 2 * s
    taps = small[TAP_ROW : TAP_ROW + 16, :].astype(f32)

    def conv_step(t, carry):
        seg = segment_of(t, ends)
        total = taps[4:5, :] + taps[3:4, :] * conv_in[rows8(t + 3), :]
        for k in range(1, TAPS):
            there = t - k * sgn
            same = wide((segment_of(there, ends) == seg).astype(f32), ch)
            total = total + taps[3 - k : 4 - k, :] * (conv_in[rows8(there + 3), :] * same)
        conv_pre[rows8(t), :] = total
        act = total * sigmoid(total)
        conv_out[rows8(t), :] = act.astype(bf16).astype(f32)
        return carry

    lax.fori_loop(0, PACK, conv_step, 0, unroll=2)
    part[...] = mm(conv_out[...].astype(bf16), wstate[...])
    sum_proj = Reduce(net, part, fold, out_low, in_low, proj)
    net.save(conv_in, conv_in_out)
    net.save(conv_pre, conv_pre_out)
    net.save(conv_out, conv_out_out)
    sum_proj.across_z()
    for c in late_y:
        c.wait_recv()
    for r in range(reps):
        wz[r * cols : (r + 1) * cols, :] = wz_all[r]
    net.save(wz, wz_out)
    gate_in[...] = mm_nt(normed[1 - s], wz[...])
    net.save(gate_in, gate_out)
    sum_proj.give()
    for c in wout_z:
        c.wait_recv()
    net.save(wout_in, wout_out)
    cot_x.wait_recv()
    sum_proj.end()
    net.finish()


def front(reps, grids, tokens, gain, wx, wz, wstep, taps, bias, step, skip, decay, wstate, wout, cot):
    cols, width = wx.shape
    ch = reps * cols
    rows = TP * PACK
    half = rows // 2
    piece = wout.shape[0]
    sds = jax.ShapeDtypeStruct
    V, H = pltpu.VMEM, pl.ANY
    args = [(grids, pltpu.SMEM), (tokens, V), (gain, V), (wx, V), (wz, V), (wstep, V), (taps, V), (bias, V)]
    args += [(step, V), (skip, V), (decay, V), (wstate, V), (wout, V), (cot, H)]
    outs = (
        (sds((2, half, width), bf16), H),
        (sds((rows + 2 * PAD, ch), f32), H),
        (sds((rows, ch), f32), H),
        (sds((rows, ch), f32), H),
        (sds((half, ch), f32), H),
        (sds((rows, width), bf16), H),
        (sds((ch, width), bf16), H),
        (sds((ch, width), bf16), H),
        (sds((TP, reps, piece, cols), bf16), H),
        (sds((HALF, width), bf16), H),
        (sds((rows, 128), bf16), V),
        (sds((1, width), f32), V),
        (sds((2, 8, 128), f32), V),
        (sds((SMALL_ROWS, ch), bf16), V),
        (sds((ch, 128), bf16), V),
    )
    scratch = (
        V((rows, width), bf16),
        V((2, half, width), bf16),
        V((reps, cols, width), bf16),
        V((reps, cols, width), bf16),
        V((ch, width), bf16),
        V((ch, width), bf16),
        V((reps, SMALL_ROWS, cols), bf16),
        V((reps, cols, 128), bf16),
        V((TP, reps, piece, cols), bf16),
        V((TP, reps, piece, cols), bf16),
        V((reps, TP, 16, 128), bf16),
        V((rows, ch), f32),
        V((rows + 2 * PAD, ch), f32),
        V((rows, ch), f32),
        V((rows, ch), f32),
        V((half, ch), f32),
        V((rows, 128), f32),
    ) + REDUCE_SCRATCH
    copies = 3 + 1 + 7 + 1 + 6 + 7 + 3 + 11 + 5 * (reps - 1)
    return fused(partial(front_kernel, reps), 1, copies, 9, outs, args, scratch)


def core_kernel(
    reps,
    proj_low, conv_out, small, ends_in, tokens, gate_hbm, wout_hbm, cot_hbm, normed_hbm,
    grad_values, grad_proj, gate_both, mixed, rows_grad, grad_wout, grad_wz,
    gate_in, wout_all, wout, cot, normed, ones, hprev, proj, step, decay_step, u, state, acc_ref, rate_ref, y_send, y_in,
    gated, mixed_part, mixed_core, mixed_low, mixed_z, mixed_sum, g, g_send, g_in,
    s1, s2, pb, pc, bias_acc, skip_acc, part,
    out_send, out_y, out_low, out_all, out_x, wz_low, wz_in,
    fold, low_out, low_in, send, recv, local,
):
    net = Net(reps, send, recv, local)
    s, z, yi, i = net.s, net.z, net.y, net.i
    sgn = 1 - 2 * s
    gh = 1 - s
    ch = conv_out.shape[1]
    cols = ch // reps
    half = TP * HALF
    rounds = HALF // CHUNK
    size = CHUNK * 8
    piece = out_all.shape[1]
    width = tokens.shape[1]
    y = grad_values
    loads = [
        net.load(gate_hbm, gate_in),
        net.load(normed_hbm, normed),
        net.load(wout_hbm, wout_all.at[yi]),
        net.load(cot_hbm, cot.at[span(z * 2 + i, HALF)]),
    ]
    net.greet()
    cot_mine = span(z * 2 + i, HALF)
    cot_z = [net.copy(cot_hbm, cot.at[cot_mine], net.along_z(m)) for m in range(1, ZS)]
    cot_core = [net.copy(cot_hbm, cot.at[cot_mine], net.sibling())]
    wout_y = [net.copy(wout_hbm, wout_all.at[yi], net.along_y(d)) for d in range(1, reps)]
    for k in range(2):
        source = lax.broadcasted_iota(jnp.int32, (STATE * 128, 128), 0) // 128
        target = lax.broadcasted_iota(jnp.int32, (STATE * 128, 128), 1)
        ones[k] = (target == DT_RANK + k * STATE + source).astype(f32).astype(bf16)
    proj[...] = proj_low[...].astype(f32)
    wstep = jnp.where(lax.broadcasted_iota(jnp.int32, (128, ch), 0) < DT_RANK, small[...], 0.0).astype(bf16)
    rows_grad[...] = jnp.zeros_like(rows_grad)
    rate_ref[...] = -LOG2E * jnp.exp(small[DT_RANK:, :].astype(f32)[DECAY_ROW - DT_RANK : DECAY_ROW - DT_RANK + STATE, :])
    vectors = small[DT_RANK : DT_RANK + 16, :].astype(f32)
    step_bias = vectors[STEP_ROW - DT_RANK : STEP_ROW - DT_RANK + 1, :]
    skip = vectors[SKIP_ROW - DT_RANK : SKIP_ROW - DT_RANK + 1, :]
    ends = (ends_in[0], ends_in[1])

    def prepare(block):
        rows = span(block, size)
        pre = mm(proj[rows, :].astype(bf16), wstep) + step_bias
        step_all = softplus(pre)
        values = conv_out[rows, :]
        step[...] = step_all
        u[...] = step_all * values
        for k in range(CHUNK):
            t = block * CHUNK + k
            fresh = segment_of(t, ends) != segment_of(t - sgn, ends)
            decay_step[8 * k : 8 * k + 8, :] = jnp.where(
                wide(fresh, ch), BIG, step_all[8 * k : 8 * k + 8, :]
            )
        return rows, pre, values

    def rates(n0):
        return [jnp.broadcast_to(rate_ref[n : n + 1, :], (8, ch)) for n in range(n0, n0 + NSTEP)]

    state[...] = jnp.zeros_like(state)

    def forward(c, carry):
        block = c + s * (2 * rounds - 1 - 2 * c)
        rows, _, values = prepare(block)
        y[rows, :] = skip * values
        for n0 in range(0, STATE, NSTEP):
            rate = rates(n0)

            def body(k, hs):
                r = s * (CHUNK - 1 - k) + (1 - s) * k
                t = block * CHUNK + r
                pv = proj[rows8(t), :]
                st = decay_step[rows8(r), :]
                uv = u[rows8(r), :]
                total = y[rows8(t), :]
                new = []
                for m in range(NSTEP):
                    n = n0 + m
                    hprev[t, n] = hs[m]
                    h = jnp.exp2(st * rate[m]) * hs[m] + uv * pv[:, DT_RANK + n : DT_RANK + n + 1]
                    total = total + h * pv[:, DT_RANK + STATE + n : DT_RANK + STATE + n + 1]
                    new.append(h)
                y[rows8(t), :] = total
                return tuple(new)

            hs = lax.fori_loop(0, CHUNK, body, tuple(state[n] for n in range(n0, n0 + NSTEP)), unroll=2)
            for m in range(NSTEP):
                state[n0 + m] = hs[m]
        return carry

    lax.fori_loop(0, rounds, forward, 0)
    y_send[...] = y[span(s, half), :].astype(bf16)
    y_copy = net.copy(y_send, y_in, net.over_x())
    lax.fori_loop(rounds, 2 * rounds - 1, forward, 0)
    for m in range(1, ZS):
        cot_z[m - 1].wait_recv()
        rows = span(net.flip(m) * 2 + i, HALF)
        cot_core.append(net.copy(cot.at[rows], cot.at[rows], net.sibling()))
    lax.fori_loop(2 * rounds - 1, 2 * rounds, forward, 0)
    for c in loads:
        c.wait()
    for c in wout_y:
        c.wait_recv()
    for p in range(TP * reps):
        zp, yp, ip = p // (2 * reps), (p // 2) % reps, p % 2
        for r in range(reps):
            wout[p * piece : (p + 1) * piece, r * cols : (r + 1) * cols] = wout_all[yp, zp * 2 + ip, r]
    for c in cot_core:
        c.wait_recv()
    y_copy.wait_recv()

    y_own = y[span(gh, half), :] + y_in[...].astype(f32)
    summed = jnp.swapaxes(y_own.reshape(HALF, 8, ch), 0, 1).reshape(half, ch)
    gate = gate_in[...]
    sig = sigmoid(gate)
    act = gate * sig
    grad_gated = mm(cot[...], wout[...])
    back = grad_gated * act
    back = jnp.swapaxes(back.reshape(8, HALF, ch), 0, 1).reshape(half, ch)
    g[span(gh, half), :] = back
    g_send[...] = back.astype(bf16)
    g_copy = net.copy(g_send, g_in, net.over_x())
    gate_both[gh] = (grad_gated * summed * sig * (1.0 + gate * (1.0 - sig))).astype(bf16)
    gate_copy = net.copy(gate_both.at[gh], gate_both.at[gh], net.over_x())
    low = (summed * act).astype(bf16)
    gated[...] = low
    mixed_part[...] = mm_nt(low, wout[...]).astype(bf16).reshape(mixed_part.shape)
    mixed_copy = net.copy(mixed_part.at[:, 1 - i], mixed_core, net.sibling())
    part_out = mm_tn(cot[...], gated[...]).astype(bf16)
    for q in range(ZS):
        for r in range(reps):
            at = (q * reps + r) * 2 * piece
            out_send[r, q * 2 * piece : (q + 1) * 2 * piece, :] = part_out[at : at + 2 * piece, :]
    out_copies = [
        net.copy(out_send.at[net.y_at(d)], out_y.at[d - 1], net.along_y(d)) for d in range(1, reps)
    ]

    state[...] = jnp.zeros_like(state)
    acc_ref[...] = jnp.zeros_like(acc_ref)
    bias_acc[...] = jnp.zeros_like(bias_acc)
    skip_acc[...] = jnp.zeros_like(skip_acc)

    def backward(c, carry):
        block = (1 - s) * (2 * rounds - 1 - c) + s * c
        rows, pre, values = prepare(block)
        s1[...] = jnp.zeros_like(s1)
        s2[...] = jnp.zeros_like(s2)
        for n0 in range(0, STATE, NSTEP):
            rate = rates(n0)

            def body(k, both):
                lams, accs = both
                r = s * k + (1 - s) * (CHUNK - 1 - k)
                t = block * CHUNK + r
                here = rows8(r)
                pv = proj[rows8(t), :]
                gv = g[rows8(t), :]
                uv = u[here, :]
                stv = step[here, :]
                st = decay_step[here, :]
                one = s1[here, :]
                two = s2[here, :]
                new_lams, new_accs = [], []
                for m in range(NSTEP):
                    n = n0 + m
                    a = jnp.exp2(st * rate[m])
                    ah = a * hprev[t, n]
                    lam = gv * pv[:, DT_RANK + STATE + n : DT_RANK + STATE + n + 1] + lams[m]
                    w = lam * ah
                    new_lams.append(a * lam)
                    two = two + rate[m] * w
                    new_accs.append(accs[m] + stv * w)
                    one = one + lam * pv[:, DT_RANK + n : DT_RANK + n + 1]
                    pb[here, 128 * n : 128 * n + 128] = tiles(lam * uv)
                    pc[here, 128 * n : 128 * n + 128] = tiles(gv * ah)
                s1[here, :] = one
                s2[here, :] = two
                return tuple(new_lams), tuple(new_accs)

            first = (
                tuple(state[n] for n in range(n0, n0 + NSTEP)),
                tuple(acc_ref[n] for n in range(n0, n0 + NSTEP)),
            )
            lams, accs = lax.fori_loop(0, CHUNK, body, first, unroll=2)
            for m in range(NSTEP):
                state[n0 + m] = lams[m]
                acc_ref[n0 + m] = accs[m]
        gv = g[rows, :]
        one = s1[...]
        grad_values[rows, :] = gv * skip + step[...] * one
        q = (LN2 * s2[...] + values * one) * sigmoid(pre)
        q_low = q.astype(bf16)
        bias_acc[...] += jnp.sum(q.reshape(CHUNK, 8, ch), axis=0)
        skip_acc[...] += jnp.sum((gv * values).reshape(CHUNK, 8, ch), axis=0)
        rank = proj_low[rows, :]
        rows_grad[0:DT_RANK, :] += mm_tn(rank, q_low)[0:DT_RANK, :]
        gu = jnp.sum(gv * u[...], axis=1, keepdims=True)
        lane = lax.broadcasted_iota(jnp.int32, (size, 128), 1)
        inject = jnp.where(lane >= DT_RANK + STATE, pltpu.roll(proj[rows, :], STATE, 1), 0.0)
        part[rows, :] = (
            mm_nt(q_low, wstep)
            + mm(pb[...].astype(bf16), ones[0])
            + mm(pc[...].astype(bf16), ones[1])
            + gu * inject
        )
        return carry

    lax.fori_loop(0, 1, backward, 0)
    mixed_copy.wait_recv()
    for q in range(ZS):
        mixed_low[q] = (mixed_part[q, i].astype(f32) + mixed_core[q].astype(f32)).astype(bf16)
    mixed_zs = [net.copy(mixed_low.at[net.flip(m)], mixed_z.at[m - 1], net.along_z(m)) for m in range(1, ZS)]
    lax.fori_loop(1, 2, backward, 0)
    for c in out_copies:
        c.wait_recv()
    total = out_send[yi].astype(f32)
    for d in range(1, reps):
        total = total + out_y[d - 1].astype(f32)
    total = total.astype(bf16)
    for q in range(TP):
        out_low[q] = total[q * piece : (q + 1) * piece]
    out_zs = []
    for m in range(1, TP):
        zm, im = net.shared(m)
        out_zs.append(net.copy(out_low.at[zm * 2 + im], out_all.at[z * 2 + i], net.to_shared(m)))
    out_all[z * 2 + i] = out_low[z * 2 + i]
    lax.fori_loop(2, rounds, backward, 0)
    g_copy.wait_recv()
    g[span(s, half), :] = g_in[...].astype(f32)
    lax.fori_loop(rounds, 2 * rounds, backward, 0)

    sum_proj = Reduce(net, part, fold, low_out, low_in, grad_proj)
    rows_grad[STEP_ROW : STEP_ROW + 1, :] = jnp.sum(bias_acc[...], axis=0, keepdims=True)
    rows_grad[SKIP_ROW : SKIP_ROW + 1, :] = jnp.sum(skip_acc[...], axis=0, keepdims=True)
    for n in range(STATE):
        rows_grad[DECAY_ROW + n : DECAY_ROW + n + 1, :] = (
            jnp.sum(acc_ref[n], axis=0, keepdims=True) * rate_ref[n : n + 1, :] * LN2
        )
    sum_proj.across_z()
    for c in mixed_zs:
        c.wait_recv()
    total = mixed_part[z, i].astype(f32) + mixed_core[z].astype(f32)
    for m in range(1, ZS):
        total = total + mixed_z[m - 1].astype(f32)
    mixed_sum[...] = (total + tokens[span(gh, HALF), :].astype(f32)).astype(bf16)
    mixed_home = net.copy(mixed_sum, mixed, net.over_x())
    gate_copy.wait_recv()
    own = pl.ds(pl.multiple_of(s * (width // 2), 128), width // 2)
    part_z = mm_tn(gate_both[0], normed[0, :, own]) + mm_tn(gate_both[1], normed[1, :, own])
    for r in range(reps):
        wz_low[r] = part_z[r * cols : (r + 1) * cols].astype(bf16)
    wz_copies = [
        net.copy(wz_low.at[net.y_at(d)], wz_in.at[d - 1], net.along_y(d)) for d in range(1, reps)
    ]
    sum_proj.give()
    for c in out_zs:
        c.wait_recv()
    out_home = net.copy(out_all.at[pl.ds((1 - s) * ZS, ZS)], out_x, net.over_x())
    sum_proj.end()
    total = wz_low[yi].astype(f32)
    for d in range(1, reps):
        wz_copies[d - 1].wait_recv()
        total = total + wz_in[d - 1].astype(f32)
    grad_wz[...] = total
    out_home.wait_recv()
    for q in range(ZS):
        total = out_all[s * ZS + q].astype(f32) + out_x[q].astype(f32)
        for r in range(reps):
            at = ((q // 2) * reps + r) * 2 + q % 2
            grad_wout[:, at * cols : (at + 1) * cols] = total[:, r * cols : (r + 1) * cols]
    mixed_home.wait_recv()
    net.finish()


def core(reps, proj, conv_out, small, ends, tokens, gate_in, wout, cot, normed):
    rows, ch = conv_out.shape
    half = rows // 2
    cols = ch // reps
    width = tokens.shape[1]
    piece = width // (TP * reps)
    V, H = pltpu.VMEM, pl.ANY
    args = [(proj, V), (conv_out, V), (small, V), (ends, V), (tokens, V)]
    args += [(gate_in, H), (wout, H), (cot, H), (normed, H)]
    sds = jax.ShapeDtypeStruct
    outs = (
        (sds((rows, ch), f32), V),
        (sds((rows, 128), bf16), V),
        (sds((2, half, ch), bf16), V),
        (sds((HALF, width), bf16), V),
        (sds((SMALL_ROWS, ch), f32), V),
        (sds((piece, ZS * ch), f32), V),
        (sds((cols, width // 2), f32), V),
    )
    size = CHUNK * 8
    scratch = (
        V((half, ch), f32),
        V((reps, TP, reps, piece, cols), bf16),
        V((width, ch), bf16),
        V((half, width), bf16),
        V((2, half, width), bf16),
        V((2, STATE * 128, 128), bf16),
        V((PACK, STATE, 8, ch), f32),
        V((rows, 128), f32),
        V((size, ch), f32),
        V((size, ch), f32),
        V((size, ch), f32),
        V((STATE, 8, ch), f32),
        V((STATE, 8, ch), f32),
        V((STATE, ch), f32),
        V((half, ch), bf16),
        V((half, ch), bf16),
        V((half, ch), bf16),
        V((ZS, 2, HALF, width), bf16),
        V((ZS, HALF, width), bf16),
        V((ZS, HALF, width), bf16),
        V((ZS - 1, HALF, width), bf16),
        V((HALF, width), bf16),
        V((rows, ch), f32),
        V((half, ch), bf16),
        V((half, ch), bf16),
        V((size, ch), f32),
        V((size, ch), f32),
        V((size, STATE * 128), f32),
        V((size, STATE * 128), f32),
        V((8, ch), f32),
        V((8, ch), f32),
        V((rows, 128), f32),
        V((reps, TP * piece, ch), bf16),
        V((reps - 1, TP * piece, ch), bf16),
        V((TP, piece, ch), bf16),
        V((TP, piece, ch), bf16),
        V((ZS, piece, ch), bf16),
        V((reps, cols, width // 2), bf16),
        V((reps - 1, cols, width // 2), bf16),
    ) + REDUCE_SCRATCH
    copies = 7 + 27 + 3 * (reps - 1)
    return fused(partial(core_kernel, reps), 2, copies, 4, outs, args, scratch)


def back_kernel(
    reps,
    grad_values, grad_proj, conv_pre, small, wstate, ends_in, gate_both, tokens, cot, gain, rows_in,
    conv_in_hbm, conv_out_hbm, wx_hbm, wz_hbm, normed_hbm, tok_hbm,
    grad_tokens, grad_gain, grad_wx, grad_taps, grad_bias, grad_step, grad_skip, grad_decay, grad_wstep, grad_wstate,
    conv_in, conv_out, wx, wz, normed, tok_all, w, slots, sums, gx, gx_in, part, core_in, low, z_in, gain_acc, gain_in,
    wx_low, wx_in, rows_part, rows_recv, state_part, state_in, send, recv, local,
):
    net = Net(reps, send, recv, local)
    s, z, yi, i = net.s, net.z, net.y, net.i
    sgn = 1 - 2 * s
    ch = conv_out.shape[1]
    cols = ch // reps
    width = tokens.shape[1]
    half = TP * HALF
    load_conv_in = net.load(conv_in_hbm, conv_in)
    load_w = [net.load(wx_hbm, wx), net.load(wz_hbm, wz)]
    load_tok = net.load(tok_hbm, tok_all)
    load_rest = [net.load(conv_out_hbm, conv_out), net.load(normed_hbm, normed)]
    net.greet()
    w[0:PAD, :] = jnp.zeros((PAD, ch), f32)
    w[PAD + 8 * PACK :, :] = jnp.zeros((PAD, ch), f32)

    def pull(b, carry):
        rows = span(b, 256)
        c = conv_pre[rows, :]
        sig = sigmoid(c)
        w[pl.ds(pl.multiple_of(PAD + b * 256, 8), 256), :] = (
            grad_values[rows, :] + mm_nt(grad_proj[rows, :], wstate[...])
        ) * (sig * (1.0 + c * (1.0 - sig)))
        return carry

    lax.fori_loop(0, 4, pull, 0)
    sums[...] = jnp.zeros_like(sums)
    ends = (ends_in[0], ends_in[1])
    taps = small[TAP_ROW : TAP_ROW + 16, :].astype(f32)

    def conv_step(t, carry):
        seg = segment_of(t, ends)
        here = w[rows8(t + 3), :]
        total = taps[3:4, :] * here
        sums[3] += here * conv_in[rows8(t + 3), :]
        sums[4] += here
        for k in range(1, TAPS):
            back = t - k * sgn
            ahead = t + k * sgn
            same_back = wide((segment_of(back, ends) == seg).astype(f32), ch)
            same_ahead = wide((segment_of(ahead, ends) == seg).astype(f32), ch)
            sums[3 - k] += here * (conv_in[rows8(back + 3), :] * same_back)
            total = total + taps[3 - k : 4 - k, :] * (w[rows8(ahead + 3), :] * same_ahead)
        slots[rows8(t), :] = total
        return carry

    gx_copies = []
    load_conv_in.wait()
    for h in (1 - s, s):
        lax.fori_loop(h * HALF, (h + 1) * HALF, conv_step, 0)
        x = slots[span(h, half), :]
        gx[h] = jnp.swapaxes(x.reshape(HALF, 8, ch), 0, 1).reshape(half, ch).astype(bf16)
        gx_copies.append(net.copy(gx.at[h], gx_in.at[h], net.over_x()))

    def rows_of(b, carry):
        rows = span(b, 2 * HALF)
        value = (
            mm(gx[s, rows, :], wx[...])
            + mm(gx_in[s, rows, :], wx[...])
            + mm(gate_both[s, rows, :], wz[...])
        )
        part[b] = value.astype(bf16).reshape(2, HALF, width)
        return carry

    for c in load_w:
        c.wait()
    gx_copies[0].wait_recv()
    lax.fori_loop(0, ZS, rows_of, 0)
    to_core = net.copy(part.at[:, 1 - i], core_in, net.sibling())

    gain_acc[0] = jnp.zeros(gain_acc.shape[1:], f32)

    def gain_terms(b, carry):
        rows = pl.ds(pl.multiple_of(b * PACK + s * HALF, HALF), HALF)
        x = tok_all[rows, :].astype(f32)
        inv = lax.rsqrt(jnp.mean(x * x, axis=1, keepdims=True) + EPS)
        terms = part[b // 2, lax.rem(b, 2)].astype(f32) * (x * inv)
        gain_acc[0] += jnp.sum(terms.reshape(HALF // 8, 8, width), axis=0)
        return carry

    to_core.wait_recv()
    for q in range(ZS):
        low[q] = (part[q, i].astype(f32) + core_in[q].astype(f32)).astype(bf16)
    to_z = [net.copy(low.at[net.flip(m)], z_in.at[m - 1], net.along_z(m)) for m in range(1, ZS)]
    load_tok.wait()
    lax.fori_loop(0, TP, gain_terms, 0)
    stages = [
        [net.sibling()],
        [net.over_x()],
        [net.along_y(d) for d in range(1, reps)],
        [net.along_z(1)],
        [net.along_z(2)],
    ]
    slot = [0]

    def gain_start(k):
        cs = []
        for peer in stages[k]:
            cs.append((slot[0], net.copy(gain_acc.at[k], gain_in.at[slot[0]], peer)))
            slot[0] += 1
        return cs

    def gain_end(k, cs):
        total = gain_acc[k]
        for at, c in cs:
            c.wait_recv()
            total = total + gain_in[at]
        gain_acc[k + 1] = total

    cs = gain_start(0)
    for c in load_rest:
        c.wait()
    state_all = mm_tn(conv_out[...].astype(bf16), grad_proj[...])
    for r in range(reps):
        state_part[r] = state_all[r * cols : (r + 1) * cols, :]
        rows_part[r] = rows_in[:, r * cols : (r + 1) * cols]
        for n in range(TAPS + 1):
            row = jnp.sum(sums[n], axis=0, keepdims=True)
            rows_part[r, TAP_ROW + n : TAP_ROW + n + 1, :] = row[:, r * cols : (r + 1) * cols]
    state_copies = [
        net.copy(state_part.at[net.y_at(d)], state_in.at[d - 1], net.along_y(d)) for d in range(1, reps)
    ]
    rows_copies = [
        net.copy(rows_part.at[net.y_at(d)], rows_recv.at[d - 1], net.along_y(d)) for d in range(1, reps)
    ]
    gain_end(0, cs)
    cs = gain_start(1)
    own = pl.ds(pl.multiple_of(s * (width // 2), 128), width // 2)
    gx_copies[1].wait_recv()
    part_x = mm_tn(gx[0], normed[0, :, own]) + mm_tn(gx[1], normed[1, :, own])
    part_x = part_x + mm_tn(gx_in[0], normed[0, :, own]) + mm_tn(gx_in[1], normed[1, :, own])
    for r in range(reps):
        wx_low[r] = part_x[r * cols : (r + 1) * cols].astype(bf16)
    wx_copies = [
        net.copy(wx_low.at[net.y_at(d)], wx_in.at[d - 1], net.along_y(d)) for d in range(1, reps)
    ]
    gain_end(1, cs)
    cs = gain_start(2)
    gain_end(2, cs)
    cs = gain_start(3)
    x = tokens[span(s, HALF), :].astype(f32)
    inv = lax.rsqrt(jnp.mean(x * x, axis=1, keepdims=True) + EPS)
    unit = x * inv
    gain_end(3, cs)
    cs = gain_start(4)
    grad = part[z, i].astype(f32) + core_in[z].astype(f32)
    for m in range(1, ZS):
        to_z[m - 1].wait_recv()
        grad = grad + z_in[m - 1].astype(f32)
    scaled = grad * gain[...]
    mean = jnp.mean(scaled * unit, axis=1, keepdims=True)
    grad_tokens[...] = inv * (scaled - unit * mean) + cot[...].astype(f32)
    gain_end(4, cs)
    grad_gain[...] = jnp.sum(gain_acc[5], axis=0, keepdims=True)
    total = rows_part[yi]
    for d in range(1, reps):
        rows_copies[d - 1].wait_recv()
        total = total + rows_recv[d - 1]
    grad_wstep[...] = total[0:DT_RANK]
    grad_taps[...] = total[TAP_ROW : TAP_ROW + TAPS]
    grad_bias[...] = total[BIAS_ROW : BIAS_ROW + 1]
    grad_step[...] = total[STEP_ROW : STEP_ROW + 1]
    grad_skip[...] = total[SKIP_ROW : SKIP_ROW + 1]
    grad_decay[...] = total[DECAY_ROW : DECAY_ROW + STATE]
    total = state_part[yi]
    for d in range(1, reps):
        state_copies[d - 1].wait_recv()
        total = total + state_in[d - 1]
    grad_wstate[...] = total
    total = wx_low[yi].astype(f32)
    for d in range(1, reps):
        wx_copies[d - 1].wait_recv()
        total = total + wx_in[d - 1].astype(f32)
    grad_wx[...] = total
    net.finish()


def backward(
    reps, grad_values, grad_proj, conv_pre, small, wstate, ends, gate_both, tokens, cot, gain, rows_in,
    conv_in, conv_out, wx, wz, normed, tok_all,
):
    rows, ch = conv_out.shape
    half = rows // 2
    cols = ch // reps
    width = tokens.shape[1]
    V, H = pltpu.VMEM, pl.ANY
    near = (grad_values, grad_proj, conv_pre, small, wstate, ends, gate_both, tokens, cot, gain, rows_in)
    far = (conv_in, conv_out, wx, wz, normed, tok_all)
    args = [(a, V) for a in near] + [(a, H) for a in far]
    sds = jax.ShapeDtypeStruct
    outs = (
        sds((HALF, width), f32),
        sds((1, width), f32),
        sds((cols, width // 2), f32),
        sds((TAPS, cols), f32),
        sds((1, cols), f32),
        sds((1, cols), f32),
        sds((1, cols), f32),
        sds((STATE, cols), f32),
        sds((DT_RANK, cols), f32),
        sds((cols, 128), f32),
    )
    scratch = tuple(V(a.shape, a.dtype) for a in far) + (
        V((rows + 2 * PAD, ch), f32),
        V((rows, ch), f32),
        V((TAPS + 1, 8, ch), f32),
        V((2, half, ch), bf16),
        V((2, half, ch), bf16),
        V((ZS, 2, HALF, width), bf16),
        V((ZS, HALF, width), bf16),
        V((ZS, HALF, width), bf16),
        V((ZS - 1, HALF, width), bf16),
        V((6, 8, width), f32),
        V((3 + reps, 8, width), f32),
        V((reps, cols, width // 2), bf16),
        V((reps - 1, cols, width // 2), bf16),
        V((reps, SMALL_ROWS, cols), f32),
        V((reps - 1, SMALL_ROWS, cols), f32),
        V((reps, cols, 128), f32),
        V((reps - 1, cols, 128), f32),
    )
    copies = 2 + 1 + 3 + 4 + 4 * (reps - 1)
    return fused(partial(back_kernel, reps), 3, copies, 6, [(o, V) for o in outs], args, scratch)


def place_kernel(index, gain, *refs):
    count = (len(refs) - 1) // 2
    for source, target in zip(refs[:count], refs[count : 2 * count]):
        target[...] = source[...]
    gain_out = refs[-1]
    width, n = gain.shape[1], gain_out.shape[1]
    moved = pltpu.roll(jnp.broadcast_to(gain[...], (8, width)), width - index[0] * n, 1)
    gain_out[...] = moved[0:1, 0:n]


def place(index, gain, n, *results):
    V = pl.BlockSpec(memory_space=pltpu.VMEM)
    return pl.pallas_call(
        place_kernel,
        out_shape=tuple(jax.ShapeDtypeStruct(r.shape, r.dtype) for r in results)
        + (jax.ShapeDtypeStruct((1, n), f32),),
        in_specs=[pl.BlockSpec(memory_space=pltpu.SMEM), V] + [V] * len(results),
        out_specs=tuple([V] * (len(results) + 1)),
    )(index, gain, *results)

def local(
    reps, tokens, item_grids, norm_gain, proj_in_x, proj_in_z, proj_out, conv_weight, conv_bias,
    proj_state, proj_step, step_bias, decay_log, skip_gain, grad_out,
):
    width = tokens.shape[1]
    cot = grad_out.reshape(HALF, width)
    (
        normed, conv_in, conv_pre, conv_out, gate_in, tok_all, wx, wz, wout, cot_other,
        proj, gain, ends, small, wstate,
    ) = front(
        reps, item_grids, tokens, norm_gain[None], proj_in_x.T, proj_in_z.T, proj_step[0], conv_weight[0],
        conv_bias, step_bias, skip_gain, decay_log[0], proj_state[0], proj_out.T, cot,
    )
    grad_values, grad_proj, gate_both, mixed, rows_grad, grad_wout, grad_wz = core(
        reps, proj, conv_out, small, ends, tokens, gate_in, wout, cot_other, normed
    )
    (
        grad_tokens, grad_gain, grad_wx, grad_taps, grad_bias, grad_step, grad_skip, grad_decay,
        grad_wstep, grad_wstate,
    ) = backward(
        reps, grad_values, grad_proj, conv_pre, small, wstate, ends, gate_both, tokens, cot, gain, rows_grad,
        conv_in, conv_out, wx, wz, normed, tok_all,
    )
    index = (lax.axis_index("dir") * lax.axis_size("dp") + lax.axis_index("dp")).astype(jnp.int32)
    (
        mixed, grad_tokens, grad_wx, grad_wz, grad_wout, grad_taps, grad_bias, grad_wstate, grad_wstep,
        grad_step, grad_decay, grad_skip, grad_gain,
    ) = place(
        index.reshape(1), grad_gain, width // (2 * TP * reps),
        mixed, grad_tokens, grad_wx, grad_wz, grad_wout, grad_taps, grad_bias, grad_wstate, grad_wstep,
        grad_step, grad_decay, grad_skip,
    )
    return (
        mixed.reshape(1, 1, HALF, width),
        grad_tokens.reshape(1, 1, HALF, width),
        grad_gain[0],
        grad_wx.T,
        grad_wz.T,
        grad_wout.T,
        grad_taps[None],
        grad_bias,
        grad_wstate[None],
        grad_wstep[None],
        grad_step,
        grad_decay[None],
        grad_skip,
    )


def solution(mesh):
    reps = mesh.shape["dp"] // TP
    return jax.shard_map(
        partial(local, reps),
        mesh=mesh,
        in_specs=(
            P("dp", None),
            P("dp", None),
            P("dp"),
            P(None, "dp"),
            P(None, "dp"),
            P(None, "dp"),
            P("dir", None, "dp"),
            P("dir", "dp"),
            P("dir", "dp", None),
            P("dir", None, "dp"),
            P("dir", "dp"),
            P("dir", None, "dp"),
            P("dir", "dp"),
            P("dp", "dir", None, None),
        ),
        out_specs=(
            P("dp", "dir", None, None),
            P("dp", "dir", None, None),
            P(("dir", "dp")),
            P("dir", "dp"),
            P("dir", "dp"),
            P("dir", "dp"),
            P("dir", None, "dp"),
            P("dir", "dp"),
            P("dir", "dp", None),
            P("dir", None, "dp"),
            P("dir", "dp"),
            P("dir", None, "dp"),
            P("dir", "dp"),
        ),
        check_vma=False,
    )
```

```python
from functools import partial

import jax
import jax.numpy as jnp
from jax import lax
from jax.experimental import pallas as pl
from jax.experimental.pallas import tpu as pltpu
from jax.sharding import PartitionSpec as P

f32 = jnp.float32
bf16 = jnp.bfloat16
EPS = 1e-05
DT_RANK = 96
STATE = 16
TAPS = 4
ZS = 4
TP = 8
PACK = 128
HALF = 64
CHUNK = 16
NSTEP = 4
LOG2E = 1.4426950408889634
LN2 = 0.6931471805599453
BIG = 1e9
PAD = 24
TAP_ROW, BIAS_ROW, STEP_ROW, SKIP_ROW, DECAY_ROW, SMALL_ROWS = 96, 100, 101, 102, 103, 128


def mm(left, right):
    return jnp.dot(left, right, preferred_element_type=f32)


def mm_nt(left, right):
    return lax.dot_general(left, right, (((1,), (1,)), ((), ())), preferred_element_type=f32)


def mm_tn(left, right):
    return lax.dot_general(left, right, (((0,), (0,)), ((), ())), preferred_element_type=f32)


def segment_of(t, ends):
    t = t.astype(f32) if hasattr(t, "astype") else float(t)
    return (t >= ends[0]).astype(f32) + (t >= ends[1]).astype(f32)


def rows8(t):
    return pl.ds(pl.multiple_of(t * 8, 8), 8)


def span(start, size):
    return pl.ds(pl.multiple_of(start * size, size), size)


def sigmoid(v):
    return 1.0 / (1.0 + jnp.exp(-v))


def softplus(v):
    return jnp.maximum(v, 0.0) + jnp.log1p(jnp.exp(-jnp.abs(v)))


def wide(mask, ch):
    return jnp.concatenate([mask] * (ch // 128), axis=1)


def tiles(v):
    total = v[:, 0:128]
    for at in range(128, v.shape[1], 128):
        total = total + v[:, at : at + 128]
    return total


class Net:
    def __init__(self, reps, send, recv, local):
        self.reps, self.send, self.recv, self.local = reps, send, recv, local
        self.s = lax.axis_index("dir")
        p = lax.axis_index("dp")
        self.i = lax.rem(p, 2)
        self.y = lax.rem(p // 2, reps)
        self.z = p // (2 * reps)
        self.used = 0
        self.moved = 0
        self.copies = []
        self.saves = []

    def place(self, s, z, y, i):
        return (s, (z * self.reps + y) * 2 + i)

    def flip(self, m):
        if m == 1:
            return self.z + 1 - 2 * lax.rem(self.z, 2)
        if m == 2:
            return lax.rem(self.z + 2, ZS)
        return ZS - 1 - self.z

    def over_x(self):
        return self.place(1 - self.s, self.z, self.y, self.i)

    def sibling(self):
        return self.place(self.s, self.z, self.y, 1 - self.i)

    def along_z(self, m):
        return self.place(self.s, self.flip(m), self.y, self.i)

    def shared(self, m):
        z = self.flip(m // 2) if m // 2 else self.z
        i = 1 - self.i if m % 2 else self.i
        return z, i

    def to_shared(self, m):
        z, i = self.shared(m)
        return self.place(self.s, z, self.y, i)

    def y_at(self, d):
        return lax.rem(self.y + d, self.reps)

    def along_y(self, d):
        return self.place(self.s, self.z, self.y_at(d), self.i)

    def greet(self):
        peers = [self.over_x()] + [self.to_shared(m) for m in range(1, TP)]
        peers += [self.along_y(d) for d in range(1, self.reps)]
        barrier = pltpu.get_barrier_semaphore()
        for peer in peers:
            pl.semaphore_signal(barrier, inc=1, device_id=peer, device_id_type=pl.DeviceIdType.MESH)
        pl.semaphore_wait(barrier, len(peers))

    def copy(self, source, target, peer):
        k = self.used
        self.used += 1
        c = pltpu.make_async_remote_copy(
            src_ref=source,
            dst_ref=target,
            send_sem=self.send.at[k],
            recv_sem=self.recv.at[k],
            device_id=peer,
            device_id_type=pl.DeviceIdType.MESH,
        )
        c.start()
        self.copies.append(c)
        return c

    def load(self, source, target):
        c = pltpu.make_async_copy(source, target, self.local.at[self.moved])
        self.moved += 1
        c.start()
        return c

    def save(self, source, target):
        self.saves.append(self.load(source, target))

    def finish(self):
        for c in self.copies:
            c.wait_send()
        for c in self.saves:
            c.wait()


class Reduce:
    def __init__(self, net, part, fold, out_low, in_low, total):
        self.net, self.part, self.fold, self.out_low, self.in_low, self.total = (
            net, part, fold, out_low, in_low, total,
        )
        self.rows = part.shape[0] // 2
        self.block = self.rows // ZS
        self.first = net.copy(part.at[span(1 - net.i, self.rows)], fold, net.sibling())

    def across_z(self):
        net, fold = self.net, self.fold
        self.first.wait_recv()
        fold[...] = self.part[span(net.i, self.rows), :] + fold[...]
        self.out_low[...] = fold[...].astype(bf16).reshape(ZS, self.block, 128)
        self.cs = [
            net.copy(self.out_low.at[net.flip(m)], self.in_low.at[m - 1], net.along_z(m))
            for m in range(1, ZS)
        ]

    def give(self):
        net, total = self.net, self.total
        mine = span(net.i * ZS + net.z, self.block)
        value = self.fold[span(net.z, self.block), :]
        for m in range(1, ZS):
            self.cs[m - 1].wait_recv()
            value = value + self.in_low[m - 1].astype(f32)
        total[mine, :] = value.astype(bf16)
        self.cs = [net.copy(total.at[mine], total.at[mine], net.along_z(m)) for m in range(1, ZS)]
        self.ds = [net.copy(total.at[mine], total.at[mine], net.sibling())]

    def end(self):
        net, total = self.net, self.total
        for m in range(1, ZS):
            self.cs[m - 1].wait_recv()
            there = span(net.i * ZS + net.flip(m), self.block)
            self.ds.append(net.copy(total.at[there], total.at[there], net.sibling()))
        for d in self.ds:
            d.wait_recv()


REDUCE_SCRATCH = (
    pltpu.VMEM((TP * PACK // 2, 128), f32),
    pltpu.VMEM((ZS, PACK, 128), bf16),
    pltpu.VMEM((ZS - 1, PACK, 128), bf16),
)


def fused(kernel, name_id, copies, moves, outs, args, scratch):
    return pl.pallas_call(
        kernel,
        out_shape=tuple(o for o, _ in outs),
        in_specs=[pl.BlockSpec(memory_space=m) for _, m in args],
        out_specs=tuple(pl.BlockSpec(memory_space=m) for _, m in outs),
        scratch_shapes=list(scratch)
        + [pltpu.SemaphoreType.DMA((n,)) for n in (copies, copies, moves)],
        compiler_params=pltpu.CompilerParams(
            collective_id=name_id, has_side_effects=True, vmem_limit_bytes=63 << 20
        ),
    )(*(a for a, _ in args))


def front_kernel(
    reps,
    grids, tokens, gain_own, wx_own, wz_own, wstep, taps_own, bias_own, step_own, skip_own, decay_own,
    wstate_own, wout_own, cot_own,
    normed_out, conv_in_out, conv_pre_out, conv_out_out, gate_out, tok_out, wx_out, wz_out,
    wout_out, cot_out, proj, gain, ends_out, small, wstate,
    tok_all, normed, wx_all, wz_all, wx, wz, small_all, wstate_all, wout_send, wout_in, meta_all, raw,
    conv_in, conv_pre, conv_out, gate_in, part,
    fold, out_low, in_low, send, recv, local,
):
    net = Net(reps, send, recv, local)
    s, z, y, i = net.s, net.z, net.y, net.i
    j = z * 2 + i
    cols, width = wx_own.shape
    ch = reps * cols
    piece = wout_own.shape[0]
    mine = span(j, PACK)
    mine_half = pl.ds(pl.multiple_of(j * PACK + s * HALF, HALF), HALF)
    tok_all[mine, :] = tokens[...]
    first_end = (grids[0, 0] * grids[0, 1]).astype(f32)
    second_end = first_end + (grids[1, 0] * grids[1, 1]).astype(f32)
    row = lax.broadcasted_iota(jnp.int32, (16, 128), 0)
    gain_row = jnp.concatenate([gain_own[...].astype(f32), jnp.zeros((1, 128 - piece), f32)], axis=1)
    meta = jnp.where(row == 0, gain_row, jnp.where(row == 1, first_end, second_end))
    meta_all[y, j] = meta.astype(bf16)
    wx_all[y] = wx_own[...]
    wz_all[y] = wz_own[...]
    small_rows = [wstep, taps_own, bias_own, step_own, skip_own, decay_own]
    small_rows = [ref[...].astype(f32) for ref in small_rows]
    small_rows.append(jnp.zeros((SMALL_ROWS - DECAY_ROW - STATE, cols), f32))
    small_all[y] = jnp.concatenate(small_rows, axis=0).astype(bf16)
    wstate_all[y] = wstate_own[...]
    net.greet()
    from_z = [net.copy(tok_all.at[mine_half], tok_all.at[mine_half], net.along_z(m)) for m in range(1, ZS)]
    from_core = [net.copy(tok_all.at[mine], tok_all.at[mine], net.sibling())]
    metas = [net.copy(meta_all.at[y, j], meta_all.at[y, j], net.to_shared(m)) for m in range(1, TP)]
    first_y = []
    for d in range(1, reps):
        for ref in (wx_all, small_all, wstate_all):
            first_y.append(net.copy(ref.at[y], ref.at[y], net.along_y(d)))
    cot_x = net.copy(cot_own, cot_out, net.over_x())
    for c in metas:
        c.wait_recv()
    meta_y = [net.copy(meta_all.at[y], meta_all.at[y], net.along_y(d)) for d in range(1, reps)]
    late_y = [net.copy(wz_all.at[y], wz_all.at[y], net.along_y(d)) for d in range(1, reps)]

    conv_in[0:PAD, :] = jnp.zeros((PAD, ch), f32)
    conv_in[PAD + 8 * PACK :, :] = jnp.zeros((PAD, ch), f32)
    for b in range(TP):
        both = meta_all[y, b].astype(f32)
        ends_out[0, b : b + 1, :] = both[1:2, :]
        ends_out[1, b : b + 1, :] = both[2:3, :]
    for p in range(TP * reps):
        zp, yp, ip = p // (2 * reps), (p // 2) % reps, p % 2
        wout_send[zp * 2 + ip, yp] = wout_own[:, p * cols : (p + 1) * cols]

    from_x = []
    for m in range(1, ZS):
        from_z[m - 1].wait_recv()
        rows = pl.ds(pl.multiple_of((net.flip(m) * 2 + i) * PACK + s * HALF, HALF), HALF)
        from_x.append(net.copy(tok_all.at[rows], tok_all.at[rows], net.over_x()))
        from_core.append(net.copy(tok_all.at[rows], tok_all.at[rows], net.sibling()))
    wout_in[j] = wout_send[j]
    wout_z = []
    for m in range(1, TP):
        zm, im = net.shared(m)
        wout_z.append(net.copy(wout_send.at[zm * 2 + im], wout_in.at[j], net.to_shared(m)))

    for c in meta_y + first_y:
        c.wait_recv()
    for p in range(TP * reps):
        zp, yp, ip = p // (2 * reps), (p // 2) % reps, p % 2
        gain[:, p * piece : (p + 1) * piece] = meta_all[yp, zp * 2 + ip].astype(f32)[0:1, 0:piece]
    for r in range(reps):
        wx[r * cols : (r + 1) * cols, :] = wx_all[r]
        small[:, r * cols : (r + 1) * cols] = small_all[r]
        wstate[r * cols : (r + 1) * cols, :] = wstate_all[r]
    net.save(wx, wx_out)

    def take(block):
        rows = span(block, PACK)
        x = tok_all[rows, :].astype(f32)
        inv = lax.rsqrt(jnp.mean(x * x, axis=1, keepdims=True) + EPS)
        low = (x * inv * gain[...]).astype(bf16)
        for h in range(2):
            normed[h, span(block, HALF), :] = low[h * HALF : (h + 1) * HALF]
        raw[rows, :] = mm_nt(low, wx[...])

    from_core[0].wait_recv()

    def take_pair(k, carry):
        take(z * 2 + k)
        return carry

    lax.fori_loop(0, 2, take_pair, 0)
    for m in range(1, ZS):
        from_x[m - 1].wait_recv()
        rows = pl.ds(pl.multiple_of((net.flip(m) * 2 + i) * PACK + (1 - s) * HALF, HALF), HALF)
        from_core.append(net.copy(tok_all.at[rows], tok_all.at[rows], net.sibling()))
    for m in range(1, ZS):
        from_core[m].wait_recv()
        from_core[m + ZS - 1].wait_recv()

        def take_far(k, carry, m=m):
            take(net.flip(m) * 2 + k)
            return carry

        lax.fori_loop(0, 2, take_far, 0)
    net.save(normed, normed_out)
    net.save(tok_all, tok_out)

    def in_order(b, carry):
        size = 32
        parts = [raw[pl.ds(pl.multiple_of(p * PACK + b * size, size), size), :] for p in range(8)]
        x = jnp.stack(parts, axis=1).reshape(8 * size, ch)
        conv_in[pl.ds(pl.multiple_of(PAD + b * size * 8, 8), 8 * size), :] = x
        return carry

    lax.fori_loop(0, PACK // 32, in_order, 0)
    ends = (ends_out[0], ends_out[1])
    sgn = 1 - 2 * s
    taps = small[TAP_ROW : TAP_ROW + 16, :].astype(f32)

    def conv_step(t, carry):
        seg = segment_of(t, ends)
        total = taps[4:5, :] + taps[3:4, :] * conv_in[rows8(t + 3), :]
        for k in range(1, TAPS):
            there = t - k * sgn
            same = wide((segment_of(there, ends) == seg).astype(f32), ch)
            total = total + taps[3 - k : 4 - k, :] * (conv_in[rows8(there + 3), :] * same)
        conv_pre[rows8(t), :] = total
        act = total * sigmoid(total)
        conv_out[rows8(t), :] = act.astype(bf16).astype(f32)
        return carry

    lax.fori_loop(0, PACK, conv_step, 0, unroll=2)
    part[...] = mm(conv_out[...].astype(bf16), wstate[...])
    sum_proj = Reduce(net, part, fold, out_low, in_low, proj)
    net.save(conv_in, conv_in_out)
    net.save(conv_pre, conv_pre_out)
    net.save(conv_out, conv_out_out)
    sum_proj.across_z()
    for c in late_y:
        c.wait_recv()
    for r in range(reps):
        wz[r * cols : (r + 1) * cols, :] = wz_all[r]
    net.save(wz, wz_out)
    gate_in[...] = mm_nt(normed[1 - s], wz[...])
    net.save(gate_in, gate_out)
    sum_proj.give()
    for c in wout_z:
        c.wait_recv()
    net.save(wout_in, wout_out)
    cot_x.wait_recv()
    sum_proj.end()
    net.finish()


def front(reps, grids, tokens, gain, wx, wz, wstep, taps, bias, step, skip, decay, wstate, wout, cot):
    cols, width = wx.shape
    ch = reps * cols
    rows = TP * PACK
    half = rows // 2
    piece = wout.shape[0]
    sds = jax.ShapeDtypeStruct
    V, H = pltpu.VMEM, pl.ANY
    args = [(grids, pltpu.SMEM), (tokens, V), (gain, V), (wx, V), (wz, V), (wstep, V), (taps, V), (bias, V)]
    args += [(step, V), (skip, V), (decay, V), (wstate, V), (wout, V), (cot, H)]
    outs = (
        (sds((2, half, width), bf16), H),
        (sds((rows + 2 * PAD, ch), f32), H),
        (sds((rows, ch), f32), H),
        (sds((rows, ch), f32), H),
        (sds((half, ch), f32), H),
        (sds((rows, width), bf16), H),
        (sds((ch, width), bf16), H),
        (sds((ch, width), bf16), H),
        (sds((TP, reps, piece, cols), bf16), H),
        (sds((HALF, width), bf16), H),
        (sds((rows, 128), bf16), V),
        (sds((1, width), f32), V),
        (sds((2, 8, 128), f32), V),
        (sds((SMALL_ROWS, ch), bf16), V),
        (sds((ch, 128), bf16), V),
    )
    scratch = (
        V((rows, width), bf16),
        V((2, half, width), bf16),
        V((reps, cols, width), bf16),
        V((reps, cols, width), bf16),
        V((ch, width), bf16),
        V((ch, width), bf16),
        V((reps, SMALL_ROWS, cols), bf16),
        V((reps, cols, 128), bf16),
        V((TP, reps, piece, cols), bf16),
        V((TP, reps, piece, cols), bf16),
        V((reps, TP, 16, 128), bf16),
        V((rows, ch), f32),
        V((rows + 2 * PAD, ch), f32),
        V((rows, ch), f32),
        V((rows, ch), f32),
        V((half, ch), f32),
        V((rows, 128), f32),
    ) + REDUCE_SCRATCH
    copies = 3 + 1 + 7 + 1 + 6 + 7 + 3 + 11 + 5 * (reps - 1)
    return fused(partial(front_kernel, reps), 1, copies, 9, outs, args, scratch)


def core_kernel(
    reps,
    proj_low, conv_out, small, ends_in, tokens, gate_hbm, wout_hbm, cot_hbm, normed_hbm,
    grad_values, grad_proj, gate_both, mixed, rows_grad, grad_wout, grad_wz,
    gate_in, wout_all, wout, cot, normed, ones, hprev, proj, step, decay_step, u, state, acc_ref, rate_ref, y_send, y_in,
    gated, mixed_part, mixed_core, mixed_low, mixed_z, mixed_sum, g_send, g_in,
    s1, s2, pb, pc, bias_acc, skip_acc, part,
    out_send, out_y, out_low, out_all, out_x, wz_low, wz_in,
    fold, low_out, low_in, send, recv, local,
):
    net = Net(reps, send, recv, local)
    s, z, yi, i = net.s, net.z, net.y, net.i
    sgn = 1 - 2 * s
    gh = 1 - s
    ch = conv_out.shape[1]
    cols = ch // reps
    half = TP * HALF
    rounds = HALF // CHUNK
    size = CHUNK * 8
    piece = out_all.shape[1]
    width = tokens.shape[1]
    y = g = grad_values
    own = pl.ds(pl.multiple_of(s * (width // 2), 128), width // 2)
    loads = [
        net.load(gate_hbm, gate_in),
        net.load(normed_hbm.at[:, :, own], normed),
        net.load(wout_hbm, wout_all.at[yi]),
        net.load(cot_hbm, cot.at[span(z * 2 + i, HALF)]),
    ]
    net.greet()
    cot_mine = span(z * 2 + i, HALF)
    cot_z = [net.copy(cot_hbm, cot.at[cot_mine], net.along_z(m)) for m in range(1, ZS)]
    cot_core = [net.copy(cot_hbm, cot.at[cot_mine], net.sibling())]
    wout_y = [net.copy(wout_hbm, wout_all.at[yi], net.along_y(d)) for d in range(1, reps)]
    for k in range(2):
        source = lax.broadcasted_iota(jnp.int32, (STATE * 128, 128), 0) // 128
        target = lax.broadcasted_iota(jnp.int32, (STATE * 128, 128), 1)
        ones[k] = (target == DT_RANK + k * STATE + source).astype(f32).astype(bf16)
    proj[...] = proj_low[...].astype(f32)
    wstep = jnp.where(lax.broadcasted_iota(jnp.int32, (128, ch), 0) < DT_RANK, small[...], 0.0).astype(bf16)
    rows_grad[...] = jnp.zeros_like(rows_grad)
    rate_ref[...] = -LOG2E * jnp.exp(small[DT_RANK:, :].astype(f32)[DECAY_ROW - DT_RANK : DECAY_ROW - DT_RANK + STATE, :])
    vectors = small[DT_RANK : DT_RANK + 16, :].astype(f32)
    step_bias = vectors[STEP_ROW - DT_RANK : STEP_ROW - DT_RANK + 1, :]
    skip = vectors[SKIP_ROW - DT_RANK : SKIP_ROW - DT_RANK + 1, :]
    ends = (ends_in[0], ends_in[1])

    def prepare(block):
        rows = span(block, size)
        pre = mm(proj[rows, :].astype(bf16), wstep) + step_bias
        step_all = softplus(pre)
        values = conv_out[rows, :]
        step[...] = step_all
        u[...] = step_all * values
        for k in range(CHUNK):
            t = block * CHUNK + k
            fresh = segment_of(t, ends) != segment_of(t - sgn, ends)
            decay_step[8 * k : 8 * k + 8, :] = jnp.where(
                wide(fresh, ch), BIG, step_all[8 * k : 8 * k + 8, :]
            )
        return rows, pre, values

    def rates(n0):
        return [jnp.broadcast_to(rate_ref[n : n + 1, :], (8, ch)) for n in range(n0, n0 + NSTEP)]

    state[...] = jnp.zeros_like(state)

    def forward(c, carry):
        block = c + s * (2 * rounds - 1 - 2 * c)
        rows, _, values = prepare(block)
        y[rows, :] = skip * values
        for n0 in range(0, STATE, NSTEP):
            rate = rates(n0)

            def body(k, hs):
                r = s * (CHUNK - 1 - k) + (1 - s) * k
                t = block * CHUNK + r
                pv = proj[rows8(t), :]
                st = decay_step[rows8(r), :]
                uv = u[rows8(r), :]
                total = y[rows8(t), :]
                new = []
                for m in range(NSTEP):
                    n = n0 + m
                    hprev[t, n] = hs[m]
                    h = jnp.exp2(st * rate[m]) * hs[m] + uv * pv[:, DT_RANK + n : DT_RANK + n + 1]
                    total = total + h * pv[:, DT_RANK + STATE + n : DT_RANK + STATE + n + 1]
                    new.append(h)
                y[rows8(t), :] = total
                return tuple(new)

            hs = lax.fori_loop(0, CHUNK, body, tuple(state[n] for n in range(n0, n0 + NSTEP)), unroll=CHUNK)
            for m in range(NSTEP):
                state[n0 + m] = hs[m]
        return carry

    lax.fori_loop(0, rounds, forward, 0)
    y_send[...] = y[span(s, half), :].astype(bf16)
    y_copy = net.copy(y_send, y_in, net.over_x())
    lax.fori_loop(rounds, 2 * rounds - 1, forward, 0)
    for m in range(1, ZS):
        cot_z[m - 1].wait_recv()
        rows = span(net.flip(m) * 2 + i, HALF)
        cot_core.append(net.copy(cot.at[rows], cot.at[rows], net.sibling()))
    lax.fori_loop(2 * rounds - 1, 2 * rounds, forward, 0)
    for c in loads:
        c.wait()
    for c in wout_y:
        c.wait_recv()
    for p in range(TP * reps):
        zp, yp, ip = p // (2 * reps), (p // 2) % reps, p % 2
        for r in range(reps):
            wout[p * piece : (p + 1) * piece, r * cols : (r + 1) * cols] = wout_all[yp, zp * 2 + ip, r]
    for c in cot_core:
        c.wait_recv()
    y_copy.wait_recv()

    y_own = y[span(gh, half), :] + y_in[...].astype(f32)
    summed = jnp.swapaxes(y_own.reshape(HALF, 8, ch), 0, 1).reshape(half, ch)
    gate = gate_in[...]
    sig = sigmoid(gate)
    act = gate * sig
    grad_gated = mm(cot[...], wout[...])
    back = grad_gated * act
    back = jnp.swapaxes(back.reshape(8, HALF, ch), 0, 1).reshape(half, ch)
    g[span(gh, half), :] = back
    g_send[...] = back.astype(bf16)
    g_copy = net.copy(g_send, g_in, net.over_x())
    gate_both[gh] = (grad_gated * summed * sig * (1.0 + gate * (1.0 - sig))).astype(bf16)
    gate_copy = net.copy(gate_both.at[gh], gate_both.at[gh], net.over_x())
    low = (summed * act).astype(bf16)
    gated[...] = low
    mixed_part[...] = mm_nt(low, wout[...]).astype(bf16).reshape(mixed_part.shape)
    mixed_copy = net.copy(mixed_part.at[:, 1 - i], mixed_core, net.sibling())
    part_out = mm_tn(cot[...], gated[...]).astype(bf16)
    for q in range(ZS):
        for r in range(reps):
            at = (q * reps + r) * 2 * piece
            out_send[r, q * 2 * piece : (q + 1) * 2 * piece, :] = part_out[at : at + 2 * piece, :]
    out_copies = [
        net.copy(out_send.at[net.y_at(d)], out_y.at[d - 1], net.along_y(d)) for d in range(1, reps)
    ]

    state[...] = jnp.zeros_like(state)
    acc_ref[...] = jnp.zeros_like(acc_ref)
    bias_acc[...] = jnp.zeros_like(bias_acc)
    skip_acc[...] = jnp.zeros_like(skip_acc)

    def backward(c, carry):
        block = (1 - s) * (2 * rounds - 1 - c) + s * c
        rows, pre, values = prepare(block)
        s1[...] = jnp.zeros_like(s1)
        s2[...] = jnp.zeros_like(s2)
        for n0 in range(0, STATE, NSTEP):
            rate = rates(n0)

            def body(k, both):
                lams, accs = both
                r = s * k + (1 - s) * (CHUNK - 1 - k)
                t = block * CHUNK + r
                here = rows8(r)
                pv = proj[rows8(t), :]
                gv = g[rows8(t), :]
                uv = u[here, :]
                stv = step[here, :]
                st = decay_step[here, :]
                one = s1[here, :]
                two = s2[here, :]
                new_lams, new_accs = [], []
                for m in range(NSTEP):
                    n = n0 + m
                    a = jnp.exp2(st * rate[m])
                    ah = a * hprev[t, n]
                    lam = gv * pv[:, DT_RANK + STATE + n : DT_RANK + STATE + n + 1] + lams[m]
                    w = lam * ah
                    new_lams.append(a * lam)
                    two = two + rate[m] * w
                    new_accs.append(accs[m] + stv * w)
                    one = one + lam * pv[:, DT_RANK + n : DT_RANK + n + 1]
                    pb[here, 128 * n : 128 * n + 128] = tiles(lam * uv)
                    pc[here, 128 * n : 128 * n + 128] = tiles(gv * ah)
                s1[here, :] = one
                s2[here, :] = two
                return tuple(new_lams), tuple(new_accs)

            first = (
                tuple(state[n] for n in range(n0, n0 + NSTEP)),
                tuple(acc_ref[n] for n in range(n0, n0 + NSTEP)),
            )
            lams, accs = lax.fori_loop(0, CHUNK, body, first, unroll=CHUNK)
            for m in range(NSTEP):
                state[n0 + m] = lams[m]
                acc_ref[n0 + m] = accs[m]
        gv = g[rows, :]
        one = s1[...]
        grad_values[rows, :] = gv * skip + step[...] * one
        q = (LN2 * s2[...] + values * one) * sigmoid(pre)
        q_low = q.astype(bf16)
        bias_acc[...] += jnp.sum(q.reshape(CHUNK, 8, ch), axis=0)
        skip_acc[...] += jnp.sum((gv * values).reshape(CHUNK, 8, ch), axis=0)
        rank = proj_low[rows, :]
        rows_grad[0:DT_RANK, :] += mm_tn(rank, q_low)[0:DT_RANK, :]
        gu = jnp.sum(gv * u[...], axis=1, keepdims=True)
        lane = lax.broadcasted_iota(jnp.int32, (size, 128), 1)
        inject = jnp.where(lane >= DT_RANK + STATE, pltpu.roll(proj[rows, :], STATE, 1), 0.0)
        part[rows, :] = (
            mm_nt(q_low, wstep)
            + mm(pb[...].astype(bf16), ones[0])
            + mm(pc[...].astype(bf16), ones[1])
            + gu * inject
        )
        return carry

    lax.fori_loop(0, 1, backward, 0)
    mixed_copy.wait_recv()
    for q in range(ZS):
        mixed_low[q] = (mixed_part[q, i].astype(f32) + mixed_core[q].astype(f32)).astype(bf16)
    mixed_zs = [net.copy(mixed_low.at[net.flip(m)], mixed_z.at[m - 1], net.along_z(m)) for m in range(1, ZS)]
    lax.fori_loop(1, 2, backward, 0)
    for c in out_copies:
        c.wait_recv()
    total = out_send[yi].astype(f32)
    for d in range(1, reps):
        total = total + out_y[d - 1].astype(f32)
    total = total.astype(bf16)
    for q in range(TP):
        out_low[q] = total[q * piece : (q + 1) * piece]
    out_zs = []
    for m in range(1, TP):
        zm, im = net.shared(m)
        out_zs.append(net.copy(out_low.at[zm * 2 + im], out_all.at[z * 2 + i], net.to_shared(m)))
    out_all[z * 2 + i] = out_low[z * 2 + i]
    lax.fori_loop(2, rounds, backward, 0)
    g_copy.wait_recv()
    g[span(s, half), :] = g_in[...].astype(f32)
    lax.fori_loop(rounds, 2 * rounds, backward, 0)

    sum_proj = Reduce(net, part, fold, low_out, low_in, grad_proj)
    rows_grad[STEP_ROW : STEP_ROW + 1, :] = jnp.sum(bias_acc[...], axis=0, keepdims=True)
    rows_grad[SKIP_ROW : SKIP_ROW + 1, :] = jnp.sum(skip_acc[...], axis=0, keepdims=True)
    for n in range(STATE):
        rows_grad[DECAY_ROW + n : DECAY_ROW + n + 1, :] = (
            jnp.sum(acc_ref[n], axis=0, keepdims=True) * rate_ref[n : n + 1, :] * LN2
        )
    sum_proj.across_z()
    for c in mixed_zs:
        c.wait_recv()
    total = mixed_part[z, i].astype(f32) + mixed_core[z].astype(f32)
    for m in range(1, ZS):
        total = total + mixed_z[m - 1].astype(f32)
    mixed_sum[...] = (total + tokens[span(gh, HALF), :].astype(f32)).astype(bf16)
    mixed_home = net.copy(mixed_sum, mixed, net.over_x())
    gate_copy.wait_recv()
    part_z = mm_tn(gate_both[0], normed[0]) + mm_tn(gate_both[1], normed[1])
    for r in range(reps):
        wz_low[r] = part_z[r * cols : (r + 1) * cols].astype(bf16)
    wz_copies = [
        net.copy(wz_low.at[net.y_at(d)], wz_in.at[d - 1], net.along_y(d)) for d in range(1, reps)
    ]
    sum_proj.give()
    for c in out_zs:
        c.wait_recv()
    out_home = net.copy(out_all.at[pl.ds((1 - s) * ZS, ZS)], out_x, net.over_x())
    sum_proj.end()
    total = wz_low[yi].astype(f32)
    for d in range(1, reps):
        wz_copies[d - 1].wait_recv()
        total = total + wz_in[d - 1].astype(f32)
    grad_wz[...] = total
    out_home.wait_recv()
    for q in range(ZS):
        total = out_all[s * ZS + q].astype(f32) + out_x[q].astype(f32)
        for r in range(reps):
            at = ((q // 2) * reps + r) * 2 + q % 2
            grad_wout[:, at * cols : (at + 1) * cols] = total[:, r * cols : (r + 1) * cols]
    mixed_home.wait_recv()
    net.finish()


def core(reps, proj, conv_out, small, ends, tokens, gate_in, wout, cot, normed):
    rows, ch = conv_out.shape
    half = rows // 2
    cols = ch // reps
    width = tokens.shape[1]
    piece = width // (TP * reps)
    V, H = pltpu.VMEM, pl.ANY
    args = [(proj, V), (conv_out, V), (small, V), (ends, V), (tokens, V)]
    args += [(gate_in, H), (wout, H), (cot, H), (normed, H)]
    sds = jax.ShapeDtypeStruct
    outs = (
        (sds((rows, ch), f32), V),
        (sds((rows, 128), bf16), V),
        (sds((2, half, ch), bf16), V),
        (sds((HALF, width), bf16), V),
        (sds((SMALL_ROWS, ch), f32), V),
        (sds((piece, ZS * ch), f32), V),
        (sds((cols, width // 2), f32), V),
    )
    size = CHUNK * 8
    scratch = (
        V((half, ch), f32),
        V((reps, TP, reps, piece, cols), bf16),
        V((width, ch), bf16),
        V((half, width), bf16),
        V((2, half, width // 2), bf16),
        V((2, STATE * 128, 128), bf16),
        V((PACK, STATE, 8, ch), f32),
        V((rows, 128), f32),
        V((size, ch), f32),
        V((size, ch), f32),
        V((size, ch), f32),
        V((STATE, 8, ch), f32),
        V((STATE, 8, ch), f32),
        V((STATE, ch), f32),
        V((half, ch), bf16),
        V((half, ch), bf16),
        V((half, ch), bf16),
        V((ZS, 2, HALF, width), bf16),
        V((ZS, HALF, width), bf16),
        V((ZS, HALF, width), bf16),
        V((ZS - 1, HALF, width), bf16),
        V((HALF, width), bf16),
        V((half, ch), bf16),
        V((half, ch), bf16),
        V((size, ch), f32),
        V((size, ch), f32),
        V((size, STATE * 128), f32),
        V((size, STATE * 128), f32),
        V((8, ch), f32),
        V((8, ch), f32),
        V((rows, 128), f32),
        V((reps, TP * piece, ch), bf16),
        V((reps - 1, TP * piece, ch), bf16),
        V((TP, piece, ch), bf16),
        V((TP, piece, ch), bf16),
        V((ZS, piece, ch), bf16),
        V((reps, cols, width // 2), bf16),
        V((reps - 1, cols, width // 2), bf16),
    ) + REDUCE_SCRATCH
    copies = 7 + 27 + 3 * (reps - 1)
    return fused(partial(core_kernel, reps), 2, copies, 4, outs, args, scratch)


def back_kernel(
    reps,
    grad_values, grad_proj, conv_pre, small, wstate, ends_in, gate_both, tokens, cot, gain, rows_in,
    conv_in_hbm, conv_out_hbm, wx_hbm, wz_hbm, normed_hbm, tok_hbm,
    grad_tokens, grad_gain, grad_wx, grad_taps, grad_bias, grad_step, grad_skip, grad_decay, grad_wstep, grad_wstate,
    conv_in, conv_out, wx, wz, normed, tok_all, w, slots, sums, gx, gx_in, part, core_in, low, z_in, gain_acc, gain_in,
    wx_low, wx_in, rows_part, rows_recv, state_part, state_in, send, recv, local,
):
    net = Net(reps, send, recv, local)
    s, z, yi, i = net.s, net.z, net.y, net.i
    sgn = 1 - 2 * s
    ch = conv_out.shape[1]
    cols = ch // reps
    width = tokens.shape[1]
    half = TP * HALF
    load_conv_in = net.load(conv_in_hbm, conv_in)
    load_w = [net.load(wx_hbm, wx), net.load(wz_hbm, wz)]
    load_tok = net.load(tok_hbm, tok_all)
    load_rest = [net.load(conv_out_hbm, conv_out), net.load(normed_hbm, normed)]
    net.greet()
    w[0:PAD, :] = jnp.zeros((PAD, ch), f32)
    w[PAD + 8 * PACK :, :] = jnp.zeros((PAD, ch), f32)

    def pull(b, carry):
        rows = span(b, 256)
        c = conv_pre[rows, :]
        sig = sigmoid(c)
        w[pl.ds(pl.multiple_of(PAD + b * 256, 8), 256), :] = (
            grad_values[rows, :] + mm_nt(grad_proj[rows, :], wstate[...])
        ) * (sig * (1.0 + c * (1.0 - sig)))
        return carry

    lax.fori_loop(0, 4, pull, 0)
    sums[...] = jnp.zeros_like(sums)
    ends = (ends_in[0], ends_in[1])
    taps = small[TAP_ROW : TAP_ROW + 16, :].astype(f32)

    def conv_step(t, carry):
        seg = segment_of(t, ends)
        here = w[rows8(t + 3), :]
        total = taps[3:4, :] * here
        sums[3] += here * conv_in[rows8(t + 3), :]
        sums[4] += here
        for k in range(1, TAPS):
            back = t - k * sgn
            ahead = t + k * sgn
            same_back = wide((segment_of(back, ends) == seg).astype(f32), ch)
            same_ahead = wide((segment_of(ahead, ends) == seg).astype(f32), ch)
            sums[3 - k] += here * (conv_in[rows8(back + 3), :] * same_back)
            total = total + taps[3 - k : 4 - k, :] * (w[rows8(ahead + 3), :] * same_ahead)
        slots[rows8(t), :] = total
        return carry

    gx_copies = []
    load_conv_in.wait()
    for h in (1 - s, s):
        lax.fori_loop(h * HALF, (h + 1) * HALF, conv_step, 0)
        x = slots[span(h, half), :]
        gx[h] = jnp.swapaxes(x.reshape(HALF, 8, ch), 0, 1).reshape(half, ch).astype(bf16)
        gx_copies.append(net.copy(gx.at[h], gx_in.at[h], net.over_x()))

    def rows_of(b, carry):
        rows = span(b, 2 * HALF)
        value = (
            mm(gx[s, rows, :], wx[...])
            + mm(gx_in[s, rows, :], wx[...])
            + mm(gate_both[s, rows, :], wz[...])
        )
        part[b] = value.astype(bf16).reshape(2, HALF, width)
        return carry

    for c in load_w:
        c.wait()
    gx_copies[0].wait_recv()
    lax.fori_loop(0, ZS, rows_of, 0)
    to_core = net.copy(part.at[:, 1 - i], core_in, net.sibling())

    gain_acc[0] = jnp.zeros(gain_acc.shape[1:], f32)

    def gain_terms(b, carry):
        rows = pl.ds(pl.multiple_of(b * PACK + s * HALF, HALF), HALF)
        x = tok_all[rows, :].astype(f32)
        inv = lax.rsqrt(jnp.mean(x * x, axis=1, keepdims=True) + EPS)
        terms = part[b // 2, lax.rem(b, 2)].astype(f32) * (x * inv)
        gain_acc[0] += jnp.sum(terms.reshape(HALF // 8, 8, width), axis=0)
        return carry

    to_core.wait_recv()
    for q in range(ZS):
        low[q] = (part[q, i].astype(f32) + core_in[q].astype(f32)).astype(bf16)
    to_z = [net.copy(low.at[net.flip(m)], z_in.at[m - 1], net.along_z(m)) for m in range(1, ZS)]
    load_tok.wait()
    lax.fori_loop(0, TP, gain_terms, 0)
    stages = [
        [net.sibling()],
        [net.over_x()],
        [net.along_y(d) for d in range(1, reps)],
        [net.along_z(1)],
        [net.along_z(2)],
    ]
    slot = [0]

    def gain_start(k):
        cs = []
        for peer in stages[k]:
            cs.append((slot[0], net.copy(gain_acc.at[k], gain_in.at[slot[0]], peer)))
            slot[0] += 1
        return cs

    def gain_end(k, cs):
        total = gain_acc[k]
        for at, c in cs:
            c.wait_recv()
            total = total + gain_in[at]
        gain_acc[k + 1] = total

    cs = gain_start(0)
    for c in load_rest:
        c.wait()
    state_all = mm_tn(conv_out[...].astype(bf16), grad_proj[...])
    for r in range(reps):
        state_part[r] = state_all[r * cols : (r + 1) * cols, :]
        rows_part[r] = rows_in[:, r * cols : (r + 1) * cols]
        for n in range(TAPS + 1):
            row = jnp.sum(sums[n], axis=0, keepdims=True)
            rows_part[r, TAP_ROW + n : TAP_ROW + n + 1, :] = row[:, r * cols : (r + 1) * cols]
    state_copies = [
        net.copy(state_part.at[net.y_at(d)], state_in.at[d - 1], net.along_y(d)) for d in range(1, reps)
    ]
    rows_copies = [
        net.copy(rows_part.at[net.y_at(d)], rows_recv.at[d - 1], net.along_y(d)) for d in range(1, reps)
    ]
    gain_end(0, cs)
    cs = gain_start(1)
    own = pl.ds(pl.multiple_of(s * (width // 2), 128), width // 2)
    gx_copies[1].wait_recv()
    part_x = mm_tn(gx[0], normed[0, :, own]) + mm_tn(gx[1], normed[1, :, own])
    part_x = part_x + mm_tn(gx_in[0], normed[0, :, own]) + mm_tn(gx_in[1], normed[1, :, own])
    for r in range(reps):
        wx_low[r] = part_x[r * cols : (r + 1) * cols].astype(bf16)
    wx_copies = [
        net.copy(wx_low.at[net.y_at(d)], wx_in.at[d - 1], net.along_y(d)) for d in range(1, reps)
    ]
    gain_end(1, cs)
    cs = gain_start(2)
    gain_end(2, cs)
    cs = gain_start(3)
    x = tokens[span(s, HALF), :].astype(f32)
    inv = lax.rsqrt(jnp.mean(x * x, axis=1, keepdims=True) + EPS)
    unit = x * inv
    gain_end(3, cs)
    cs = gain_start(4)
    grad = part[z, i].astype(f32) + core_in[z].astype(f32)
    for m in range(1, ZS):
        to_z[m - 1].wait_recv()
        grad = grad + z_in[m - 1].astype(f32)
    scaled = grad * gain[...]
    mean = jnp.mean(scaled * unit, axis=1, keepdims=True)
    grad_tokens[...] = inv * (scaled - unit * mean) + cot[...].astype(f32)
    gain_end(4, cs)
    grad_gain[...] = jnp.sum(gain_acc[5], axis=0, keepdims=True)
    total = rows_part[yi]
    for d in range(1, reps):
        rows_copies[d - 1].wait_recv()
        total = total + rows_recv[d - 1]
    grad_wstep[...] = total[0:DT_RANK]
    grad_taps[...] = total[TAP_ROW : TAP_ROW + TAPS]
    grad_bias[...] = total[BIAS_ROW : BIAS_ROW + 1]
    grad_step[...] = total[STEP_ROW : STEP_ROW + 1]
    grad_skip[...] = total[SKIP_ROW : SKIP_ROW + 1]
    grad_decay[...] = total[DECAY_ROW : DECAY_ROW + STATE]
    total = state_part[yi]
    for d in range(1, reps):
        state_copies[d - 1].wait_recv()
        total = total + state_in[d - 1]
    grad_wstate[...] = total
    total = wx_low[yi].astype(f32)
    for d in range(1, reps):
        wx_copies[d - 1].wait_recv()
        total = total + wx_in[d - 1].astype(f32)
    grad_wx[...] = total
    net.finish()


def backward(
    reps, grad_values, grad_proj, conv_pre, small, wstate, ends, gate_both, tokens, cot, gain, rows_in,
    conv_in, conv_out, wx, wz, normed, tok_all,
):
    rows, ch = conv_out.shape
    half = rows // 2
    cols = ch // reps
    width = tokens.shape[1]
    V, H = pltpu.VMEM, pl.ANY
    near = (grad_values, grad_proj, conv_pre, small, wstate, ends, gate_both, tokens, cot, gain, rows_in)
    far = (conv_in, conv_out, wx, wz, normed, tok_all)
    args = [(a, V) for a in near] + [(a, H) for a in far]
    sds = jax.ShapeDtypeStruct
    outs = (
        sds((HALF, width), f32),
        sds((1, width), f32),
        sds((cols, width // 2), f32),
        sds((TAPS, cols), f32),
        sds((1, cols), f32),
        sds((1, cols), f32),
        sds((1, cols), f32),
        sds((STATE, cols), f32),
        sds((DT_RANK, cols), f32),
        sds((cols, 128), f32),
    )
    scratch = tuple(V(a.shape, a.dtype) for a in far) + (
        V((rows + 2 * PAD, ch), f32),
        V((rows, ch), f32),
        V((TAPS + 1, 8, ch), f32),
        V((2, half, ch), bf16),
        V((2, half, ch), bf16),
        V((ZS, 2, HALF, width), bf16),
        V((ZS, HALF, width), bf16),
        V((ZS, HALF, width), bf16),
        V((ZS - 1, HALF, width), bf16),
        V((6, 8, width), f32),
        V((3 + reps, 8, width), f32),
        V((reps, cols, width // 2), bf16),
        V((reps - 1, cols, width // 2), bf16),
        V((reps, SMALL_ROWS, cols), f32),
        V((reps - 1, SMALL_ROWS, cols), f32),
        V((reps, cols, 128), f32),
        V((reps - 1, cols, 128), f32),
    )
    copies = 2 + 1 + 3 + 4 + 4 * (reps - 1)
    return fused(partial(back_kernel, reps), 3, copies, 6, [(o, V) for o in outs], args, scratch)


def place_kernel(index, gain, *refs):
    count = (len(refs) - 1) // 2
    for source, target in zip(refs[:count], refs[count : 2 * count]):
        target[...] = source[...]
    gain_out = refs[-1]
    width, n = gain.shape[1], gain_out.shape[1]
    moved = pltpu.roll(jnp.broadcast_to(gain[...], (8, width)), width - index[0] * n, 1)
    gain_out[...] = moved[0:1, 0:n]


def place(index, gain, n, *results):
    V = pl.BlockSpec(memory_space=pltpu.VMEM)
    return pl.pallas_call(
        place_kernel,
        out_shape=tuple(jax.ShapeDtypeStruct(r.shape, r.dtype) for r in results)
        + (jax.ShapeDtypeStruct((1, n), f32),),
        in_specs=[pl.BlockSpec(memory_space=pltpu.SMEM), V] + [V] * len(results),
        out_specs=tuple([V] * (len(results) + 1)),
    )(index, gain, *results)

def local(
    reps, tokens, item_grids, norm_gain, proj_in_x, proj_in_z, proj_out, conv_weight, conv_bias,
    proj_state, proj_step, step_bias, decay_log, skip_gain, grad_out,
):
    width = tokens.shape[1]
    cot = grad_out.reshape(HALF, width)
    (
        normed, conv_in, conv_pre, conv_out, gate_in, tok_all, wx, wz, wout, cot_other,
        proj, gain, ends, small, wstate,
    ) = front(
        reps, item_grids, tokens, norm_gain[None], proj_in_x.T, proj_in_z.T, proj_step[0], conv_weight[0],
        conv_bias, step_bias, skip_gain, decay_log[0], proj_state[0], proj_out.T, cot,
    )
    grad_values, grad_proj, gate_both, mixed, rows_grad, grad_wout, grad_wz = core(
        reps, proj, conv_out, small, ends, tokens, gate_in, wout, cot_other, normed
    )
    (
        grad_tokens, grad_gain, grad_wx, grad_taps, grad_bias, grad_step, grad_skip, grad_decay,
        grad_wstep, grad_wstate,
    ) = backward(
        reps, grad_values, grad_proj, conv_pre, small, wstate, ends, gate_both, tokens, cot, gain, rows_grad,
        conv_in, conv_out, wx, wz, normed, tok_all,
    )
    index = (lax.axis_index("dir") * lax.axis_size("dp") + lax.axis_index("dp")).astype(jnp.int32)
    (
        mixed, grad_tokens, grad_wx, grad_wz, grad_wout, grad_taps, grad_bias, grad_wstate, grad_wstep,
        grad_step, grad_decay, grad_skip, grad_gain,
    ) = place(
        index.reshape(1), grad_gain, width // (2 * TP * reps),
        mixed, grad_tokens, grad_wx, grad_wz, grad_wout, grad_taps, grad_bias, grad_wstate, grad_wstep,
        grad_step, grad_decay, grad_skip,
    )
    return (
        mixed.reshape(1, 1, HALF, width),
        grad_tokens.reshape(1, 1, HALF, width),
        grad_gain[0],
        grad_wx.T,
        grad_wz.T,
        grad_wout.T,
        grad_taps[None],
        grad_bias,
        grad_wstate[None],
        grad_wstep[None],
        grad_step,
        grad_decay[None],
        grad_skip,
    )


def solution(mesh):
    reps = mesh.shape["dp"] // TP
    return jax.shard_map(
        partial(local, reps),
        mesh=mesh,
        in_specs=(
            P("dp", None),
            P("dp", None),
            P("dp"),
            P(None, "dp"),
            P(None, "dp"),
            P(None, "dp"),
            P("dir", None, "dp"),
            P("dir", "dp"),
            P("dir", "dp", None),
            P("dir", None, "dp"),
            P("dir", "dp"),
            P("dir", None, "dp"),
            P("dir", "dp"),
            P("dp", "dir", None, None),
        ),
        out_specs=(
            P("dp", "dir", None, None),
            P("dp", "dir", None, None),
            P(("dir", "dp")),
            P("dir", "dp"),
            P("dir", "dp"),
            P("dir", "dp"),
            P("dir", None, "dp"),
            P("dir", "dp"),
            P("dir", "dp", None),
            P("dir", None, "dp"),
            P("dir", "dp"),
            P("dir", None, "dp"),
            P("dir", "dp"),
        ),
        check_vma=False,
    )
```

```python
from functools import partial

import jax
import jax.numpy as jnp
from jax import lax
from jax.experimental import pallas as pl
from jax.experimental.pallas import tpu as pltpu
from jax.sharding import PartitionSpec as P

f32 = jnp.float32
bf16 = jnp.bfloat16
EPS = 1e-05
DT_RANK = 96
STATE = 16
TAPS = 4
ZS = 4
TP = 8
PACK = 128
HALF = 64
CHUNK = 16
NSTEP = 4
LOG2E = 1.4426950408889634
LN2 = 0.6931471805599453
BIG = 1e9
PAD = 24
TAP_ROW, BIAS_ROW, STEP_ROW, SKIP_ROW, DECAY_ROW, SMALL_ROWS = 96, 100, 101, 102, 103, 128


def mm(left, right):
    return jnp.dot(left, right, preferred_element_type=f32)


def mm_nt(left, right):
    return lax.dot_general(left, right, (((1,), (1,)), ((), ())), preferred_element_type=f32)


def mm_tn(left, right):
    return lax.dot_general(left, right, (((0,), (0,)), ((), ())), preferred_element_type=f32)


def segment_of(t, ends):
    t = t.astype(f32) if hasattr(t, "astype") else float(t)
    return (t >= ends[0]).astype(f32) + (t >= ends[1]).astype(f32)


def rows8(t):
    return pl.ds(pl.multiple_of(t * 8, 8), 8)


def span(start, size):
    return pl.ds(pl.multiple_of(start * size, size), size)


def sigmoid(v):
    return 1.0 / (1.0 + jnp.exp(-v))


def softplus(v):
    return jnp.maximum(v, 0.0) + jnp.log1p(jnp.exp(-jnp.abs(v)))


def wide(mask, ch):
    return jnp.concatenate([mask] * (ch // 128), axis=1)


def tiles(v):
    total = v[:, 0:128]
    for at in range(128, v.shape[1], 128):
        total = total + v[:, at : at + 128]
    return total


class Copy:
    def __init__(self, copy):
        self.copy, self.sent, self.got = copy, False, False
        copy.start()

    def wait_send(self):
        if not self.sent:
            self.copy.wait_send()
            self.sent = True

    def wait_recv(self):
        if not self.got:
            self.copy.wait_recv()
            self.got = True


class Net:
    def __init__(self, reps, send, recv, local):
        self.reps, self.send, self.recv, self.local = reps, send, recv, local
        self.s = lax.axis_index("dir")
        p = lax.axis_index("dp")
        self.i = lax.rem(p, 2)
        self.y = lax.rem(p // 2, reps)
        self.z = p // (2 * reps)
        self.used = 0
        self.moved = 0
        self.copies = []
        self.saves = []

    def place(self, s, z, y, i):
        return (s, (z * self.reps + y) * 2 + i)

    def flip(self, m):
        if m == 1:
            return self.z + 1 - 2 * lax.rem(self.z, 2)
        if m == 2:
            return lax.rem(self.z + 2, ZS)
        return ZS - 1 - self.z

    def over_x(self):
        return self.place(1 - self.s, self.z, self.y, self.i)

    def sibling(self):
        return self.place(self.s, self.z, self.y, 1 - self.i)

    def along_z(self, m):
        return self.place(self.s, self.flip(m), self.y, self.i)

    def shared(self, m):
        z = self.flip(m // 2) if m // 2 else self.z
        i = 1 - self.i if m % 2 else self.i
        return z, i

    def to_shared(self, m):
        z, i = self.shared(m)
        return self.place(self.s, z, self.y, i)

    def y_at(self, d):
        return lax.rem(self.y + d, self.reps)

    def along_y(self, d):
        return self.place(self.s, self.z, self.y_at(d), self.i)

    def greet(self):
        self.peers = [self.over_x()] + [self.to_shared(m) for m in range(1, TP)]
        self.peers += [self.along_y(d) for d in range(1, self.reps)]
        barrier = pltpu.get_barrier_semaphore()
        for peer in self.peers:
            pl.semaphore_signal(barrier, inc=1, device_id=peer, device_id_type=pl.DeviceIdType.MESH)

    def met(self):
        pl.semaphore_wait(pltpu.get_barrier_semaphore(), len(self.peers))

    def copy(self, source, target, peer):
        k = self.used
        self.used += 1
        c = Copy(
            pltpu.make_async_remote_copy(
                src_ref=source,
                dst_ref=target,
                send_sem=self.send.at[k],
                recv_sem=self.recv.at[k],
                device_id=peer,
                device_id_type=pl.DeviceIdType.MESH,
            )
        )
        self.copies.append(c)
        return c

    def load(self, source, target):
        c = pltpu.make_async_copy(source, target, self.local.at[self.moved])
        self.moved += 1
        c.start()
        return c

    def save(self, source, target):
        self.saves.append(self.load(source, target))

    def finish(self):
        for c in self.copies:
            c.wait_recv()
            c.wait_send()
        for c in self.saves:
            c.wait()


class Reduce:
    def __init__(self, net, part, base, size, fold, out_low, in_low, total):
        self.net, self.part, self.base = net, part, base
        self.fold, self.out_low, self.in_low, self.total = fold, out_low, in_low, total
        self.rows = size // 2
        self.block = self.rows // ZS
        self.first = net.copy(part.at[self.at(1 - net.i, self.rows)], fold, net.sibling())

    def at(self, n, size):
        return pl.ds(pl.multiple_of(self.base + n * size, size), size)

    def across_z(self):
        net, fold = self.net, self.fold
        self.first.wait_recv()
        fold[...] = self.part[self.at(net.i, self.rows), :] + fold[...]
        self.out_low[...] = fold[...].astype(bf16).reshape(ZS, self.block, 128)
        self.cs = [
            net.copy(self.out_low.at[net.flip(m)], self.in_low.at[m - 1], net.along_z(m))
            for m in range(1, ZS)
        ]

    def give(self):
        net, total = self.net, self.total
        mine = self.at(net.i * ZS + net.z, self.block)
        value = self.fold[span(net.z, self.block), :]
        for m in range(1, ZS):
            self.cs[m - 1].wait_recv()
            value = value + self.in_low[m - 1].astype(f32)
        total[mine, :] = value.astype(bf16)
        self.cs = [net.copy(total.at[mine], total.at[mine], net.along_z(m)) for m in range(1, ZS)]
        self.ds = [net.copy(total.at[mine], total.at[mine], net.sibling())]

    def end(self):
        net, total = self.net, self.total
        for m in range(1, ZS):
            self.cs[m - 1].wait_recv()
            there = self.at(net.i * ZS + net.flip(m), self.block)
            self.ds.append(net.copy(total.at[there], total.at[there], net.sibling()))
        for d in self.ds:
            d.wait_recv()


REDUCE_ROWS = TP * HALF
REDUCE_SCRATCH = (
    pltpu.VMEM((REDUCE_ROWS // 2, 128), f32),
    pltpu.VMEM((ZS, REDUCE_ROWS // 2 // ZS, 128), bf16),
    pltpu.VMEM((ZS - 1, REDUCE_ROWS // 2 // ZS, 128), bf16),
)


def fused(kernel, name_id, copies, moves, outs, args, scratch):
    return pl.pallas_call(
        kernel,
        out_shape=tuple(o for o, _ in outs),
        in_specs=[pl.BlockSpec(memory_space=m) for _, m in args],
        out_specs=tuple(pl.BlockSpec(memory_space=m) for _, m in outs),
        scratch_shapes=list(scratch)
        + [pltpu.SemaphoreType.DMA((n,)) for n in (copies, copies, moves)],
        compiler_params=pltpu.CompilerParams(
            collective_id=name_id, has_side_effects=True, vmem_limit_bytes=63 << 20
        ),
    )(*(a for a, _ in args))


def block_kernel(reps, *refs):
    refs = list(refs)

    def take_refs(n):
        out = refs[:n]
        del refs[:n]
        return out

    (
        grids, gain_own, wstep_own, taps_own, bias_own, step_own, skip_own, decay_own, wstate_own, wout_own,
        cot_own, tokens, wx_own, wz_own,
    ) = take_refs(14)
    (
        mixed, grad_tokens, wx_mine, wx_theirs, wz_mine, wz_theirs, out_mine, out_theirs, rows_mine,
        rows_theirs, state_mine, state_theirs, grad_gain,
    ) = take_refs(13)
    (
        meta_all, gain, ends_ref, wx_all, wx, wz_all, wz, small_all, small, wstate_all, wstate,
        wout_send, wout_in, wout_all, wout,
    ) = take_refs(15)
    (tok, normed, raw, conv_in, conv_pre, conv_out, gate_in, part, proj_low, proj) = take_refs(10)
    (
        hprev, step, decay_step, u, state, acc_ref, rate_ref, s1, s2, pb, pc, ones, bias_acc, skip_acc, g,
    ) = take_refs(15)
    (y_send, y_in, g_send, g_in, gated, gate_both, cot, mixed_core, mixed_low, mixed_z, mixed_sum, tok_last) = take_refs(12)
    (out_send, out_y, out_low, out_x_in, out_all, wz_low, part_back, grad_proj, sums, gx, gx_in) = take_refs(11)
    (wx_low, rows_grad, rows_part, state_part, gain_acc, gain_in) = take_refs(6)
    reduces = [take_refs(3) for _ in range(4)]
    send, recv, local_sems = refs
    net = Net(reps, send, recv, local_sems)
    net.greet()
    s, z, yi, i = net.s, net.z, net.y, net.i
    sgn = 1 - 2 * s
    gh = 1 - s
    j = z * 2 + i
    cols, width = wx_own.shape
    ch = reps * cols
    piece = wout_own.shape[0]
    half = TP * HALF
    rounds = HALF // CHUNK
    size = CHUNK * 8
    share = piece % 32 == 0
    hp = piece // 2 if share else piece
    own_part = pl.ds(pl.multiple_of(s * hp, hp), hp) if share else pl.ds(0, piece)
    half_cols = pl.ds(pl.multiple_of(s * (width // 2), 128), width // 2)

    own_loads = [net.load(tokens.at[pl.ds(h * HALF, HALF)], tok.at[h, z, i]) for h in range(2)]
    own_loads += [net.load(wx_own, wx_all.at[yi]), net.load(wz_own, wz_all.at[yi])]
    own_loads += [net.load(tokens.at[pl.ds(pl.multiple_of(gh * HALF, HALF), HALF)], tok_last)]
    first_end = (grids[0, 0] * grids[0, 1]).astype(f32)
    second_end = first_end + (grids[1, 0] * grids[1, 1]).astype(f32)
    row = lax.broadcasted_iota(jnp.int32, (16, 128), 0)
    gain_row = jnp.concatenate([gain_own[...].astype(f32), jnp.zeros((1, 128 - piece), f32)], axis=1)
    meta = jnp.where(row == 0, gain_row, jnp.where(row == 1, first_end, second_end))
    meta_all[yi, j] = meta.astype(bf16)
    small_rows = [ref[...].astype(f32) for ref in (wstep_own, taps_own, bias_own, step_own, skip_own, decay_own)]
    small_rows.append(jnp.zeros((SMALL_ROWS - DECAY_ROW - STATE, cols), f32))
    small_all[yi] = jnp.concatenate(small_rows, axis=0).astype(bf16)
    wstate_all[yi] = wstate_own[...]
    net.met()
    own_first = tokens.at[pl.ds(pl.multiple_of(s * HALF, HALF), HALF)]
    own_last = tokens.at[pl.ds(pl.multiple_of(gh * HALF, HALF), HALF)]
    from_z = [net.copy(own_first, tok.at[s, z, i], net.along_z(m)) for m in range(1, ZS)]
    core_first = [net.copy(own_first, tok.at[s, z, i], net.sibling())]
    core_last = [net.copy(own_last, tok.at[gh, z, i], net.sibling())]
    metas = [net.copy(meta_all.at[yi, j], meta_all.at[yi, j], net.to_shared(m)) for m in range(1, TP)]
    first_y = []
    for d in range(1, reps):
        first_y.append(net.copy(wx_own, wx_all.at[yi], net.along_y(d)))
        for ref in (small_all, wstate_all):
            first_y.append(net.copy(ref.at[yi], ref.at[yi], net.along_y(d)))
    cot_mine = span(j, HALF)
    cot_x = net.copy(cot_own, cot.at[cot_mine], net.over_x())
    for c in metas:
        c.wait_recv()
    meta_y = [net.copy(meta_all.at[yi], meta_all.at[yi], net.along_y(d)) for d in range(1, reps)]
    late_y = [net.copy(wz_own, wz_all.at[yi], net.along_y(d)) for d in range(1, reps)]

    for ref in (conv_in, conv_pre):
        ref[0:PAD, :] = jnp.zeros((PAD, ch), f32)
        ref[PAD + 8 * PACK :, :] = jnp.zeros((PAD, ch), f32)
    for b in range(TP):
        both = meta_all[yi, b].astype(f32)
        ends_ref[0, b : b + 1, :] = both[1:2, :]
        ends_ref[1, b : b + 1, :] = both[2:3, :]
    for p in range(TP * reps):
        zp, yp, ip = p // (2 * reps), (p // 2) % reps, p % 2
        wout_send[zp * 2 + ip, :, yp * cols : (yp + 1) * cols] = wout_own[:, p * cols : (p + 1) * cols]
    wout_in[j, own_part] = wout_send[j, own_part]
    source = lax.broadcasted_iota(jnp.int32, (STATE * 128, 128), 0) // 128
    target = lax.broadcasted_iota(jnp.int32, (STATE * 128, 128), 1)
    ones[...] = (target == DT_RANK + source).astype(f32).astype(bf16)
    rows_grad[...] = jnp.zeros_like(rows_grad)
    state[...] = jnp.zeros_like(state)
    for c in own_loads:
        c.wait()

    from_x = []
    for m in range(1, ZS):
        from_z[m - 1].wait_recv()
        there = tok.at[s, net.flip(m), i]
        core_first.append(net.copy(there, there, net.sibling()))
        from_x.append(net.copy(there, there, net.over_x()))
    wout_z = []
    for m in range(1, TP):
        zm, im = net.shared(m)
        wout_z.append(net.copy(wout_send.at[zm * 2 + im, own_part], wout_in.at[j, own_part], net.to_shared(m)))
    cot_x.wait_recv()
    cot_z = [net.copy(cot.at[cot_mine], cot.at[cot_mine], net.along_z(m)) for m in range(1, ZS)]
    cot_core = [net.copy(cot.at[cot_mine], cot.at[cot_mine], net.sibling())]
    for c in meta_y + first_y:
        c.wait_recv()
    for p in range(TP * reps):
        zp, yp, ip = p // (2 * reps), (p // 2) % reps, p % 2
        gain[:, p * piece : (p + 1) * piece] = meta_all[yp, zp * 2 + ip].astype(f32)[0:1, 0:piece]
    for r in range(reps):
        wx[r * cols : (r + 1) * cols, :] = wx_all[r]
        small[:, r * cols : (r + 1) * cols] = small_all[r]
        wstate[r * cols : (r + 1) * cols, :] = wstate_all[r]
    for c in core_first:
        c.wait_recv()

    ends = (ends_ref[0], ends_ref[1])
    vectors = small[DT_RANK : DT_RANK + 16, :].astype(f32)
    taps = vectors[0 : TAPS + 1, :]
    step_bias = vectors[STEP_ROW - DT_RANK : STEP_ROW - DT_RANK + 1, :]
    skip = vectors[SKIP_ROW - DT_RANK : SKIP_ROW - DT_RANK + 1, :]

    def take(h):
        def one(q, carry):
            rows = span(q, PACK)
            x = tok[h, q].astype(f32).reshape(PACK, width)
            inv = lax.rsqrt(jnp.mean(x * x, axis=1, keepdims=True) + EPS)
            low = (x * inv * gain[...]).astype(bf16)
            normed[h, rows, :] = low
            raw[rows, :] = mm_nt(low, wx[...])
            return carry

        lax.fori_loop(0, ZS, one, 0)
        x = jnp.swapaxes(raw[...].reshape(8, HALF, ch), 0, 1).reshape(half, ch)
        conv_in[pl.ds(pl.multiple_of(PAD + h * half, 8), half), :] = x

    def convolve(h, sums):
        def one(k, carry):
            t = h * HALF + k
            seg = segment_of(t, ends)
            total = taps[4:5, :] + taps[3:4, :] * conv_in[rows8(t + 3), :]
            for n in range(1, TAPS):
                there = t - n * sgn
                same = wide((segment_of(there, ends) == seg).astype(f32), ch)
                total = total + taps[3 - n : 4 - n, :] * (conv_in[rows8(there + 3), :] * same)
            conv_pre[rows8(t + 3), :] = total
            act = total * sigmoid(total)
            conv_out[rows8(t), :] = act.astype(bf16).astype(f32)
            return carry

        lax.fori_loop(0, HALF, one, 0, unroll=4)
        rows = span(h, half)
        part[rows, :] = mm(conv_out[rows, :].astype(bf16), wstate[...])
        return Reduce(net, part, h * half, half, *sums, proj_low)

    take(s)
    sum_first = convolve(s, reduces[0])
    for m in range(1, ZS):
        from_x[m - 1].wait_recv()
        there = tok.at[gh, net.flip(m), i]
        core_last.append(net.copy(there, there, net.sibling()))
    sum_first.across_z()
    for c in wout_z:
        c.wait_recv()
    wout_x = [net.copy(wout_in.at[:, own_part], wout_in.at[:, own_part], net.over_x())] if share else []
    for c in core_last:
        c.wait_recv()
    take(gh)
    sum_first.give()
    sum_last = convolve(gh, reduces[1])
    for c in late_y:
        c.wait_recv()
    for r in range(reps):
        wz[r * cols : (r + 1) * cols, :] = wz_all[r]
    sum_first.end()
    first_rows = span(s, half)
    last_rows = span(gh, half)
    proj[first_rows, :] = proj_low[first_rows, :].astype(f32)

    wstep = jnp.where(lax.broadcasted_iota(jnp.int32, (128, ch), 0) < DT_RANK, small[...], 0.0).astype(bf16)
    rate_ref[...] = -LOG2E * jnp.exp(small[DT_RANK:, :].astype(f32)[DECAY_ROW - DT_RANK : DECAY_ROW - DT_RANK + STATE, :])
    y = g

    def prepare(block):
        rows = span(block, size)
        pre = mm(proj_low[rows, :], wstep) + step_bias
        step_all = softplus(pre)
        values = conv_out[rows, :]
        step[...] = step_all
        u[...] = step_all * values
        for k in range(CHUNK):
            t = block * CHUNK + k
            fresh = segment_of(t, ends) != segment_of(t - sgn, ends)
            decay_step[8 * k : 8 * k + 8, :] = jnp.where(
                wide(fresh, ch), BIG, step_all[8 * k : 8 * k + 8, :]
            )
        return rows, pre, values

    def rates(n0):
        return [jnp.broadcast_to(rate_ref[n : n + 1, :], (8, ch)) for n in range(n0, n0 + NSTEP)]

    def forward(c, carry):
        block = c + s * (2 * rounds - 1 - 2 * c)
        rows, _, values = prepare(block)
        y[rows, :] = skip * values
        for n0 in range(0, STATE, NSTEP):
            rate = rates(n0)

            def body(k, hs):
                r = s * (CHUNK - 1 - k) + (1 - s) * k
                t = block * CHUNK + r
                pv = proj[rows8(t), :]
                st = decay_step[rows8(r), :]
                uv = u[rows8(r), :]
                total = y[rows8(t), :]
                new = []
                for m in range(NSTEP):
                    n = n0 + m
                    if m % 2 == 0:
                        hprev[t, n // 2] = jnp.concatenate([hs[m], hs[m + 1]], axis=0).astype(bf16)
                    h = jnp.exp2(st * rate[m]) * hs[m] + uv * pv[:, DT_RANK + n : DT_RANK + n + 1]
                    total = total + h * pv[:, DT_RANK + STATE + n : DT_RANK + STATE + n + 1]
                    new.append(h)
                y[rows8(t), :] = total
                return tuple(new)

            hs = lax.fori_loop(0, CHUNK, body, tuple(state[n] for n in range(n0, n0 + NSTEP)), unroll=CHUNK)
            for m in range(NSTEP):
                state[n0 + m] = hs[m]
        return carry

    sum_last.across_z()
    for c in wout_x:
        c.wait_recv()
    wout_y = [net.copy(wout_in, wout_all.at[yi], net.along_y(d)) for d in range(1, reps)]
    wout_all[yi] = wout_in[...]
    lax.fori_loop(0, rounds // 2, forward, 0)
    sum_last.give()
    lax.fori_loop(rounds // 2, rounds, forward, 0)
    y_send[...] = y[first_rows, :].astype(bf16)
    y_copy = net.copy(y_send, y_in, net.over_x())
    sum_last.end()
    proj[last_rows, :] = proj_low[last_rows, :].astype(f32)
    gate_in[...] = mm_nt(normed[gh], wz[...])
    lax.fori_loop(rounds, 2 * rounds - 1, forward, 0)
    for m in range(1, ZS):
        cot_z[m - 1].wait_recv()
        rows = span(net.flip(m) * 2 + i, HALF)
        cot_core.append(net.copy(cot.at[rows], cot.at[rows], net.sibling()))
    lax.fori_loop(2 * rounds - 1, 2 * rounds, forward, 0)
    for c in wout_y:
        c.wait_recv()
    for p in range(TP * reps):
        zp, yp, ip = p // (2 * reps), (p // 2) % reps, p % 2
        wout[p * piece : (p + 1) * piece, :] = wout_all[yp, zp * 2 + ip]
    for c in cot_core:
        c.wait_recv()
    y_copy.wait_recv()

    summed = y[last_rows, :] + y_in[...].astype(f32)
    raw[...] = jnp.swapaxes(summed.reshape(HALF, 8, ch), 0, 1).reshape(half, ch)

    def gate_rows(q, carry):
        rows = span(q, PACK)
        gate = gate_in[rows, :]
        sig = sigmoid(gate)
        act = gate * sig
        summed = raw[rows, :]
        grad_gated = mm(cot[rows, :], wout[...])
        gate_both[gh, rows, :] = (grad_gated * summed * sig * (1.0 + gate * (1.0 - sig))).astype(bf16)
        gate_in[rows, :] = grad_gated * act
        low = (summed * act).astype(bf16)
        gated[rows, :] = low
        return carry

    lax.fori_loop(0, ZS, gate_rows, 0)
    back = jnp.swapaxes(gate_in[...].reshape(8, HALF, ch), 0, 1).reshape(half, ch)
    g[last_rows, :] = back
    g_send[...] = back.astype(bf16)
    g_copy = net.copy(g_send, g_in, net.over_x())
    gate_copy = net.copy(gate_both.at[gh], gate_both.at[gh], net.over_x())

    for c in core_last:
        c.wait_send()

    def mixed_rows(q, carry):
        tok[gh, q] = mm_nt(gated[span(q, PACK), :], wout[...]).astype(bf16).reshape(2, HALF, width)
        return carry

    lax.fori_loop(0, ZS, mixed_rows, 0)
    mixed_copy = net.copy(tok.at[gh, :, 1 - i], mixed_core, net.sibling())
    quarter = width // ZS
    for q in range(ZS):
        value = mm_tn(cot[:, q * quarter : (q + 1) * quarter], gated[...]).astype(bf16)
        for r in range(reps):
            out_send[r, q * 2 * piece : (q + 1) * 2 * piece, :] = value[r * 2 * piece : (r + 1) * 2 * piece, :]
    out_copies = [
        net.copy(out_send.at[net.y_at(d)], out_y.at[d - 1], net.along_y(d)) for d in range(1, reps)
    ]

    state[...] = jnp.zeros_like(state)
    acc_ref[...] = jnp.zeros_like(acc_ref)
    bias_acc[...] = jnp.zeros_like(bias_acc)
    skip_acc[...] = jnp.zeros_like(skip_acc)

    def backward(c, carry):
        block = (1 - s) * (2 * rounds - 1 - c) + s * c
        rows, pre, values = prepare(block)
        s1[...] = jnp.zeros_like(s1)
        s2[...] = jnp.zeros_like(s2)
        for n0 in range(0, STATE, NSTEP):
            rate = rates(n0)

            def body(k, both):
                lams, accs = both
                r = s * k + (1 - s) * (CHUNK - 1 - k)
                t = block * CHUNK + r
                here = rows8(r)
                pv = proj[rows8(t), :]
                gv = g[rows8(t), :]
                uv = u[here, :]
                stv = step[here, :]
                st = decay_step[here, :]
                one = s1[here, :]
                two = s2[here, :]
                new_lams, new_accs = [], []
                for m in range(NSTEP):
                    n = n0 + m
                    if m % 2 == 0:
                        pair = hprev[t, n // 2].astype(f32)
                    a = jnp.exp2(st * rate[m])
                    ah = a * pair[8 * (m % 2) : 8 * (m % 2) + 8]
                    lam = gv * pv[:, DT_RANK + STATE + n : DT_RANK + STATE + n + 1] + lams[m]
                    w = lam * ah
                    new_lams.append(a * lam)
                    two = two + rate[m] * w
                    new_accs.append(accs[m] + stv * w)
                    one = one + lam * pv[:, DT_RANK + n : DT_RANK + n + 1]
                    pb[here, 128 * n : 128 * n + 128] = tiles(lam * uv)
                    pc[here, 128 * n : 128 * n + 128] = tiles(gv * ah)
                s1[here, :] = one
                s2[here, :] = two
                return tuple(new_lams), tuple(new_accs)

            first = (
                tuple(state[n] for n in range(n0, n0 + NSTEP)),
                tuple(acc_ref[n] for n in range(n0, n0 + NSTEP)),
            )
            lams, accs = lax.fori_loop(0, CHUNK, body, first, unroll=CHUNK)
            for m in range(NSTEP):
                state[n0 + m] = lams[m]
                acc_ref[n0 + m] = accs[m]
        gv = g[rows, :]
        one = s1[...]
        q = (LN2 * s2[...] + values * one) * sigmoid(pre)
        q_low = q.astype(bf16)
        bias_acc[...] += jnp.sum(q.reshape(CHUNK, 8, ch), axis=0)
        skip_acc[...] += jnp.sum((gv * values).reshape(CHUNK, 8, ch), axis=0)
        rows_grad[0:DT_RANK, :] += mm_tn(proj_low[rows, :], q_low)[0:DT_RANK, :]
        gu = jnp.sum(gv * u[...], axis=1, keepdims=True)
        lane = lax.broadcasted_iota(jnp.int32, (size, 128), 1)
        read_part = mm(pc[...].astype(bf16), ones[...]) + gu * jnp.where(
            lane < DT_RANK + STATE, proj[rows, :], 0.0
        )
        read_part = jnp.where(lane >= DT_RANK + STATE, pltpu.roll(read_part, STATE, 1), 0.0)
        part_back[rows, :] = mm_nt(q_low, wstep) + mm(pb[...].astype(bf16), ones[...]) + read_part
        g[rows, :] = gv * skip + step[...] * one
        return carry

    lax.fori_loop(0, 1, backward, 0)
    mixed_copy.wait_recv()
    for q in range(ZS):
        mixed_low[q] = (tok[gh, q, i].astype(f32) + mixed_core[q].astype(f32)).astype(bf16)
    mixed_zs = [net.copy(mixed_low.at[net.flip(m)], mixed_z.at[m - 1], net.along_z(m)) for m in range(1, ZS)]
    lax.fori_loop(1, 2, backward, 0)
    for c in out_copies:
        c.wait_recv()
    total = out_send[yi].astype(f32)
    for d in range(1, reps):
        total = total + out_y[d - 1].astype(f32)
    total = total.astype(bf16)
    for q in range(TP):
        out_low[q] = total[q * piece : (q + 1) * piece]
    if share:
        other_part = pl.ds(pl.multiple_of(gh * hp, hp), hp)
        out_x = net.copy(out_low.at[:, other_part], out_x_in, net.over_x())
    lax.fori_loop(2, rounds, backward, 0)
    back_last = Reduce(net, part_back, gh * half, half, *reduces[2], grad_proj)
    g_copy.wait_recv()
    g[first_rows, :] = g_in[...].astype(f32)
    lax.fori_loop(rounds, rounds + 1, backward, 0)
    back_last.across_z()
    lax.fori_loop(rounds + 1, rounds + 2, backward, 0)
    back_last.give()
    lax.fori_loop(rounds + 2, 2 * rounds, backward, 0)
    back_first = Reduce(net, part_back, s * half, half, *reduces[3], grad_proj)
    back_last.end()

    w = conv_pre
    sums[...] = jnp.zeros_like(sums)

    def pull(h):
        def one(b, carry):
            at = h * half + b * PACK
            rows = pl.ds(pl.multiple_of(PAD + at, 8), PACK)
            at = pl.ds(pl.multiple_of(at, PACK), PACK)
            c = conv_pre[rows, :]
            sig = sigmoid(c)
            w[rows, :] = (g[at, :] + mm_nt(grad_proj[at, :], wstate[...])) * (sig * (1.0 + c * (1.0 - sig)))
            return carry

        lax.fori_loop(0, half // PACK, one, 0)

    def convolve_back(h):
        def one(k, carry):
            t = h * HALF + k
            seg = segment_of(t, ends)
            here = w[rows8(t + 3), :]
            total = taps[3:4, :] * here
            new = [carry[3] + here * conv_in[rows8(t + 3), :], carry[4] + here]
            first = []
            for n in range(1, TAPS):
                back = t - n * sgn
                ahead = t + n * sgn
                same_back = wide((segment_of(back, ends) == seg).astype(f32), ch)
                same_ahead = wide((segment_of(ahead, ends) == seg).astype(f32), ch)
                first.insert(0, carry[3 - n] + here * (conv_in[rows8(back + 3), :] * same_back))
                total = total + taps[3 - n : 4 - n, :] * (w[rows8(ahead + 3), :] * same_ahead)
            raw[rows8(k), :] = total
            return tuple(first + new)

        carry = lax.fori_loop(0, HALF, one, tuple(sums[n] for n in range(TAPS + 1)), unroll=4)
        for n in range(TAPS + 1):
            sums[n] = carry[n]
        gx[h] = jnp.swapaxes(raw[...].reshape(HALF, 8, ch), 0, 1).reshape(half, ch).astype(bf16)
        return net.copy(gx.at[h], gx_in.at[h], net.over_x())

    pull(gh)
    back_first.across_z()
    gx_last = convolve_back(gh)
    for c in mixed_zs:
        c.wait_recv()
    total = tok[gh, z, i].astype(f32) + mixed_core[z].astype(f32)
    for m in range(1, ZS):
        total = total + mixed_z[m - 1].astype(f32)
    mixed_sum[...] = (total + tok_last[...].astype(f32)).astype(bf16)
    net.copy(mixed_sum, mixed, net.over_x())
    back_first.give()
    gate_copy.wait_recv()
    part_z = mm_tn(gate_both[0], normed[0, :, half_cols]) + mm_tn(gate_both[1], normed[1, :, half_cols])
    for r in range(reps):
        wz_low[r] = part_z[r * cols : (r + 1) * cols].astype(bf16)
    for d in range(1, reps):
        net.copy(wz_low.at[net.y_at(d)], wz_theirs.at[d - 1], net.along_y(d))
    net.save(wz_low.at[yi], wz_mine)
    back_first.end()
    out_half = out_low
    if share:
        out_x.wait_recv()
        out_half = out_x_in
        out_half[...] = (out_low[:, own_part].astype(f32) + out_x_in[...].astype(f32)).astype(bf16)
    out_all[j] = out_half[j]
    out_zs = []
    for m in range(1, TP):
        zm, im = net.shared(m)
        out_zs.append(net.copy(out_half.at[zm * 2 + im], out_all.at[j], net.to_shared(m)))
    pull(s)
    gx_first = convolve_back(s)

    def rows_of(q, carry):
        rows = span(q, PACK)
        value = (
            mm(gx[s, rows, :], wx[...]) + mm(gx_in[s, rows, :], wx[...]) + mm(gate_both[s, rows, :], wz[...])
        )
        tok[gh, q] = value.astype(bf16).reshape(2, HALF, width)
        return carry

    mixed_copy.wait_send()
    gx_last.wait_recv()
    lax.fori_loop(0, ZS, rows_of, 0)
    to_core = net.copy(tok.at[gh, :, 1 - i], mixed_core, net.sibling())
    for c in mixed_zs:
        c.wait_send()
    gain_acc[0] = jnp.zeros(gain_acc.shape[1:], f32)
    to_core.wait_recv()
    for q in range(ZS):
        mixed_low[q] = (tok[gh, q, i].astype(f32) + mixed_core[q].astype(f32)).astype(bf16)
    to_z = [net.copy(mixed_low.at[net.flip(m)], mixed_z.at[m - 1], net.along_z(m)) for m in range(1, ZS)]

    def gain_terms(q, carry):
        x = tok[s, q].astype(f32).reshape(PACK, width)
        inv = lax.rsqrt(jnp.mean(x * x, axis=1, keepdims=True) + EPS)
        terms = tok[gh, q].astype(f32).reshape(PACK, width) * (x * inv)
        gain_acc[0] += jnp.sum(terms.reshape(PACK // 8, 8, width), axis=0)
        return carry

    lax.fori_loop(0, ZS, gain_terms, 0)
    stages = [
        [net.sibling()],
        [net.over_x()],
        [net.along_y(d) for d in range(1, reps)],
        [net.along_z(1)],
        [net.along_z(2)],
    ]
    slot = [0]

    def gain_start(k):
        cs = []
        for peer in stages[k]:
            cs.append((slot[0], net.copy(gain_acc.at[k], gain_in.at[slot[0]], peer)))
            slot[0] += 1
        return cs

    def gain_end(k, cs):
        total = gain_acc[k]
        for at, c in cs:
            c.wait_recv()
            total = total + gain_in[at]
        gain_acc[k + 1] = total

    cs = gain_start(0)
    gx_first.wait_recv()
    part_x = mm_tn(gx[0], normed[0, :, half_cols]) + mm_tn(gx[1], normed[1, :, half_cols])
    part_x = part_x + mm_tn(gx_in[0], normed[0, :, half_cols]) + mm_tn(gx_in[1], normed[1, :, half_cols])
    for r in range(reps):
        wx_low[r] = part_x[r * cols : (r + 1) * cols].astype(bf16)
    for d in range(1, reps):
        net.copy(wx_low.at[net.y_at(d)], wx_theirs.at[d - 1], net.along_y(d))
    net.save(wx_low.at[yi], wx_mine)
    gain_end(0, cs)
    cs = gain_start(1)
    state_all = mm_tn(conv_out[...].astype(bf16), grad_proj[...])
    rows_grad[STEP_ROW : STEP_ROW + 1, :] = jnp.sum(bias_acc[...], axis=0, keepdims=True)
    rows_grad[SKIP_ROW : SKIP_ROW + 1, :] = jnp.sum(skip_acc[...], axis=0, keepdims=True)
    for n in range(STATE):
        rows_grad[DECAY_ROW + n : DECAY_ROW + n + 1, :] = (
            jnp.sum(acc_ref[n], axis=0, keepdims=True) * rate_ref[n : n + 1, :] * LN2
        )
    for n in range(TAPS + 1):
        rows_grad[TAP_ROW + n : TAP_ROW + n + 1, :] = jnp.sum(sums[n], axis=0, keepdims=True)
    for r in range(reps):
        state_part[r] = state_all[r * cols : (r + 1) * cols, :]
        rows_part[r] = rows_grad[:, r * cols : (r + 1) * cols]
    for d in range(1, reps):
        net.copy(state_part.at[net.y_at(d)], state_theirs.at[d - 1], net.along_y(d))
        net.copy(rows_part.at[net.y_at(d)], rows_theirs.at[d - 1], net.along_y(d))
    net.save(state_part.at[yi], state_mine)
    net.save(rows_part.at[yi], rows_mine)
    gain_end(1, cs)
    cs = gain_start(2)
    gain_end(2, cs)
    cs = gain_start(3)
    for c in out_zs:
        c.wait_recv()
    net.copy(out_all.at[pl.ds(gh * ZS, ZS)], out_theirs, net.over_x())
    net.save(out_all.at[pl.ds(s * ZS, ZS)], out_mine)
    x = tok[s, z, i].astype(f32)
    inv = lax.rsqrt(jnp.mean(x * x, axis=1, keepdims=True) + EPS)
    unit = x * inv
    gain_end(3, cs)
    cs = gain_start(4)
    grad = tok[gh, z, i].astype(f32) + mixed_core[z].astype(f32)
    for m in range(1, ZS):
        to_z[m - 1].wait_recv()
        grad = grad + mixed_z[m - 1].astype(f32)
    scaled = grad * gain[...]
    mean = jnp.mean(scaled * unit, axis=1, keepdims=True)
    grad_tokens[...] = inv * (scaled - unit * mean) + cot_own[...].astype(f32)
    gain_end(4, cs)
    grad_gain[...] = jnp.sum(gain_acc[5], axis=0, keepdims=True)
    net.finish()


def block(reps, grids, gain, wstep, taps, bias, step, skip, decay, wstate, wout, cot, tokens, wx, wz):
    cols, width = wx.shape
    ch = reps * cols
    rows = TP * PACK
    half = rows // 2
    piece = wout.shape[0]
    hp = piece // 2 if piece % 32 == 0 else piece
    size = CHUNK * 8
    sds = jax.ShapeDtypeStruct
    V, H = pltpu.VMEM, pl.ANY
    args = [(grids, pltpu.SMEM)]
    args += [(a, V) for a in (gain, wstep, taps, bias, step, skip, decay, wstate, wout, cot)]
    args += [(a, H) for a in (tokens, wx, wz)]
    outs = (
        (sds((HALF, width), bf16), H),
        (sds((HALF, width), f32), V),
        (sds((cols, width // 2), bf16), H),
        (sds((reps - 1, cols, width // 2), bf16), H),
        (sds((cols, width // 2), bf16), H),
        (sds((reps - 1, cols, width // 2), bf16), H),
        (sds((ZS, hp, ch), bf16), H),
        (sds((ZS, hp, ch), bf16), H),
        (sds((SMALL_ROWS, cols), f32), H),
        (sds((reps - 1, SMALL_ROWS, cols), f32), H),
        (sds((cols, 128), f32), H),
        (sds((reps - 1, cols, 128), f32), H),
        (sds((1, width), f32), V),
    )
    big = V((rows, ch), f32)
    padded = V((rows + 2 * PAD, ch), f32)
    part = V((rows, 128), f32)
    low = V((half, ch), bf16)
    round_rows = V((size, ch), f32)
    state = V((STATE, 8, ch), f32)
    scratch = (
        V((reps, TP, 16, 128), bf16),
        V((1, width), f32),
        V((2, 8, 128), f32),
        V((reps, cols, width), bf16),
        V((ch, width), bf16),
        V((reps, cols, width), bf16),
        V((ch, width), bf16),
        V((reps, SMALL_ROWS, cols), bf16),
        V((SMALL_ROWS, ch), bf16),
        V((reps, cols, 128), bf16),
        V((ch, 128), bf16),
        V((TP, piece, ch), bf16),
        V((TP, piece, ch), bf16),
        V((reps, TP, piece, ch), bf16),
        V((width, ch), bf16),
        V((2, ZS, 2, HALF, width), bf16),
        V((2, half, width), bf16),
        V((half, ch), f32),
        padded,
        padded,
        big,
        V((half, ch), f32),
        part,
        V((rows, 128), bf16),
        part,
        V((PACK, STATE // 2, 16, ch), bf16),
        round_rows,
        round_rows,
        round_rows,
        state,
        state,
        V((STATE, ch), f32),
        round_rows,
        round_rows,
        V((size, STATE * 128), f32),
        V((size, STATE * 128), f32),
        V((STATE * 128, 128), bf16),
        V((8, ch), f32),
        V((8, ch), f32),
        big,
        low,
        low,
        low,
        low,
        low,
        V((2, half, ch), bf16),
        V((half, width), bf16),
        V((ZS, HALF, width), bf16),
        V((ZS, HALF, width), bf16),
        V((ZS - 1, HALF, width), bf16),
        V((HALF, width), bf16),
        V((HALF, width), bf16),
        V((reps, TP * piece, ch), bf16),
        V((reps - 1, TP * piece, ch), bf16),
        V((TP, piece, ch), bf16),
        V((TP, hp, ch), bf16),
        V((TP, hp, ch), bf16),
        V((reps, cols, width // 2), bf16),
        part,
        V((rows, 128), bf16),
        V((TAPS + 1, 8, ch), f32),
        V((2, half, ch), bf16),
        V((2, half, ch), bf16),
        V((reps, cols, width // 2), bf16),
        V((SMALL_ROWS, ch), f32),
        V((reps, SMALL_ROWS, cols), f32),
        V((reps, cols, 128), f32),
        V((6, 8, width), f32),
        V((3 + reps, 8, width), f32),
    ) + REDUCE_SCRATCH * 4
    copies = 120 + 10 * (reps - 1)
    return fused(partial(block_kernel, reps), 1, copies, 12, outs, args, scratch)


def place_kernel(
    reps, index, mixed_in, tokens_in, wx_mine, wx_theirs, wz_mine, wz_theirs, out_mine, out_theirs,
    rows_mine, rows_theirs, state_mine, state_theirs, gain_in,
    mixed, grad_tokens, gain, wx, wz, wout, taps, bias, wstate, wstep, step, decay, skip,
):
    mixed[...] = mixed_in[...]
    grad_tokens[...] = tokens_in[...]
    width, n = gain_in.shape[1], gain.shape[1]
    moved = pltpu.roll(jnp.broadcast_to(gain_in[...], (8, width)), width - index[0] * n, 1)
    gain[...] = moved[0:1, 0:n]

    def total(mine, theirs):
        value = mine[...].astype(f32)
        for d in range(reps - 1):
            value = value + theirs[d].astype(f32)
        return value

    wx[...] = total(wx_mine, wx_theirs)
    wz[...] = total(wz_mine, wz_theirs)
    cols = wx.shape[0]
    hp = out_mine.shape[1]
    share = hp < wout.shape[0]
    s = index[1]
    for q in range(ZS):
        parts = [(out_mine[q].astype(f32), s), (out_theirs[q].astype(f32), 1 - s)]
        if not share:
            parts = [(parts[0][0] + parts[1][0], 0)]
        for value, place in parts:
            for r in range(reps):
                at = ((q // 2) * reps + r) * 2 + q % 2
                rows = pl.ds(pl.multiple_of(place * hp, hp), hp) if share else pl.ds(0, hp)
                wout[rows, at * cols : (at + 1) * cols] = value[:, r * cols : (r + 1) * cols]
    rows = total(rows_mine, rows_theirs)
    wstep[...] = rows[0:DT_RANK]
    taps[...] = rows[TAP_ROW : TAP_ROW + TAPS]
    bias[...] = rows[BIAS_ROW : BIAS_ROW + 1]
    step[...] = rows[STEP_ROW : STEP_ROW + 1]
    skip[...] = rows[SKIP_ROW : SKIP_ROW + 1]
    decay[...] = rows[DECAY_ROW : DECAY_ROW + STATE]
    wstate[...] = total(state_mine, state_theirs)


def place(reps, index, results):
    mixed, grad_tokens, wx = results[0], results[1], results[2]
    ch = results[6].shape[2]
    cols = wx.shape[0]
    width = mixed.shape[1]
    piece = width // (TP * reps)
    sds = jax.ShapeDtypeStruct
    V = pl.BlockSpec(memory_space=pltpu.VMEM)
    outs = (
        sds(mixed.shape, bf16),
        sds(grad_tokens.shape, f32),
        sds((1, width // (2 * TP * reps)), f32),
        sds(wx.shape, f32),
        sds(wx.shape, f32),
        sds((piece, ZS * ch), f32),
        sds((TAPS, cols), f32),
        sds((1, cols), f32),
        sds((cols, 128), f32),
        sds((DT_RANK, cols), f32),
        sds((1, cols), f32),
        sds((STATE, cols), f32),
        sds((1, cols), f32),
    )
    return pl.pallas_call(
        partial(place_kernel, reps),
        out_shape=outs,
        in_specs=[pl.BlockSpec(memory_space=pltpu.SMEM)] + [V] * len(results),
        out_specs=tuple([V] * len(outs)),
        compiler_params=pltpu.CompilerParams(vmem_limit_bytes=63 << 20),
    )(index, *results)


def local(
    reps, tokens, item_grids, norm_gain, proj_in_x, proj_in_z, proj_out, conv_weight, conv_bias,
    proj_state, proj_step, step_bias, decay_log, skip_gain, grad_out,
):
    width = tokens.shape[1]
    results = block(
        reps, item_grids, norm_gain[None], proj_step[0], conv_weight[0], conv_bias, step_bias, skip_gain,
        decay_log[0], proj_state[0], proj_out.T, grad_out.reshape(HALF, width), tokens, proj_in_x.T,
        proj_in_z.T,
    )
    s = lax.axis_index("dir")
    index = jnp.stack([s * lax.axis_size("dp") + lax.axis_index("dp"), s]).astype(jnp.int32)
    (
        mixed, grad_tokens, grad_gain, grad_wx, grad_wz, grad_wout, grad_taps, grad_bias, grad_wstate,
        grad_wstep, grad_step, grad_decay, grad_skip,
    ) = place(reps, index, results)
    return (
        mixed.reshape(1, 1, HALF, width),
        grad_tokens.reshape(1, 1, HALF, width),
        grad_gain[0],
        grad_wx.T,
        grad_wz.T,
        grad_wout.T,
        grad_taps[None],
        grad_bias,
        grad_wstate[None],
        grad_wstep[None],
        grad_step,
        grad_decay[None],
        grad_skip,
    )


def solution(mesh):
    reps = mesh.shape["dp"] // TP
    return jax.shard_map(
        partial(local, reps),
        mesh=mesh,
        in_specs=(
            P("dp", None),
            P("dp", None),
            P("dp"),
            P(None, "dp"),
            P(None, "dp"),
            P(None, "dp"),
            P("dir", None, "dp"),
            P("dir", "dp"),
            P("dir", "dp", None),
            P("dir", None, "dp"),
            P("dir", "dp"),
            P("dir", None, "dp"),
            P("dir", "dp"),
            P("dp", "dir", None, None),
        ),
        out_specs=(
            P("dp", "dir", None, None),
            P("dp", "dir", None, None),
            P(("dir", "dp")),
            P("dir", "dp"),
            P("dir", "dp"),
            P("dir", "dp"),
            P("dir", None, "dp"),
            P("dir", "dp"),
            P("dir", "dp", None),
            P("dir", None, "dp"),
            P("dir", "dp"),
            P("dir", None, "dp"),
            P("dir", "dp"),
        ),
        check_vma=False,
    )
```

```python
from functools import partial

import jax
import jax.numpy as jnp
from jax import lax
from jax.experimental import pallas as pl
from jax.experimental.pallas import tpu as pltpu
from jax.sharding import PartitionSpec as P

f32 = jnp.float32
bf16 = jnp.bfloat16
EPS = 1e-05
DT_RANK = 96
STATE = 16
TAPS = 4
ZS = 4
TP = 8
PACK = 128
HALF = 64
CHUNK = 16
NSTEP = 4
LOG2E = 1.4426950408889634
LN2 = 0.6931471805599453
BIG = 1e9
PAD = 24
TAP_ROW, BIAS_ROW, STEP_ROW, SKIP_ROW, DECAY_ROW, SMALL_ROWS = 96, 100, 101, 102, 103, 128


def mm(left, right):
    return jnp.dot(left, right, preferred_element_type=f32)


def mm_nt(left, right):
    return lax.dot_general(left, right, (((1,), (1,)), ((), ())), preferred_element_type=f32)


def mm_tn(left, right):
    return lax.dot_general(left, right, (((0,), (0,)), ((), ())), preferred_element_type=f32)


def segment_of(t, ends):
    t = t.astype(f32) if hasattr(t, "astype") else float(t)
    return (t >= ends[0]).astype(f32) + (t >= ends[1]).astype(f32)


def rows8(t):
    return pl.ds(pl.multiple_of(t * 8, 8), 8)


def span(start, size):
    return pl.ds(pl.multiple_of(start * size, size), size)


def sigmoid(v):
    return 1.0 / (1.0 + jnp.exp(-v))


def softplus(v):
    return jnp.maximum(v, 0.0) + jnp.log1p(jnp.exp(-jnp.abs(v)))


def wide(mask, ch):
    return jnp.concatenate([mask] * (ch // 128), axis=1)


def tiles(v):
    total = v[:, 0:128]
    for at in range(128, v.shape[1], 128):
        total = total + v[:, at : at + 128]
    return total


class Copy:
    def __init__(self, copy):
        self.copy, self.sent, self.got = copy, False, False
        copy.start()

    def wait_send(self):
        if not self.sent:
            self.copy.wait_send()
            self.sent = True

    def wait_recv(self):
        if not self.got:
            self.copy.wait_recv()
            self.got = True


class Net:
    def __init__(self, reps, send, recv, local):
        self.reps, self.send, self.recv, self.local = reps, send, recv, local
        self.s = lax.axis_index("dir")
        p = lax.axis_index("dp")
        self.i = lax.rem(p, 2)
        self.y = lax.rem(p // 2, reps)
        self.z = p // (2 * reps)
        self.used = 0
        self.moved = 0
        self.copies = []
        self.saves = []

    def place(self, s, z, y, i):
        return (s, (z * self.reps + y) * 2 + i)

    def flip(self, m):
        if m == 1:
            return self.z + 1 - 2 * lax.rem(self.z, 2)
        if m == 2:
            return lax.rem(self.z + 2, ZS)
        return ZS - 1 - self.z

    def over_x(self):
        return self.place(1 - self.s, self.z, self.y, self.i)

    def sibling(self):
        return self.place(self.s, self.z, self.y, 1 - self.i)

    def along_z(self, m):
        return self.place(self.s, self.flip(m), self.y, self.i)

    def shared(self, m):
        z = self.flip(m // 2) if m // 2 else self.z
        i = 1 - self.i if m % 2 else self.i
        return z, i

    def to_shared(self, m):
        z, i = self.shared(m)
        return self.place(self.s, z, self.y, i)

    def y_at(self, d):
        return lax.rem(self.y + d, self.reps)

    def along_y(self, d):
        return self.place(self.s, self.z, self.y_at(d), self.i)

    def greet(self):
        self.peers = [self.over_x()] + [self.to_shared(m) for m in range(1, TP)]
        self.peers += [self.along_y(d) for d in range(1, self.reps)]
        barrier = pltpu.get_barrier_semaphore()
        for peer in self.peers:
            pl.semaphore_signal(barrier, inc=1, device_id=peer, device_id_type=pl.DeviceIdType.MESH)

    def met(self):
        pl.semaphore_wait(pltpu.get_barrier_semaphore(), len(self.peers))

    def copy(self, source, target, peer):
        k = self.used
        self.used += 1
        c = Copy(
            pltpu.make_async_remote_copy(
                src_ref=source,
                dst_ref=target,
                send_sem=self.send.at[k],
                recv_sem=self.recv.at[k],
                device_id=peer,
                device_id_type=pl.DeviceIdType.MESH,
            )
        )
        self.copies.append(c)
        return c

    def gather_z(self, source, at):
        c = ZGather(self, source, at)
        self.copies.append(c)
        return c

    def load(self, source, target):
        c = pltpu.make_async_copy(source, target, self.local.at[self.moved])
        self.moved += 1
        c.start()
        return c

    def save(self, source, target):
        self.saves.append(self.load(source, target))

    def finish(self):
        for c in self.copies:
            c.wait_recv()
            c.wait_send()
        for c in self.saves:
            c.wait()


class ZGather:
    def __init__(self, net, source, at):
        self.net, self.at = net, at
        self.near = [net.copy(source, at(net.z), net.along_z(m)) for m in (1, 2)]
        self.inner = lax.rem(net.z + 1, ZS) >= 2
        k = net.used
        net.used += 2
        self.direct = self.make(source, at(net.z), k, k, 3)
        far = at(net.flip(2))
        self.onward = self.make(far, far, k + 1, k, 1)
        self.got = False

        @pl.when(self.inner)
        def _():
            self.direct.start()

    def make(self, source, target, out, arrival, m):
        return pltpu.make_async_remote_copy(
            src_ref=source,
            dst_ref=target,
            send_sem=self.net.send.at[out],
            recv_sem=self.net.recv.at[arrival],
            device_id=self.net.along_z(m),
            device_id_type=pl.DeviceIdType.MESH,
        )

    def wait(self, m):
        if m < 3:
            self.near[m - 1].wait_recv()
            if m == 2:

                @pl.when(self.inner)
                def _():
                    self.onward.start()

        elif not self.got:
            self.direct.wait_recv()
            self.got = True
        return self.at(self.net.flip(m))

    def wait_recv(self):
        pass

    def wait_send(self):
        @pl.when(self.inner)
        def _():
            self.direct.wait_send()
            self.onward.wait_send()


class Reduce:
    def __init__(self, net, part, base, size, fold, out_low, in_low, total):
        self.net, self.part, self.base = net, part, base
        self.fold, self.out_low, self.in_low, self.total = fold, out_low, in_low, total
        self.rows = size // 2
        self.block = self.rows // ZS
        self.first = net.copy(part.at[self.at(1 - net.i, self.rows)], fold, net.sibling())

    def at(self, n, size):
        return pl.ds(pl.multiple_of(self.base + n * size, size), size)

    def across_z(self):
        net, fold = self.net, self.fold
        self.first.wait_recv()
        fold[...] = self.part[self.at(net.i, self.rows), :] + fold[...]
        self.out_low[...] = fold[...].astype(bf16).reshape(ZS, self.block, 128)
        self.cs = [
            net.copy(self.out_low.at[net.flip(m)], self.in_low.at[m - 1], net.along_z(m))
            for m in range(1, ZS)
        ]

    def give(self):
        net, total = self.net, self.total
        mine = self.at(net.i * ZS + net.z, self.block)
        value = self.fold[span(net.z, self.block), :]
        for m in range(1, ZS):
            self.cs[m - 1].wait_recv()
            value = value + self.in_low[m - 1].astype(f32)
        total[mine, :] = value.astype(bf16)
        self.cs = [net.copy(total.at[mine], total.at[mine], net.along_z(m)) for m in range(1, ZS)]
        self.ds = [net.copy(total.at[mine], total.at[mine], net.sibling())]

    def end(self):
        net, total = self.net, self.total
        for m in range(1, ZS):
            self.cs[m - 1].wait_recv()
            there = self.at(net.i * ZS + net.flip(m), self.block)
            self.ds.append(net.copy(total.at[there], total.at[there], net.sibling()))
        for d in self.ds:
            d.wait_recv()


REDUCE_ROWS = TP * HALF
REDUCE_SCRATCH = (
    pltpu.VMEM((REDUCE_ROWS // 2, 128), f32),
    pltpu.VMEM((ZS, REDUCE_ROWS // 2 // ZS, 128), bf16),
    pltpu.VMEM((ZS - 1, REDUCE_ROWS // 2 // ZS, 128), bf16),
)


def fused(kernel, name_id, copies, moves, outs, args, scratch):
    return pl.pallas_call(
        kernel,
        out_shape=tuple(o for o, _ in outs),
        in_specs=[pl.BlockSpec(memory_space=m) for _, m in args],
        out_specs=tuple(pl.BlockSpec(memory_space=m) for _, m in outs),
        scratch_shapes=list(scratch)
        + [pltpu.SemaphoreType.DMA((n,)) for n in (copies, copies, moves)],
        compiler_params=pltpu.CompilerParams(
            collective_id=name_id, has_side_effects=True, vmem_limit_bytes=63 << 20
        ),
    )(*(a for a, _ in args))


def block_kernel(reps, *refs):
    refs = list(refs)

    def take_refs(n):
        out = refs[:n]
        del refs[:n]
        return out

    (
        grids, gain_own, wstep_own, taps_own, bias_own, step_own, skip_own, decay_own, wstate_own, wout_own,
        cot_own, tokens, wx_own, wz_own,
    ) = take_refs(14)
    (
        mixed, grad_tokens, wx_mine, wx_theirs, wz_mine, wz_theirs, out_mine, out_theirs, rows_mine,
        rows_theirs, state_mine, state_theirs, grad_gain,
    ) = take_refs(13)
    (
        meta_all, gain, ends_ref, wx_all, wx, wz_all, wz, small_all, small, wstate_all, wstate,
        wout_send, wout_in, wout_all, wout,
    ) = take_refs(15)
    (tok, normed, raw, conv_in, conv_pre, conv_out, gate_in, part, proj_low, proj) = take_refs(10)
    (
        hprev, step, decay_step, u, state, acc_ref, rate_ref, s1, s2, pb, pc, ones, bias_acc, skip_acc, g,
    ) = take_refs(15)
    (y_send, y_in, g_send, g_in, gated, gate_both, cot, mixed_core, mixed_low, mixed_z, mixed_sum, tok_last) = take_refs(12)
    (out_send, out_y, out_low, out_x_in, out_all, wz_low, part_back, grad_proj, sums, gx, gx_in) = take_refs(11)
    (wx_low, rows_grad, rows_part, state_part, rows_low, state_low, gain_acc, gain_in) = take_refs(8)
    reduces = [take_refs(3) for _ in range(4)]
    send, recv, local_sems = refs
    net = Net(reps, send, recv, local_sems)
    net.greet()
    s, z, yi, i = net.s, net.z, net.y, net.i
    sgn = 1 - 2 * s
    gh = 1 - s
    j = z * 2 + i
    cols, width = wx_own.shape
    ch = reps * cols
    piece = wout_own.shape[0]
    half = TP * HALF
    rounds = HALF // CHUNK
    size = CHUNK * 8
    share = piece % 32 == 0
    hp = piece // 2 if share else piece
    own_part = pl.ds(pl.multiple_of(s * hp, hp), hp) if share else pl.ds(0, piece)
    half_cols = pl.ds(pl.multiple_of(s * (width // 2), 128), width // 2)

    own_loads = [net.load(tokens.at[pl.ds(h * HALF, HALF)], tok.at[h, z, i]) for h in range(2)]
    own_loads += [net.load(wx_own, wx_all.at[yi]), net.load(wz_own, wz_all.at[yi])]
    own_loads += [net.load(tokens.at[pl.ds(pl.multiple_of(gh * HALF, HALF), HALF)], tok_last)]
    first_end = (grids[0, 0] * grids[0, 1]).astype(f32)
    second_end = first_end + (grids[1, 0] * grids[1, 1]).astype(f32)
    row = lax.broadcasted_iota(jnp.int32, (16, 128), 0)
    gain_row = jnp.concatenate([gain_own[...].astype(f32), jnp.zeros((1, 128 - piece), f32)], axis=1)
    meta = jnp.where(row == 0, gain_row, jnp.where(row == 1, first_end, second_end))
    meta_all[yi, j] = meta.astype(bf16)
    small_rows = [ref[...].astype(f32) for ref in (wstep_own, taps_own, bias_own, step_own, skip_own, decay_own)]
    small_rows.append(jnp.zeros((SMALL_ROWS - DECAY_ROW - STATE, cols), f32))
    small_all[yi] = jnp.concatenate(small_rows, axis=0).astype(bf16)
    wstate_all[yi] = wstate_own[...]
    net.met()
    own_first = tokens.at[pl.ds(pl.multiple_of(s * HALF, HALF), HALF)]
    own_last = tokens.at[pl.ds(pl.multiple_of(gh * HALF, HALF), HALF)]
    from_z = net.gather_z(own_first, lambda zz: tok.at[s, zz, i])
    core_first = [net.copy(own_first, tok.at[s, z, i], net.sibling())]
    core_last = [net.copy(own_last, tok.at[gh, z, i], net.sibling())]
    metas = [net.copy(meta_all.at[yi, j], meta_all.at[yi, j], net.to_shared(m)) for m in range(1, TP)]
    first_y = []
    for d in range(1, reps):
        first_y.append(net.copy(wx_own, wx_all.at[yi], net.along_y(d)))
        for ref in (small_all, wstate_all):
            first_y.append(net.copy(ref.at[yi], ref.at[yi], net.along_y(d)))
    cot_mine = span(j, HALF)
    cot_x = net.copy(cot_own, cot.at[cot_mine], net.over_x())
    for c in metas:
        c.wait_recv()
    meta_y = [net.copy(meta_all.at[yi], meta_all.at[yi], net.along_y(d)) for d in range(1, reps)]
    late_y = [net.copy(wz_own, wz_all.at[yi], net.along_y(d)) for d in range(1, reps)]

    for ref in (conv_in, conv_pre):
        ref[0:PAD, :] = jnp.zeros((PAD, ch), f32)
        ref[PAD + 8 * PACK :, :] = jnp.zeros((PAD, ch), f32)
    for b in range(TP):
        both = meta_all[yi, b].astype(f32)
        ends_ref[0, b : b + 1, :] = both[1:2, :]
        ends_ref[1, b : b + 1, :] = both[2:3, :]
    for p in range(TP * reps):
        zp, yp, ip = p // (2 * reps), (p // 2) % reps, p % 2
        wout_send[zp * 2 + ip, :, yp * cols : (yp + 1) * cols] = wout_own[:, p * cols : (p + 1) * cols]
    wout_in[j, own_part] = wout_send[j, own_part]
    source = lax.broadcasted_iota(jnp.int32, (STATE * 128, 128), 0) // 128
    target = lax.broadcasted_iota(jnp.int32, (STATE * 128, 128), 1)
    ones[...] = (target == DT_RANK + source).astype(f32).astype(bf16)
    rows_grad[...] = jnp.zeros_like(rows_grad)
    state[...] = jnp.zeros_like(state)
    for c in own_loads:
        c.wait()

    from_x = []
    for m in range(1, ZS):
        there = from_z.wait(m)
        core_first.append(net.copy(there, there, net.sibling()))
        from_x.append(net.copy(there, there, net.over_x()))
    wout_z = []
    for m in range(1, TP):
        zm, im = net.shared(m)
        wout_z.append(net.copy(wout_send.at[zm * 2 + im, own_part], wout_in.at[j, own_part], net.to_shared(m)))
    cot_x.wait_recv()
    cot_z = net.gather_z(cot.at[cot_mine], lambda zz: cot.at[span(zz * 2 + i, HALF)])
    cot_core = [net.copy(cot.at[cot_mine], cot.at[cot_mine], net.sibling())]
    for c in meta_y + first_y:
        c.wait_recv()
    for p in range(TP * reps):
        zp, yp, ip = p // (2 * reps), (p // 2) % reps, p % 2
        gain[:, p * piece : (p + 1) * piece] = meta_all[yp, zp * 2 + ip].astype(f32)[0:1, 0:piece]
    for r in range(reps):
        wx[r * cols : (r + 1) * cols, :] = wx_all[r]
        small[:, r * cols : (r + 1) * cols] = small_all[r]
        wstate[r * cols : (r + 1) * cols, :] = wstate_all[r]
    for c in core_first:
        c.wait_recv()

    ends = (ends_ref[0], ends_ref[1])
    vectors = small[DT_RANK : DT_RANK + 16, :].astype(f32)
    taps = vectors[0 : TAPS + 1, :]
    step_bias = vectors[STEP_ROW - DT_RANK : STEP_ROW - DT_RANK + 1, :]
    skip = vectors[SKIP_ROW - DT_RANK : SKIP_ROW - DT_RANK + 1, :]

    def take(h):
        def one(q, carry):
            rows = span(q, PACK)
            x = tok[h, q].astype(f32).reshape(PACK, width)
            inv = lax.rsqrt(jnp.mean(x * x, axis=1, keepdims=True) + EPS)
            low = (x * inv * gain[...]).astype(bf16)
            normed[h, rows, :] = low
            raw[rows, :] = mm_nt(low, wx[...])
            return carry

        lax.fori_loop(0, ZS, one, 0)
        x = jnp.swapaxes(raw[...].reshape(8, HALF, ch), 0, 1).reshape(half, ch)
        conv_in[pl.ds(pl.multiple_of(PAD + h * half, 8), half), :] = x

    def convolve(h, sums):
        def one(k, carry):
            t = h * HALF + k
            seg = segment_of(t, ends)
            total = taps[4:5, :] + taps[3:4, :] * conv_in[rows8(t + 3), :]
            for n in range(1, TAPS):
                there = t - n * sgn
                same = wide((segment_of(there, ends) == seg).astype(f32), ch)
                total = total + taps[3 - n : 4 - n, :] * (conv_in[rows8(there + 3), :] * same)
            conv_pre[rows8(t + 3), :] = total
            act = total * sigmoid(total)
            conv_out[rows8(t), :] = act.astype(bf16).astype(f32)
            return carry

        lax.fori_loop(0, HALF, one, 0, unroll=4)
        rows = span(h, half)
        part[rows, :] = mm(conv_out[rows, :].astype(bf16), wstate[...])
        return Reduce(net, part, h * half, half, *sums, proj_low)

    take(s)
    sum_first = convolve(s, reduces[0])

    def last_tokens(m):
        from_x[m - 1].wait_recv()
        there = tok.at[gh, net.flip(m), i]
        core_last.append(net.copy(there, there, net.sibling()))

    last_tokens(1)
    sum_first.across_z()
    last_tokens(2)
    last_tokens(3)
    for c in wout_z:
        c.wait_recv()
    wout_x = [net.copy(wout_in.at[:, own_part], wout_in.at[:, own_part], net.over_x())] if share else []
    sum_first.give()
    for c in core_last:
        c.wait_recv()
    take(gh)
    sum_last = convolve(gh, reduces[1])
    sum_first.end()
    first_rows = span(s, half)
    last_rows = span(gh, half)
    proj[first_rows, :] = proj_low[first_rows, :].astype(f32)

    wstep = jnp.where(lax.broadcasted_iota(jnp.int32, (128, ch), 0) < DT_RANK, small[...], 0.0).astype(bf16)
    rate_ref[...] = -LOG2E * jnp.exp(small[DT_RANK:, :].astype(f32)[DECAY_ROW - DT_RANK : DECAY_ROW - DT_RANK + STATE, :])
    y = g

    def prepare(block):
        rows = span(block, size)
        pre = mm(proj_low[rows, :], wstep) + step_bias
        step_all = softplus(pre)
        values = conv_out[rows, :]
        step[...] = step_all
        u[...] = step_all * values
        for k in range(CHUNK):
            t = block * CHUNK + k
            fresh = segment_of(t, ends) != segment_of(t - sgn, ends)
            decay_step[8 * k : 8 * k + 8, :] = jnp.where(
                wide(fresh, ch), BIG, step_all[8 * k : 8 * k + 8, :]
            )
        return rows, pre, values

    def rates(n0):
        return [jnp.broadcast_to(rate_ref[n : n + 1, :], (8, ch)) for n in range(n0, n0 + NSTEP)]

    def forward(c, carry):
        block = c + s * (2 * rounds - 1 - 2 * c)
        rows, _, values = prepare(block)
        y[rows, :] = skip * values
        for n0 in range(0, STATE, NSTEP):
            rate = rates(n0)

            def body(k, hs):
                r = s * (CHUNK - 1 - k) + (1 - s) * k
                t = block * CHUNK + r
                pv = proj[rows8(t), :]
                st = decay_step[rows8(r), :]
                uv = u[rows8(r), :]
                total = y[rows8(t), :]
                new = []
                for m in range(NSTEP):
                    n = n0 + m
                    if m % 2 == 0:
                        hprev[t, n // 2] = jnp.concatenate([hs[m], hs[m + 1]], axis=0).astype(bf16)
                    h = jnp.exp2(st * rate[m]) * hs[m] + uv * pv[:, DT_RANK + n : DT_RANK + n + 1]
                    total = total + h * pv[:, DT_RANK + STATE + n : DT_RANK + STATE + n + 1]
                    new.append(h)
                y[rows8(t), :] = total
                return tuple(new)

            hs = lax.fori_loop(0, CHUNK, body, tuple(state[n] for n in range(n0, n0 + NSTEP)), unroll=CHUNK)
            for m in range(NSTEP):
                state[n0 + m] = hs[m]
        return carry

    sum_last.across_z()
    for c in wout_x:
        c.wait_recv()
    wout_y = [net.copy(wout_in, wout_all.at[yi], net.along_y(d)) for d in range(1, reps)]
    wout_all[yi] = wout_in[...]
    lax.fori_loop(0, rounds // 2, forward, 0)
    sum_last.give()
    for m in (1, 2):
        there = cot_z.wait(m)
        cot_core.append(net.copy(there, there, net.sibling()))
    lax.fori_loop(rounds // 2, rounds, forward, 0)
    y_send[...] = y[first_rows, :].astype(bf16)
    y_copy = net.copy(y_send, y_in, net.over_x())
    sum_last.end()
    proj[last_rows, :] = proj_low[last_rows, :].astype(f32)
    for c in late_y:
        c.wait_recv()
    for r in range(reps):
        wz[r * cols : (r + 1) * cols, :] = wz_all[r]
    gate_in[...] = mm_nt(normed[gh], wz[...])
    lax.fori_loop(rounds, 2 * rounds - 1, forward, 0)
    there = cot_z.wait(3)
    cot_core.append(net.copy(there, there, net.sibling()))
    lax.fori_loop(2 * rounds - 1, 2 * rounds, forward, 0)
    for c in wout_y:
        c.wait_recv()
    for p in range(TP * reps):
        zp, yp, ip = p // (2 * reps), (p // 2) % reps, p % 2
        wout[p * piece : (p + 1) * piece, :] = wout_all[yp, zp * 2 + ip]
    y_copy.wait_recv()

    summed = y[last_rows, :] + y_in[...].astype(f32)
    raw[...] = jnp.swapaxes(summed.reshape(HALF, 8, ch), 0, 1).reshape(half, ch)

    def gate_rows(q, carry):
        rows = span(q, PACK)
        gate = gate_in[rows, :]
        low = (raw[rows, :] * (gate * sigmoid(gate))).astype(bf16)
        gated[rows, :] = low
        tok[gh, q] = mm_nt(low, wout[...]).astype(bf16).reshape(2, HALF, width)
        return carry

    def grad_rows(q, carry):
        rows = span(q, PACK)
        gate = gate_in[rows, :]
        sig = sigmoid(gate)
        grad_gated = mm(cot[rows, :], wout[...])
        gate_both[gh, rows, :] = (grad_gated * raw[rows, :] * sig * (1.0 + gate * (1.0 - sig))).astype(bf16)
        gate_in[rows, :] = grad_gated * (gate * sig)
        return carry

    for c in core_last:
        c.wait_send()
    lax.fori_loop(0, ZS, gate_rows, 0)
    mixed_copy = net.copy(tok.at[gh, :, 1 - i], mixed_core, net.sibling())
    for c in cot_core:
        c.wait_recv()
    lax.fori_loop(0, ZS, grad_rows, 0)
    back = jnp.swapaxes(gate_in[...].reshape(8, HALF, ch), 0, 1).reshape(half, ch)
    g[last_rows, :] = back
    g_send[...] = back.astype(bf16)
    g_copy = net.copy(g_send, g_in, net.over_x())
    gate_copy = net.copy(gate_both.at[gh], gate_both.at[gh], net.over_x())
    mixed_copy.wait_recv()
    for q in range(ZS):
        mixed_low[q] = (tok[gh, q, i].astype(f32) + mixed_core[q].astype(f32)).astype(bf16)
    mixed_zs = [net.copy(mixed_low.at[net.flip(m)], mixed_z.at[m - 1], net.along_z(m)) for m in range(1, ZS)]

    state[...] = jnp.zeros_like(state)
    acc_ref[...] = jnp.zeros_like(acc_ref)
    bias_acc[...] = jnp.zeros_like(bias_acc)
    skip_acc[...] = jnp.zeros_like(skip_acc)

    def backward(c, carry):
        block = (1 - s) * (2 * rounds - 1 - c) + s * c
        rows, pre, values = prepare(block)
        s1[...] = jnp.zeros_like(s1)
        s2[...] = jnp.zeros_like(s2)
        for n0 in range(0, STATE, NSTEP):
            rate = rates(n0)

            def body(k, both):
                lams, accs = both
                r = s * k + (1 - s) * (CHUNK - 1 - k)
                t = block * CHUNK + r
                here = rows8(r)
                pv = proj[rows8(t), :]
                gv = g[rows8(t), :]
                uv = u[here, :]
                stv = step[here, :]
                st = decay_step[here, :]
                one = s1[here, :]
                two = s2[here, :]
                new_lams, new_accs = [], []
                for m in range(NSTEP):
                    n = n0 + m
                    if m % 2 == 0:
                        pair = hprev[t, n // 2].astype(f32)
                    a = jnp.exp2(st * rate[m])
                    ah = a * pair[8 * (m % 2) : 8 * (m % 2) + 8]
                    lam = gv * pv[:, DT_RANK + STATE + n : DT_RANK + STATE + n + 1] + lams[m]
                    w = lam * ah
                    new_lams.append(a * lam)
                    two = two + rate[m] * w
                    new_accs.append(accs[m] + stv * w)
                    one = one + lam * pv[:, DT_RANK + n : DT_RANK + n + 1]
                    pb[here, 128 * n : 128 * n + 128] = tiles(lam * uv)
                    pc[here, 128 * n : 128 * n + 128] = tiles(gv * ah)
                s1[here, :] = one
                s2[here, :] = two
                return tuple(new_lams), tuple(new_accs)

            first = (
                tuple(state[n] for n in range(n0, n0 + NSTEP)),
                tuple(acc_ref[n] for n in range(n0, n0 + NSTEP)),
            )
            lams, accs = lax.fori_loop(0, CHUNK, body, first, unroll=CHUNK)
            for m in range(NSTEP):
                state[n0 + m] = lams[m]
                acc_ref[n0 + m] = accs[m]
        gv = g[rows, :]
        one = s1[...]
        q = (LN2 * s2[...] + values * one) * sigmoid(pre)
        q_low = q.astype(bf16)
        bias_acc[...] += jnp.sum(q.reshape(CHUNK, 8, ch), axis=0)
        skip_acc[...] += jnp.sum((gv * values).reshape(CHUNK, 8, ch), axis=0)
        rows_grad[0:DT_RANK, :] += mm_tn(proj_low[rows, :], q_low)[0:DT_RANK, :]
        gu = jnp.sum(gv * u[...], axis=1, keepdims=True)
        lane = lax.broadcasted_iota(jnp.int32, (size, 128), 1)
        read_part = mm(pc[...].astype(bf16), ones[...]) + gu * jnp.where(
            lane < DT_RANK + STATE, proj[rows, :], 0.0
        )
        read_part = jnp.where(lane >= DT_RANK + STATE, pltpu.roll(read_part, STATE, 1), 0.0)
        part_back[rows, :] = mm_nt(q_low, wstep) + mm(pb[...].astype(bf16), ones[...]) + read_part
        g[rows, :] = gv * skip + step[...] * one
        return carry

    lax.fori_loop(0, 1, backward, 0)
    quarter = width // ZS
    for q in range(ZS):
        value = mm_tn(cot[:, q * quarter : (q + 1) * quarter], gated[...]).astype(bf16)
        for r in range(reps):
            out_send[r, q * 2 * piece : (q + 1) * 2 * piece, :] = value[r * 2 * piece : (r + 1) * 2 * piece, :]
    out_copies = [
        net.copy(out_send.at[net.y_at(d)], out_y.at[d - 1], net.along_y(d)) for d in range(1, reps)
    ]
    lax.fori_loop(1, rounds, backward, 0)
    back_last = Reduce(net, part_back, gh * half, half, *reduces[2], grad_proj)
    g_copy.wait_recv()
    g[first_rows, :] = g_in[...].astype(f32)
    lax.fori_loop(rounds, rounds + 1, backward, 0)
    for c in out_copies:
        c.wait_recv()
    total = out_send[yi].astype(f32)
    for d in range(1, reps):
        total = total + out_y[d - 1].astype(f32)
    total = total.astype(bf16)
    for q in range(TP):
        out_low[q] = total[q * piece : (q + 1) * piece]
    if share:
        other_part = pl.ds(pl.multiple_of(gh * hp, hp), hp)
        out_x = net.copy(out_low.at[:, other_part], out_x_in, net.over_x())
    back_last.across_z()
    lax.fori_loop(rounds + 1, 2 * rounds - 1, backward, 0)
    back_last.give()
    lax.fori_loop(2 * rounds - 1, 2 * rounds, backward, 0)
    back_first = Reduce(net, part_back, s * half, half, *reduces[3], grad_proj)
    back_last.end()

    w = conv_pre
    sums[...] = jnp.zeros_like(sums)

    def pull(h):
        def one(b, carry):
            at = h * half + b * PACK
            rows = pl.ds(pl.multiple_of(PAD + at, 8), PACK)
            at = pl.ds(pl.multiple_of(at, PACK), PACK)
            c = conv_pre[rows, :]
            sig = sigmoid(c)
            w[rows, :] = (g[at, :] + mm_nt(grad_proj[at, :], wstate[...])) * (sig * (1.0 + c * (1.0 - sig)))
            return carry

        lax.fori_loop(0, half // PACK, one, 0)

    def convolve_back(h):
        def one(k, carry):
            t = h * HALF + k
            seg = segment_of(t, ends)
            here = w[rows8(t + 3), :]
            total = taps[3:4, :] * here
            new = [carry[3] + here * conv_in[rows8(t + 3), :], carry[4] + here]
            first = []
            for n in range(1, TAPS):
                back = t - n * sgn
                ahead = t + n * sgn
                same_back = wide((segment_of(back, ends) == seg).astype(f32), ch)
                same_ahead = wide((segment_of(ahead, ends) == seg).astype(f32), ch)
                first.insert(0, carry[3 - n] + here * (conv_in[rows8(back + 3), :] * same_back))
                total = total + taps[3 - n : 4 - n, :] * (w[rows8(ahead + 3), :] * same_ahead)
            raw[rows8(k), :] = total
            return tuple(first + new)

        carry = lax.fori_loop(0, HALF, one, tuple(sums[n] for n in range(TAPS + 1)), unroll=4)
        for n in range(TAPS + 1):
            sums[n] = carry[n]
        gx[h] = jnp.swapaxes(raw[...].reshape(HALF, 8, ch), 0, 1).reshape(half, ch).astype(bf16)
        return net.copy(gx.at[h], gx_in.at[h], net.over_x())

    pull(gh)
    back_first.across_z()
    gx_last = convolve_back(gh)
    for c in mixed_zs:
        c.wait_recv()
    total = tok[gh, z, i].astype(f32) + mixed_core[z].astype(f32)
    for m in range(1, ZS):
        total = total + mixed_z[m - 1].astype(f32)
    mixed_sum[...] = (total + tok_last[...].astype(f32)).astype(bf16)
    net.copy(mixed_sum, mixed, net.over_x())
    back_first.give()
    gate_copy.wait_recv()
    part_z = mm_tn(gate_both[0], normed[0, :, half_cols]) + mm_tn(gate_both[1], normed[1, :, half_cols])
    for r in range(reps):
        wz_low[r] = part_z[r * cols : (r + 1) * cols].astype(bf16)
    for d in range(1, reps):
        net.copy(wz_low.at[net.y_at(d)], wz_theirs.at[d - 1], net.along_y(d))
    net.save(wz_low.at[yi], wz_mine)
    back_first.end()
    out_half = out_low
    if share:
        out_x.wait_recv()
        out_half = out_x_in
        out_half[...] = (out_low[:, own_part].astype(f32) + out_x_in[...].astype(f32)).astype(bf16)
    out_all[j] = out_half[j]
    out_zs = []
    for m in range(1, TP):
        zm, im = net.shared(m)
        out_zs.append(net.copy(out_half.at[zm * 2 + im], out_all.at[j], net.to_shared(m)))
    pull(s)
    gx_first = convolve_back(s)

    def rows_of(q, carry):
        rows = span(q, PACK)
        value = (
            mm(gx[s, rows, :], wx[...]) + mm(gx_in[s, rows, :], wx[...]) + mm(gate_both[s, rows, :], wz[...])
        )
        tok[gh, q] = value.astype(bf16).reshape(2, HALF, width)
        return carry

    mixed_copy.wait_send()
    gx_last.wait_recv()
    lax.fori_loop(0, ZS, rows_of, 0)
    to_core = net.copy(tok.at[gh, :, 1 - i], mixed_core, net.sibling())
    for c in mixed_zs:
        c.wait_send()
    def gain_terms(q, carry):
        x = tok[s, q].astype(f32).reshape(PACK, width)
        inv = lax.rsqrt(jnp.mean(x * x, axis=1, keepdims=True) + EPS)
        terms = tok[gh, q].astype(f32).reshape(PACK, width) * (x * inv)
        return carry + jnp.sum(terms.reshape(PACK // 8, 8, width), axis=0)

    gain_acc[0] = jnp.sum(lax.fori_loop(0, ZS, gain_terms, jnp.zeros((8, width), f32)), axis=0, keepdims=True)
    stages = [
        [net.along_y(d) for d in range(1, reps)],
        [net.sibling()],
        [net.over_x()],
        [net.along_z(1)],
        [net.along_z(2)],
    ]
    slot = [0]

    def gain_start(k):
        cs = []
        for peer in stages[k]:
            cs.append((slot[0], net.copy(gain_acc.at[k], gain_in.at[slot[0]], peer)))
            slot[0] += 1
        return cs

    def gain_end(k, cs):
        total = gain_acc[k]
        for at, c in cs:
            c.wait_recv()
            total = total + gain_in[at]
        gain_acc[k + 1] = total

    cs = gain_start(0)
    to_core.wait_recv()
    for q in range(ZS):
        mixed_low[q] = (tok[gh, q, i].astype(f32) + mixed_core[q].astype(f32)).astype(bf16)
    to_z = [net.copy(mixed_low.at[net.flip(m)], mixed_z.at[m - 1], net.along_z(m)) for m in range(1, ZS)]
    state_all = mm_tn(conv_out[...].astype(bf16), grad_proj[...])
    rows_grad[STEP_ROW : STEP_ROW + 1, :] = jnp.sum(bias_acc[...], axis=0, keepdims=True)
    rows_grad[SKIP_ROW : SKIP_ROW + 1, :] = jnp.sum(skip_acc[...], axis=0, keepdims=True)
    for n in range(STATE):
        rows_grad[DECAY_ROW + n : DECAY_ROW + n + 1, :] = (
            jnp.sum(acc_ref[n], axis=0, keepdims=True) * rate_ref[n : n + 1, :] * LN2
        )
    for n in range(TAPS + 1):
        rows_grad[TAP_ROW + n : TAP_ROW + n + 1, :] = jnp.sum(sums[n], axis=0, keepdims=True)
    for r in range(reps):
        state_part[r] = state_all[r * cols : (r + 1) * cols, :]
        rows_part[r] = rows_grad[:, r * cols : (r + 1) * cols]
    for r in range(reps):
        state_low[r] = state_part[r].astype(bf16)
        rows_low[r] = rows_part[r].astype(bf16)
    for d in range(1, reps):
        net.copy(state_low.at[net.y_at(d)], state_theirs.at[d - 1], net.along_y(d))
        net.copy(rows_low.at[net.y_at(d)], rows_theirs.at[d - 1], net.along_y(d))
    net.save(state_part.at[yi], state_mine)
    net.save(rows_part.at[yi], rows_mine)
    gain_end(0, cs)
    cs = gain_start(1)
    gx_first.wait_recv()
    part_x = mm_tn(gx[0], normed[0, :, half_cols]) + mm_tn(gx[1], normed[1, :, half_cols])
    part_x = part_x + mm_tn(gx_in[0], normed[0, :, half_cols]) + mm_tn(gx_in[1], normed[1, :, half_cols])
    for r in range(reps):
        wx_low[r] = part_x[r * cols : (r + 1) * cols].astype(bf16)
    for d in range(1, reps):
        net.copy(wx_low.at[net.y_at(d)], wx_theirs.at[d - 1], net.along_y(d))
    net.save(wx_low.at[yi], wx_mine)
    gain_end(1, cs)
    cs = gain_start(2)
    for c in out_zs:
        c.wait_recv()
    net.copy(out_all.at[pl.ds(gh * ZS, ZS)], out_theirs, net.over_x())
    net.save(out_all.at[pl.ds(s * ZS, ZS)], out_mine)
    gain_end(2, cs)
    cs = gain_start(3)
    x = tok[s, z, i].astype(f32)
    inv = lax.rsqrt(jnp.mean(x * x, axis=1, keepdims=True) + EPS)
    unit = x * inv
    gain_end(3, cs)
    cs = gain_start(4)
    grad = tok[gh, z, i].astype(f32) + mixed_core[z].astype(f32)
    for m in range(1, ZS):
        to_z[m - 1].wait_recv()
        grad = grad + mixed_z[m - 1].astype(f32)
    scaled = grad * gain[...]
    mean = jnp.mean(scaled * unit, axis=1, keepdims=True)
    grad_tokens[...] = inv * (scaled - unit * mean) + cot_own[...].astype(f32)
    gain_end(4, cs)
    grad_gain[...] = gain_acc[5]
    net.finish()


def block(reps, grids, gain, wstep, taps, bias, step, skip, decay, wstate, wout, cot, tokens, wx, wz):
    cols, width = wx.shape
    ch = reps * cols
    rows = TP * PACK
    half = rows // 2
    piece = wout.shape[0]
    hp = piece // 2 if piece % 32 == 0 else piece
    size = CHUNK * 8
    sds = jax.ShapeDtypeStruct
    V, H = pltpu.VMEM, pl.ANY
    args = [(grids, pltpu.SMEM)]
    args += [(a, V) for a in (gain, wstep, taps, bias, step, skip, decay, wstate, wout, cot)]
    args += [(a, H) for a in (tokens, wx, wz)]
    outs = (
        (sds((HALF, width), bf16), H),
        (sds((HALF, width), f32), V),
        (sds((cols, width // 2), bf16), H),
        (sds((reps - 1, cols, width // 2), bf16), H),
        (sds((cols, width // 2), bf16), H),
        (sds((reps - 1, cols, width // 2), bf16), H),
        (sds((ZS, hp, ch), bf16), H),
        (sds((ZS, hp, ch), bf16), H),
        (sds((SMALL_ROWS, cols), f32), H),
        (sds((reps - 1, SMALL_ROWS, cols), bf16), H),
        (sds((cols, 128), f32), H),
        (sds((reps - 1, cols, 128), bf16), H),
        (sds((1, width), f32), V),
    )
    big = V((rows, ch), f32)
    padded = V((rows + 2 * PAD, ch), f32)
    part = V((rows, 128), f32)
    low = V((half, ch), bf16)
    round_rows = V((size, ch), f32)
    state = V((STATE, 8, ch), f32)
    scratch = (
        V((reps, TP, 16, 128), bf16),
        V((1, width), f32),
        V((2, 8, 128), f32),
        V((reps, cols, width), bf16),
        V((ch, width), bf16),
        V((reps, cols, width), bf16),
        V((ch, width), bf16),
        V((reps, SMALL_ROWS, cols), bf16),
        V((SMALL_ROWS, ch), bf16),
        V((reps, cols, 128), bf16),
        V((ch, 128), bf16),
        V((TP, piece, ch), bf16),
        V((TP, piece, ch), bf16),
        V((reps, TP, piece, ch), bf16),
        V((width, ch), bf16),
        V((2, ZS, 2, HALF, width), bf16),
        V((2, half, width), bf16),
        V((half, ch), f32),
        padded,
        padded,
        big,
        V((half, ch), f32),
        part,
        V((rows, 128), bf16),
        part,
        V((PACK, STATE // 2, 16, ch), bf16),
        round_rows,
        round_rows,
        round_rows,
        state,
        state,
        V((STATE, ch), f32),
        round_rows,
        round_rows,
        V((size, STATE * 128), f32),
        V((size, STATE * 128), f32),
        V((STATE * 128, 128), bf16),
        V((8, ch), f32),
        V((8, ch), f32),
        big,
        low,
        low,
        low,
        low,
        low,
        V((2, half, ch), bf16),
        V((half, width), bf16),
        V((ZS, HALF, width), bf16),
        V((ZS, HALF, width), bf16),
        V((ZS - 1, HALF, width), bf16),
        V((HALF, width), bf16),
        V((HALF, width), bf16),
        V((reps, TP * piece, ch), bf16),
        V((reps - 1, TP * piece, ch), bf16),
        V((TP, piece, ch), bf16),
        V((TP, hp, ch), bf16),
        V((TP, hp, ch), bf16),
        V((reps, cols, width // 2), bf16),
        part,
        V((rows, 128), bf16),
        V((TAPS + 1, 8, ch), f32),
        V((2, half, ch), bf16),
        V((2, half, ch), bf16),
        V((reps, cols, width // 2), bf16),
        V((SMALL_ROWS, ch), f32),
        V((reps, SMALL_ROWS, cols), f32),
        V((reps, cols, 128), f32),
        V((reps, SMALL_ROWS, cols), bf16),
        V((reps, cols, 128), bf16),
        V((6, 1, width), f32),
        V((3 + reps, 1, width), f32),
    ) + REDUCE_SCRATCH * 4
    copies = 120 + 10 * (reps - 1)
    return fused(partial(block_kernel, reps), 1, copies, 12, outs, args, scratch)


def place_kernel(
    reps, index, mixed_in, tokens_in, wx_mine, wx_theirs, wz_mine, wz_theirs, out_mine, out_theirs,
    rows_mine, rows_theirs, state_mine, state_theirs, gain_in,
    mixed, grad_tokens, gain, wx, wz, wout, taps, bias, wstate, wstep, step, decay, skip,
):
    mixed[...] = mixed_in[...]
    grad_tokens[...] = tokens_in[...]
    width, n = gain_in.shape[1], gain.shape[1]
    moved = pltpu.roll(jnp.broadcast_to(gain_in[...], (8, width)), width - index[0] * n, 1)
    gain[...] = moved[0:1, 0:n]

    def total(mine, theirs):
        value = mine[...].astype(f32)
        for d in range(reps - 1):
            value = value + theirs[d].astype(f32)
        return value

    wx[...] = total(wx_mine, wx_theirs)
    wz[...] = total(wz_mine, wz_theirs)
    cols = wx.shape[0]
    hp = out_mine.shape[1]
    share = hp < wout.shape[0]
    s = index[1]
    for q in range(ZS):
        parts = [(out_mine[q].astype(f32), s), (out_theirs[q].astype(f32), 1 - s)]
        if not share:
            parts = [(parts[0][0] + parts[1][0], 0)]
        for value, place in parts:
            for r in range(reps):
                at = ((q // 2) * reps + r) * 2 + q % 2
                rows = pl.ds(pl.multiple_of(place * hp, hp), hp) if share else pl.ds(0, hp)
                wout[rows, at * cols : (at + 1) * cols] = value[:, r * cols : (r + 1) * cols]
    rows = total(rows_mine, rows_theirs)
    wstep[...] = rows[0:DT_RANK]
    taps[...] = rows[TAP_ROW : TAP_ROW + TAPS]
    bias[...] = rows[BIAS_ROW : BIAS_ROW + 1]
    step[...] = rows[STEP_ROW : STEP_ROW + 1]
    skip[...] = rows[SKIP_ROW : SKIP_ROW + 1]
    decay[...] = rows[DECAY_ROW : DECAY_ROW + STATE]
    wstate[...] = total(state_mine, state_theirs)


def place(reps, index, results):
    mixed, grad_tokens, wx = results[0], results[1], results[2]
    ch = results[6].shape[2]
    cols = wx.shape[0]
    width = mixed.shape[1]
    piece = width // (TP * reps)
    sds = jax.ShapeDtypeStruct
    V = pl.BlockSpec(memory_space=pltpu.VMEM)
    outs = (
        sds(mixed.shape, bf16),
        sds(grad_tokens.shape, f32),
        sds((1, width // (2 * TP * reps)), f32),
        sds(wx.shape, f32),
        sds(wx.shape, f32),
        sds((piece, ZS * ch), f32),
        sds((TAPS, cols), f32),
        sds((1, cols), f32),
        sds((cols, 128), f32),
        sds((DT_RANK, cols), f32),
        sds((1, cols), f32),
        sds((STATE, cols), f32),
        sds((1, cols), f32),
    )
    return pl.pallas_call(
        partial(place_kernel, reps),
        out_shape=outs,
        in_specs=[pl.BlockSpec(memory_space=pltpu.SMEM)] + [V] * len(results),
        out_specs=tuple([V] * len(outs)),
        compiler_params=pltpu.CompilerParams(vmem_limit_bytes=63 << 20),
    )(index, *results)


def local(
    reps, tokens, item_grids, norm_gain, proj_in_x, proj_in_z, proj_out, conv_weight, conv_bias,
    proj_state, proj_step, step_bias, decay_log, skip_gain, grad_out,
):
    width = tokens.shape[1]
    results = block(
        reps, item_grids, norm_gain[None], proj_step[0], conv_weight[0], conv_bias, step_bias, skip_gain,
        decay_log[0], proj_state[0], proj_out.T, grad_out.reshape(HALF, width), tokens, proj_in_x.T,
        proj_in_z.T,
    )
    s = lax.axis_index("dir")
    index = jnp.stack([s * lax.axis_size("dp") + lax.axis_index("dp"), s]).astype(jnp.int32)
    (
        mixed, grad_tokens, grad_gain, grad_wx, grad_wz, grad_wout, grad_taps, grad_bias, grad_wstate,
        grad_wstep, grad_step, grad_decay, grad_skip,
    ) = place(reps, index, results)
    return (
        mixed.reshape(1, 1, HALF, width),
        grad_tokens.reshape(1, 1, HALF, width),
        grad_gain[0],
        grad_wx.T,
        grad_wz.T,
        grad_wout.T,
        grad_taps[None],
        grad_bias,
        grad_wstate[None],
        grad_wstep[None],
        grad_step,
        grad_decay[None],
        grad_skip,
    )


def solution(mesh):
    reps = mesh.shape["dp"] // TP
    return jax.shard_map(
        partial(local, reps),
        mesh=mesh,
        in_specs=(
            P("dp", None),
            P("dp", None),
            P("dp"),
            P(None, "dp"),
            P(None, "dp"),
            P(None, "dp"),
            P("dir", None, "dp"),
            P("dir", "dp"),
            P("dir", "dp", None),
            P("dir", None, "dp"),
            P("dir", "dp"),
            P("dir", None, "dp"),
            P("dir", "dp"),
            P("dp", "dir", None, None),
        ),
        out_specs=(
            P("dp", "dir", None, None),
            P("dp", "dir", None, None),
            P(("dir", "dp")),
            P("dir", "dp"),
            P("dir", "dp"),
            P("dir", "dp"),
            P("dir", None, "dp"),
            P("dir", "dp"),
            P("dir", "dp", None),
            P("dir", None, "dp"),
            P("dir", "dp"),
            P("dir", None, "dp"),
            P("dir", "dp"),
        ),
        check_vma=False,
    )
```

```python
from functools import partial

import jax
import jax.numpy as jnp
from jax import lax
from jax.experimental import pallas as pl
from jax.experimental.pallas import tpu as pltpu
from jax.sharding import PartitionSpec as P

f32 = jnp.float32
bf16 = jnp.bfloat16
EPS = 1e-05
DT_RANK = 96
STATE = 16
TAPS = 4
ZS = 4
TP = 8
PACK = 128
HALF = 64
CHUNK = 16
NSTEP = 4
LOG2E = 1.4426950408889634
LN2 = 0.6931471805599453
BIG = 1e9
PAD = 24
TAP_ROW, BIAS_ROW, STEP_ROW, SKIP_ROW, DECAY_ROW, SMALL_ROWS = 96, 100, 101, 102, 103, 128


def mm(left, right):
    return jnp.dot(left, right, preferred_element_type=f32)


def mm_nt(left, right):
    return lax.dot_general(left, right, (((1,), (1,)), ((), ())), preferred_element_type=f32)


def mm_tn(left, right):
    return lax.dot_general(left, right, (((0,), (0,)), ((), ())), preferred_element_type=f32)


def segment_of(t, ends):
    t = t.astype(f32) if hasattr(t, "astype") else float(t)
    return (t >= ends[0]).astype(f32) + (t >= ends[1]).astype(f32)


def rows8(t):
    return pl.ds(pl.multiple_of(t * 8, 8), 8)


def span(start, size):
    return pl.ds(pl.multiple_of(start * size, size), size)


def sigmoid(v):
    return 1.0 / (1.0 + jnp.exp(-v))


def softplus(v):
    return jnp.maximum(v, 0.0) + jnp.log1p(jnp.exp(-jnp.abs(v)))


def wide(mask, ch):
    return jnp.concatenate([mask] * (ch // 128), axis=1)


def tiles(v):
    total = v[:, 0:128]
    for at in range(128, v.shape[1], 128):
        total = total + v[:, at : at + 128]
    return total


class Copy:
    def __init__(self, copy):
        self.copy, self.sent, self.got = copy, False, False
        copy.start()

    def wait_send(self):
        if not self.sent:
            self.copy.wait_send()
            self.sent = True

    def wait_recv(self):
        if not self.got:
            self.copy.wait_recv()
            self.got = True


class Net:
    def __init__(self, reps, send, recv, local):
        self.reps, self.send, self.recv, self.local = reps, send, recv, local
        self.s = lax.axis_index("dir")
        p = lax.axis_index("dp")
        self.i = lax.rem(p, 2)
        self.y = lax.rem(p // 2, reps)
        self.z = p // (2 * reps)
        self.used = 0
        self.moved = 0
        self.copies = []
        self.saves = []

    def place(self, s, z, y, i):
        return (s, (z * self.reps + y) * 2 + i)

    def flip(self, m):
        if m == 1:
            return self.z + 1 - 2 * lax.rem(self.z, 2)
        if m == 2:
            return lax.rem(self.z + 2, ZS)
        return ZS - 1 - self.z

    def over_x(self):
        return self.place(1 - self.s, self.z, self.y, self.i)

    def sibling(self):
        return self.place(self.s, self.z, self.y, 1 - self.i)

    def along_z(self, m):
        return self.place(self.s, self.flip(m), self.y, self.i)

    def shared(self, m):
        z = self.flip(m // 2) if m // 2 else self.z
        i = 1 - self.i if m % 2 else self.i
        return z, i

    def to_shared(self, m):
        z, i = self.shared(m)
        return self.place(self.s, z, self.y, i)

    def y_at(self, d):
        return lax.rem(self.y + d, self.reps)

    def along_y(self, d):
        return self.place(self.s, self.z, self.y_at(d), self.i)

    def greet(self):
        self.peers = [self.over_x()] + [self.to_shared(m) for m in range(1, TP)]
        self.peers += [self.along_y(d) for d in range(1, self.reps)]
        barrier = pltpu.get_barrier_semaphore()
        for peer in self.peers:
            pl.semaphore_signal(barrier, inc=1, device_id=peer, device_id_type=pl.DeviceIdType.MESH)

    def met(self):
        pl.semaphore_wait(pltpu.get_barrier_semaphore(), len(self.peers))

    def copy(self, source, target, peer):
        k = self.used
        self.used += 1
        c = Copy(
            pltpu.make_async_remote_copy(
                src_ref=source,
                dst_ref=target,
                send_sem=self.send.at[k],
                recv_sem=self.recv.at[k],
                device_id=peer,
                device_id_type=pl.DeviceIdType.MESH,
            )
        )
        self.copies.append(c)
        return c

    def gather_z(self, source, at):
        c = ZGather(self, source, at)
        self.copies.append(c)
        return c

    def load(self, source, target):
        c = pltpu.make_async_copy(source, target, self.local.at[self.moved])
        self.moved += 1
        c.start()
        return c

    def save(self, source, target):
        self.saves.append(self.load(source, target))

    def finish(self):
        for c in self.copies:
            c.wait_recv()
            c.wait_send()
        for c in self.saves:
            c.wait()


class ZGather:
    def __init__(self, net, source, at):
        self.net, self.at = net, at
        self.near = [net.copy(source, at(net.z), net.along_z(m)) for m in (1, 2)]
        self.inner = lax.rem(net.z + 1, ZS) >= 2
        k = net.used
        net.used += 2
        self.direct = self.make(source, at(net.z), k, k, 3)
        far = at(net.flip(2))
        self.onward = self.make(far, far, k + 1, k, 1)
        self.got = False

        @pl.when(self.inner)
        def _():
            self.direct.start()

    def make(self, source, target, out, arrival, m):
        return pltpu.make_async_remote_copy(
            src_ref=source,
            dst_ref=target,
            send_sem=self.net.send.at[out],
            recv_sem=self.net.recv.at[arrival],
            device_id=self.net.along_z(m),
            device_id_type=pl.DeviceIdType.MESH,
        )

    def wait(self, m):
        if m < 3:
            self.near[m - 1].wait_recv()
            if m == 2:

                @pl.when(self.inner)
                def _():
                    self.onward.start()

        elif not self.got:
            self.direct.wait_recv()
            self.got = True
        return self.at(self.net.flip(m))

    def wait_recv(self):
        pass

    def wait_send(self):
        @pl.when(self.inner)
        def _():
            self.direct.wait_send()
            self.onward.wait_send()


class Reduce:
    def __init__(self, net, part, base, size, fold, out_low, in_low, total):
        self.net, self.part, self.base = net, part, base
        self.fold, self.out_low, self.in_low, self.total = fold, out_low, in_low, total
        self.rows = size // 2
        self.block = self.rows // ZS
        self.first = net.copy(part.at[self.at(1 - net.i, self.rows)], fold, net.sibling())

    def at(self, n, size):
        return pl.ds(pl.multiple_of(self.base + n * size, size), size)

    def across_z(self):
        net, fold = self.net, self.fold
        self.first.wait_recv()
        fold[...] = self.part[self.at(net.i, self.rows), :] + fold[...]
        self.out_low[...] = fold[...].astype(bf16).reshape(ZS, self.block, 128)
        self.cs = [
            net.copy(self.out_low.at[net.flip(m)], self.in_low.at[m - 1], net.along_z(m))
            for m in range(1, ZS)
        ]

    def give(self):
        net, total = self.net, self.total
        mine = self.at(net.i * ZS + net.z, self.block)
        value = self.fold[span(net.z, self.block), :]
        for m in range(1, ZS):
            self.cs[m - 1].wait_recv()
            value = value + self.in_low[m - 1].astype(f32)
        total[mine, :] = value.astype(bf16)
        self.cs = [net.copy(total.at[mine], total.at[mine], net.along_z(m)) for m in range(1, ZS)]
        self.ds = [net.copy(total.at[mine], total.at[mine], net.sibling())]

    def end(self):
        net, total = self.net, self.total
        for m in range(1, ZS):
            self.cs[m - 1].wait_recv()
            there = self.at(net.i * ZS + net.flip(m), self.block)
            self.ds.append(net.copy(total.at[there], total.at[there], net.sibling()))
        for d in self.ds:
            d.wait_recv()


REDUCE_ROWS = TP * HALF
REDUCE_SCRATCH = (
    pltpu.VMEM((REDUCE_ROWS // 2, 128), f32),
    pltpu.VMEM((ZS, REDUCE_ROWS // 2 // ZS, 128), bf16),
    pltpu.VMEM((ZS - 1, REDUCE_ROWS // 2 // ZS, 128), bf16),
)


def fused(kernel, name_id, copies, moves, outs, args, scratch):
    return pl.pallas_call(
        kernel,
        out_shape=tuple(o for o, _ in outs),
        in_specs=[pl.BlockSpec(memory_space=m) for _, m in args],
        out_specs=tuple(pl.BlockSpec(memory_space=m) for _, m in outs),
        scratch_shapes=list(scratch)
        + [pltpu.SemaphoreType.DMA((n,)) for n in (copies, copies, moves)],
        compiler_params=pltpu.CompilerParams(
            collective_id=name_id, has_side_effects=True, vmem_limit_bytes=63 << 20
        ),
    )(*(a for a, _ in args))


def block_kernel(reps, *refs):
    refs = list(refs)

    def take_refs(n):
        out = refs[:n]
        del refs[:n]
        return out

    (
        grids, gain_own, wstep_own, taps_own, bias_own, step_own, skip_own, decay_own, wstate_own, wout_hbm,
        cot_hbm, tokens, wx_own, wz_own,
    ) = take_refs(14)
    (
        mixed, grad_tokens, wx_mine, wx_theirs, wz_mine, wz_theirs, out_mine, out_theirs, rows_mine,
        rows_theirs, state_mine, state_theirs, grad_gain,
    ) = take_refs(13)
    (
        meta_all, gain, ends_ref, wx_all, wx, wz_all, wz, small_all, small, wstate_all, wstate,
        wout_send, wout_in, wout_all, wout,
    ) = take_refs(15)
    (tok, normed, raw, conv_in, conv_pre, conv_out, gate_in, part, proj_low, proj) = take_refs(10)
    (
        hprev, step, decay_step, u, state, acc_ref, rate_ref, s1, s2, pb, pc, ones, bias_acc, skip_acc, g,
    ) = take_refs(15)
    (y_send, y_in, g_send, g_in, gated, gate_both, cot, mixed_core, mixed_low, mixed_z, mixed_sum, tok_last, wout_own, cot_own) = take_refs(14)
    (out_send, out_y, out_low, out_x_in, out_all, wz_low, part_back, grad_proj, sums, gx, gx_in) = take_refs(11)
    (wx_low, rows_grad, rows_part, state_part, rows_low, state_low, gain_acc, gain_in) = take_refs(8)
    reduces = [take_refs(3) for _ in range(4)]
    send, recv, local_sems = refs
    net = Net(reps, send, recv, local_sems)
    net.greet()
    s, z, yi, i = net.s, net.z, net.y, net.i
    sgn = 1 - 2 * s
    gh = 1 - s
    j = z * 2 + i
    cols, width = wx_own.shape
    ch = reps * cols
    piece = wout_hbm.shape[0]
    half = TP * HALF
    rounds = HALF // CHUNK
    size = CHUNK * 8
    share = piece % 32 == 0
    hp = piece // 2 if share else piece
    own_part = pl.ds(pl.multiple_of(s * hp, hp), hp) if share else pl.ds(0, piece)
    half_cols = pl.ds(pl.multiple_of(s * (width // 2), 128), width // 2)

    own_loads = [net.load(tokens.at[pl.ds(h * HALF, HALF)], tok.at[h, z, i]) for h in range(2)]
    own_loads += [net.load(wx_own, wx_all.at[yi]), net.load(wz_own, wz_all.at[yi])]
    own_loads += [net.load(wout_hbm, wout_own), net.load(cot_hbm, cot_own)]
    own_loads += [net.load(tokens.at[pl.ds(pl.multiple_of(gh * HALF, HALF), HALF)], tok_last)]
    first_end = (grids[0, 0] * grids[0, 1]).astype(f32)
    second_end = first_end + (grids[1, 0] * grids[1, 1]).astype(f32)
    row = lax.broadcasted_iota(jnp.int32, (16, 128), 0)
    gain_row = jnp.concatenate([gain_own[...].astype(f32), jnp.zeros((1, 128 - piece), f32)], axis=1)
    meta = jnp.where(row == 0, gain_row, jnp.where(row == 1, first_end, second_end))
    meta_all[yi, j] = meta.astype(bf16)
    small_rows = [ref[...].astype(f32) for ref in (wstep_own, taps_own, bias_own, step_own, skip_own, decay_own)]
    small_rows.append(jnp.zeros((SMALL_ROWS - DECAY_ROW - STATE, cols), f32))
    small_all[yi] = jnp.concatenate(small_rows, axis=0).astype(bf16)
    wstate_all[yi] = wstate_own[...]
    net.met()
    own_first = tokens.at[pl.ds(pl.multiple_of(s * HALF, HALF), HALF)]
    own_last = tokens.at[pl.ds(pl.multiple_of(gh * HALF, HALF), HALF)]
    from_z = net.gather_z(own_first, lambda zz: tok.at[s, zz, i])
    core_first = [net.copy(own_first, tok.at[s, z, i], net.sibling())]
    core_last = [net.copy(own_last, tok.at[gh, z, i], net.sibling())]
    metas = [net.copy(meta_all.at[yi, j], meta_all.at[yi, j], net.to_shared(m)) for m in range(1, TP)]
    first_y = []
    for d in range(1, reps):
        first_y.append(net.copy(wx_own, wx_all.at[yi], net.along_y(d)))
        for ref in (small_all, wstate_all):
            first_y.append(net.copy(ref.at[yi], ref.at[yi], net.along_y(d)))
    cot_mine = span(j, HALF)
    cot_x = net.copy(cot_hbm, cot.at[cot_mine], net.over_x())
    for c in metas:
        c.wait_recv()
    meta_y = [net.copy(meta_all.at[yi], meta_all.at[yi], net.along_y(d)) for d in range(1, reps)]
    late_y = [net.copy(wz_own, wz_all.at[yi], net.along_y(d)) for d in range(1, reps)]

    for ref in (conv_in, conv_pre):
        ref[0:PAD, :] = jnp.zeros((PAD, ch), f32)
        ref[PAD + 8 * PACK :, :] = jnp.zeros((PAD, ch), f32)
    for b in range(TP):
        both = meta_all[yi, b].astype(f32)
        ends_ref[0, b : b + 1, :] = both[1:2, :]
        ends_ref[1, b : b + 1, :] = both[2:3, :]
    source = lax.broadcasted_iota(jnp.int32, (STATE * 128, 128), 0) // 128
    target = lax.broadcasted_iota(jnp.int32, (STATE * 128, 128), 1)
    ones[...] = (target == DT_RANK + source).astype(f32).astype(bf16)
    rows_grad[...] = jnp.zeros_like(rows_grad)
    state[...] = jnp.zeros_like(state)
    for c in own_loads:
        c.wait()
    for p in range(TP * reps):
        zp, yp, ip = p // (2 * reps), (p // 2) % reps, p % 2
        wout_send[zp * 2 + ip, :, yp * cols : (yp + 1) * cols] = wout_own[:, p * cols : (p + 1) * cols]
    wout_in[j, own_part] = wout_send[j, own_part]

    from_x = []
    for m in range(1, ZS):
        there = from_z.wait(m)
        core_first.append(net.copy(there, there, net.sibling()))
        from_x.append(net.copy(there, there, net.over_x()))
    wout_z = []
    for m in range(1, TP):
        zm, im = net.shared(m)
        wout_z.append(net.copy(wout_send.at[zm * 2 + im, own_part], wout_in.at[j, own_part], net.to_shared(m)))
    cot_x.wait_recv()

    def gather_cot(part):
        rows = lambda zz: cot.at[span((zz * 2 + i) * 2 + part, HALF // 2)]
        return net.gather_z(rows(z), rows)

    def pass_cot(part, m):
        there = cot_zs[part].wait(m)
        cot_core.append(net.copy(there, there, net.sibling()))

    cot_zs = [gather_cot(0)]
    cot_core = [net.copy(cot.at[cot_mine], cot.at[cot_mine], net.sibling())]
    for c in meta_y + first_y:
        c.wait_recv()
    for p in range(TP * reps):
        zp, yp, ip = p // (2 * reps), (p // 2) % reps, p % 2
        gain[:, p * piece : (p + 1) * piece] = meta_all[yp, zp * 2 + ip].astype(f32)[0:1, 0:piece]
    for r in range(reps):
        wx[r * cols : (r + 1) * cols, :] = wx_all[r]
        small[:, r * cols : (r + 1) * cols] = small_all[r]
        wstate[r * cols : (r + 1) * cols, :] = wstate_all[r]
    for c in core_first:
        c.wait_recv()

    ends = (ends_ref[0], ends_ref[1])
    vectors = small[DT_RANK : DT_RANK + 16, :].astype(f32)
    taps = vectors[0 : TAPS + 1, :]
    step_bias = vectors[STEP_ROW - DT_RANK : STEP_ROW - DT_RANK + 1, :]
    skip = vectors[SKIP_ROW - DT_RANK : SKIP_ROW - DT_RANK + 1, :]

    def take(h):
        def one(q, carry):
            rows = span(q, PACK)
            x = tok[h, q].astype(f32).reshape(PACK, width)
            inv = lax.rsqrt(jnp.mean(x * x, axis=1, keepdims=True) + EPS)
            low = (x * inv * gain[...]).astype(bf16)
            normed[h, rows, :] = low
            raw[rows, :] = mm_nt(low, wx[...])
            return carry

        lax.fori_loop(0, ZS, one, 0)
        x = jnp.swapaxes(raw[...].reshape(8, HALF, ch), 0, 1).reshape(half, ch)
        conv_in[pl.ds(pl.multiple_of(PAD + h * half, 8), half), :] = x

    def convolve(h, sums):
        def one(k, carry):
            t = h * HALF + k
            seg = segment_of(t, ends)
            total = taps[4:5, :] + taps[3:4, :] * conv_in[rows8(t + 3), :]
            for n in range(1, TAPS):
                there = t - n * sgn
                same = wide((segment_of(there, ends) == seg).astype(f32), ch)
                total = total + taps[3 - n : 4 - n, :] * (conv_in[rows8(there + 3), :] * same)
            conv_pre[rows8(t + 3), :] = total
            act = total * sigmoid(total)
            conv_out[rows8(t), :] = act.astype(bf16).astype(f32)
            return carry

        lax.fori_loop(0, HALF, one, 0, unroll=4)
        rows = span(h, half)
        part[rows, :] = mm(conv_out[rows, :].astype(bf16), wstate[...])
        return Reduce(net, part, h * half, half, *sums, proj_low)

    take(s)
    sum_first = convolve(s, reduces[0])

    def last_tokens(m):
        from_x[m - 1].wait_recv()
        there = tok.at[gh, net.flip(m), i]
        core_last.append(net.copy(there, there, net.sibling()))

    last_tokens(1)
    sum_first.across_z()
    last_tokens(2)
    last_tokens(3)
    for c in wout_z:
        c.wait_recv()
    wout_x = [net.copy(wout_in.at[:, own_part], wout_in.at[:, own_part], net.over_x())] if share else []
    sum_first.give()
    cot_zs.append(gather_cot(1))
    pass_cot(0, 1)
    pass_cot(0, 2)
    for c in core_last:
        c.wait_recv()
    take(gh)
    sum_last = convolve(gh, reduces[1])
    sum_first.end()
    first_rows = span(s, half)
    last_rows = span(gh, half)
    proj[first_rows, :] = proj_low[first_rows, :].astype(f32)

    wstep = jnp.where(lax.broadcasted_iota(jnp.int32, (128, ch), 0) < DT_RANK, small[...], 0.0).astype(bf16)
    rate_ref[...] = -LOG2E * jnp.exp(small[DT_RANK:, :].astype(f32)[DECAY_ROW - DT_RANK : DECAY_ROW - DT_RANK + STATE, :])
    y = g

    def prepare(block, first):
        rows = span(block, size)
        pre = mm(proj_low[rows, :], wstep) + step_bias
        if first:
            step[rows, :] = softplus(pre)
        step_all = step[rows, :]
        values = conv_out[rows, :]
        u[...] = step_all * values
        for k in range(CHUNK):
            t = block * CHUNK + k
            fresh = segment_of(t, ends) != segment_of(t - sgn, ends)
            decay_step[8 * k : 8 * k + 8, :] = jnp.where(
                wide(fresh, ch), BIG, step_all[8 * k : 8 * k + 8, :]
            )
        return rows, pre, values

    def rates(n0):
        return [jnp.broadcast_to(rate_ref[n : n + 1, :], (8, ch)) for n in range(n0, n0 + NSTEP)]

    def forward(c, carry):
        block = c + s * (2 * rounds - 1 - 2 * c)
        rows, _, values = prepare(block, True)
        y[rows, :] = skip * values
        for n0 in range(0, STATE, NSTEP):
            rate = rates(n0)

            def body(k, hs):
                r = s * (CHUNK - 1 - k) + (1 - s) * k
                t = block * CHUNK + r
                pv = proj[rows8(t), :]
                st = decay_step[rows8(r), :]
                uv = u[rows8(r), :]
                total = y[rows8(t), :]
                new = []
                for m in range(NSTEP):
                    n = n0 + m
                    if m % 2 == 0:
                        hprev[t, n // 2] = jnp.concatenate([hs[m], hs[m + 1]], axis=0).astype(bf16)
                    h = jnp.exp2(st * rate[m]) * hs[m] + uv * pv[:, DT_RANK + n : DT_RANK + n + 1]
                    total = total + h * pv[:, DT_RANK + STATE + n : DT_RANK + STATE + n + 1]
                    new.append(h)
                y[rows8(t), :] = total
                return tuple(new)

            hs = lax.fori_loop(0, CHUNK, body, tuple(state[n] for n in range(n0, n0 + NSTEP)), unroll=CHUNK)
            for m in range(NSTEP):
                state[n0 + m] = hs[m]
        return carry

    def send_readout(n):
        at = n + s * (rounds - 1 - 2 * n)
        rows = span(at, size)
        y_send[rows, :] = y[span(s * rounds + at, size), :].astype(bf16)
        return net.copy(y_send.at[rows], y_in.at[rows], net.over_x())

    sum_last.across_z()
    for c in wout_x:
        c.wait_recv()
    wout_y = [net.copy(wout_in, wout_all.at[yi], net.along_y(d)) for d in range(1, reps)]
    wout_all[yi] = wout_in[...]
    lax.fori_loop(0, rounds // 2, forward, 0)
    sum_last.give()
    y_copies = [send_readout(n) for n in range(rounds // 2)]
    lax.fori_loop(rounds // 2, rounds, forward, 0)
    y_copies += [send_readout(n) for n in (rounds // 2, rounds - 1)]
    pass_cot(0, 3)
    sum_last.end()
    pass_cot(1, 1)
    pass_cot(1, 2)
    proj[last_rows, :] = proj_low[last_rows, :].astype(f32)
    for c in late_y:
        c.wait_recv()
    for r in range(reps):
        wz[r * cols : (r + 1) * cols, :] = wz_all[r]
    gate_in[...] = mm_nt(normed[gh], wz[...])
    lax.fori_loop(rounds, 2 * rounds - 1, forward, 0)
    lax.fori_loop(2 * rounds - 1, 2 * rounds, forward, 0)
    for c in wout_y:
        c.wait_recv()
    for p in range(TP * reps):
        zp, yp, ip = p // (2 * reps), (p // 2) % reps, p % 2
        wout[p * piece : (p + 1) * piece, :] = wout_all[yp, zp * 2 + ip]
    for c in y_copies:
        c.wait_recv()

    summed = y[last_rows, :] + y_in[...].astype(f32)
    raw[...] = jnp.swapaxes(summed.reshape(HALF, 8, ch), 0, 1).reshape(half, ch)

    def gate_rows(q, carry):
        rows = span(q, PACK)
        gate = gate_in[rows, :]
        low = (raw[rows, :] * (gate * sigmoid(gate))).astype(bf16)
        gated[rows, :] = low
        tok[gh, q] = mm_nt(low, wout[...]).astype(bf16).reshape(2, HALF, width)
        return carry

    def grad_rows(q, carry):
        rows = span(q, PACK)
        gate = gate_in[rows, :]
        sig = sigmoid(gate)
        grad_gated = mm(cot[rows, :], wout[...])
        gate_both[gh, rows, :] = (grad_gated * raw[rows, :] * sig * (1.0 + gate * (1.0 - sig))).astype(bf16)
        gate_in[rows, :] = grad_gated * (gate * sig)
        return carry

    for c in core_last:
        c.wait_send()
    lax.fori_loop(0, ZS, gate_rows, 0)
    mixed_copy = net.copy(tok.at[gh, :, 1 - i], mixed_core, net.sibling())
    pass_cot(1, 3)
    for c in cot_core:
        c.wait_recv()
    lax.fori_loop(0, ZS, grad_rows, 0)
    back = jnp.swapaxes(gate_in[...].reshape(8, HALF, ch), 0, 1).reshape(half, ch)
    g[last_rows, :] = back
    g_send[...] = back.astype(bf16)
    g_copy = net.copy(g_send, g_in, net.over_x())
    gate_copy = net.copy(gate_both.at[gh], gate_both.at[gh], net.over_x())
    mixed_copy.wait_recv()
    for q in range(ZS):
        mixed_low[q] = (tok[gh, q, i].astype(f32) + mixed_core[q].astype(f32)).astype(bf16)
    mixed_zs = [net.copy(mixed_low.at[net.flip(m)], mixed_z.at[m - 1], net.along_z(m)) for m in range(1, ZS)]

    state[...] = jnp.zeros_like(state)
    acc_ref[...] = jnp.zeros_like(acc_ref)
    bias_acc[...] = jnp.zeros_like(bias_acc)
    skip_acc[...] = jnp.zeros_like(skip_acc)

    def backward(c, carry):
        block = (1 - s) * (2 * rounds - 1 - c) + s * c
        rows, pre, values = prepare(block, False)
        s1[...] = jnp.zeros_like(s1)
        s2[...] = jnp.zeros_like(s2)
        for n0 in range(0, STATE, NSTEP):
            rate = rates(n0)

            def body(k, both):
                lams, accs = both
                r = s * k + (1 - s) * (CHUNK - 1 - k)
                t = block * CHUNK + r
                here = rows8(r)
                pv = proj[rows8(t), :]
                gv = g[rows8(t), :]
                uv = u[here, :]
                stv = step[rows8(t), :]
                st = decay_step[here, :]
                one = s1[here, :]
                two = s2[here, :]
                new_lams, new_accs = [], []
                for m in range(NSTEP):
                    n = n0 + m
                    if m % 2 == 0:
                        pair = hprev[t, n // 2].astype(f32)
                    a = jnp.exp2(st * rate[m])
                    ah = a * pair[8 * (m % 2) : 8 * (m % 2) + 8]
                    lam = gv * pv[:, DT_RANK + STATE + n : DT_RANK + STATE + n + 1] + lams[m]
                    w = lam * ah
                    new_lams.append(a * lam)
                    two = two + rate[m] * w
                    new_accs.append(accs[m] + stv * w)
                    one = one + lam * pv[:, DT_RANK + n : DT_RANK + n + 1]
                    pb[here, 128 * n : 128 * n + 128] = tiles(lam * uv)
                    pc[here, 128 * n : 128 * n + 128] = tiles(gv * ah)
                s1[here, :] = one
                s2[here, :] = two
                return tuple(new_lams), tuple(new_accs)

            first = (
                tuple(state[n] for n in range(n0, n0 + NSTEP)),
                tuple(acc_ref[n] for n in range(n0, n0 + NSTEP)),
            )
            lams, accs = lax.fori_loop(0, CHUNK, body, first, unroll=CHUNK)
            for m in range(NSTEP):
                state[n0 + m] = lams[m]
                acc_ref[n0 + m] = accs[m]
        gv = g[rows, :]
        one = s1[...]
        q = (LN2 * s2[...] + values * one) * sigmoid(pre)
        q_low = q.astype(bf16)
        bias_acc[...] += jnp.sum(q.reshape(CHUNK, 8, ch), axis=0)
        skip_acc[...] += jnp.sum((gv * values).reshape(CHUNK, 8, ch), axis=0)
        rows_grad[0:DT_RANK, :] += mm_tn(proj_low[rows, :], q_low)[0:DT_RANK, :]
        gu = jnp.sum(gv * u[...], axis=1, keepdims=True)
        lane = lax.broadcasted_iota(jnp.int32, (size, 128), 1)
        read_part = mm(pc[...].astype(bf16), ones[...]) + gu * jnp.where(
            lane < DT_RANK + STATE, proj[rows, :], 0.0
        )
        read_part = jnp.where(lane >= DT_RANK + STATE, pltpu.roll(read_part, STATE, 1), 0.0)
        part_back[rows, :] = mm_nt(q_low, wstep) + mm(pb[...].astype(bf16), ones[...]) + read_part
        g[rows, :] = gv * skip + step[rows, :] * one
        return carry

    lax.fori_loop(0, 1, backward, 0)
    quarter = width // ZS
    for q in range(ZS):
        value = mm_tn(cot[:, q * quarter : (q + 1) * quarter], gated[...]).astype(bf16)
        for r in range(reps):
            out_send[r, q * 2 * piece : (q + 1) * 2 * piece, :] = value[r * 2 * piece : (r + 1) * 2 * piece, :]
    out_copies = [
        net.copy(out_send.at[net.y_at(d)], out_y.at[d - 1], net.along_y(d)) for d in range(1, reps)
    ]
    lax.fori_loop(1, rounds, backward, 0)
    back_last = Reduce(net, part_back, gh * half, half, *reduces[2], grad_proj)
    g_copy.wait_recv()
    g[first_rows, :] = g_in[...].astype(f32)
    lax.fori_loop(rounds, rounds + 1, backward, 0)
    for c in out_copies:
        c.wait_recv()
    total = out_send[yi].astype(f32)
    for d in range(1, reps):
        total = total + out_y[d - 1].astype(f32)
    total = total.astype(bf16)
    for q in range(TP):
        out_low[q] = total[q * piece : (q + 1) * piece]
    if share:
        other_part = pl.ds(pl.multiple_of(gh * hp, hp), hp)
        out_x = net.copy(out_low.at[:, other_part], out_x_in, net.over_x())
    back_last.across_z()
    lax.fori_loop(rounds + 1, 2 * rounds - 1, backward, 0)
    back_last.give()
    lax.fori_loop(2 * rounds - 1, 2 * rounds, backward, 0)
    back_first = Reduce(net, part_back, s * half, half, *reduces[3], grad_proj)
    back_last.end()

    w = conv_pre
    sums[...] = jnp.zeros_like(sums)

    def pull(h):
        def one(b, carry):
            at = h * half + b * PACK
            rows = pl.ds(pl.multiple_of(PAD + at, 8), PACK)
            at = pl.ds(pl.multiple_of(at, PACK), PACK)
            c = conv_pre[rows, :]
            sig = sigmoid(c)
            w[rows, :] = (g[at, :] + mm_nt(grad_proj[at, :], wstate[...])) * (sig * (1.0 + c * (1.0 - sig)))
            return carry

        lax.fori_loop(0, half // PACK, one, 0)

    def convolve_back(h):
        def one(k, carry):
            t = h * HALF + k
            seg = segment_of(t, ends)
            here = w[rows8(t + 3), :]
            total = taps[3:4, :] * here
            new = [carry[3] + here * conv_in[rows8(t + 3), :], carry[4] + here]
            first = []
            for n in range(1, TAPS):
                back = t - n * sgn
                ahead = t + n * sgn
                same_back = wide((segment_of(back, ends) == seg).astype(f32), ch)
                same_ahead = wide((segment_of(ahead, ends) == seg).astype(f32), ch)
                first.insert(0, carry[3 - n] + here * (conv_in[rows8(back + 3), :] * same_back))
                total = total + taps[3 - n : 4 - n, :] * (w[rows8(ahead + 3), :] * same_ahead)
            raw[rows8(k), :] = total
            return tuple(first + new)

        carry = lax.fori_loop(0, HALF, one, tuple(sums[n] for n in range(TAPS + 1)), unroll=4)
        for n in range(TAPS + 1):
            sums[n] = carry[n]
        gx[h] = jnp.swapaxes(raw[...].reshape(HALF, 8, ch), 0, 1).reshape(half, ch).astype(bf16)
        return net.copy(gx.at[h], gx_in.at[h], net.over_x())

    pull(gh)
    back_first.across_z()
    gx_last = convolve_back(gh)
    for c in mixed_zs:
        c.wait_recv()
    total = tok[gh, z, i].astype(f32) + mixed_core[z].astype(f32)
    for m in range(1, ZS):
        total = total + mixed_z[m - 1].astype(f32)
    mixed_sum[...] = (total + tok_last[...].astype(f32)).astype(bf16)
    net.copy(mixed_sum, mixed, net.over_x())
    back_first.give()
    out_half = out_low
    if share:
        out_x.wait_recv()
        out_half = out_x_in
        out_half[...] = (out_low[:, own_part].astype(f32) + out_x_in[...].astype(f32)).astype(bf16)
    out_all[j] = out_half[j]
    out_zs = []
    for m in range(1, TP):
        zm, im = net.shared(m)
        out_zs.append(net.copy(out_half.at[zm * 2 + im], out_all.at[j], net.to_shared(m)))
    gate_copy.wait_recv()
    part_z = mm_tn(gate_both[0], normed[0, :, half_cols]) + mm_tn(gate_both[1], normed[1, :, half_cols])
    for r in range(reps):
        wz_low[r] = part_z[r * cols : (r + 1) * cols].astype(bf16)
    for d in range(1, reps):
        net.copy(wz_low.at[net.y_at(d)], wz_theirs.at[d - 1], net.along_y(d))
    net.save(wz_low.at[yi], wz_mine)
    back_first.end()
    pull(s)
    gx_first = convolve_back(s)

    def rows_of(q):
        rows = span(q, PACK)
        both = gx[s, rows, :].astype(f32) + gx_in[s, rows, :].astype(f32)
        value = (
            mm(both.astype(bf16), wx[...]) + mm(gate_both[s, rows, :], wz[...])
        )
        tok[gh, q] = value.astype(bf16).reshape(2, HALF, width)
        return net.copy(tok.at[gh, q, 1 - i], mixed_core.at[q], net.sibling())

    def send_on(m, c):
        q = net.flip(m)
        c.wait_recv()
        mixed_low[q] = (tok[gh, q, i].astype(f32) + mixed_core[q].astype(f32)).astype(bf16)
        to_z.append(net.copy(mixed_low.at[q], mixed_z.at[m - 1], net.along_z(m)))

    mixed_copy.wait_send()
    for c in mixed_zs:
        c.wait_send()
    gx_last.wait_recv()
    to_z = []
    far = rows_of(net.flip(2))
    middle = rows_of(net.flip(3))
    send_on(2, far)
    near = rows_of(net.flip(1))
    send_on(3, middle)
    to_core = rows_of(z)
    send_on(1, near)
    def gain_terms(q, carry):
        x = tok[s, q].astype(f32).reshape(PACK, width)
        inv = lax.rsqrt(jnp.mean(x * x, axis=1, keepdims=True) + EPS)
        terms = tok[gh, q].astype(f32).reshape(PACK, width) * (x * inv)
        return carry + jnp.sum(terms.reshape(PACK // 8, 8, width), axis=0)

    gain_acc[0] = jnp.sum(lax.fori_loop(0, ZS, gain_terms, jnp.zeros((8, width), f32)), axis=0, keepdims=True)
    stages = [
        [net.along_y(d) for d in range(1, reps)],
        [net.sibling()],
        [net.over_x()],
        [net.along_z(1)],
        [net.along_z(2)],
    ]
    slot = [0]

    def gain_start(k):
        cs = []
        for peer in stages[k]:
            cs.append((slot[0], net.copy(gain_acc.at[k], gain_in.at[slot[0]], peer)))
            slot[0] += 1
        return cs

    def gain_end(k, cs):
        total = gain_acc[k]
        for at, c in cs:
            c.wait_recv()
            total = total + gain_in[at]
        gain_acc[k + 1] = total

    cs = gain_start(0)
    state_all = mm_tn(conv_out[...].astype(bf16), grad_proj[...])
    rows_grad[STEP_ROW : STEP_ROW + 1, :] = jnp.sum(bias_acc[...], axis=0, keepdims=True)
    rows_grad[SKIP_ROW : SKIP_ROW + 1, :] = jnp.sum(skip_acc[...], axis=0, keepdims=True)
    for n in range(STATE):
        rows_grad[DECAY_ROW + n : DECAY_ROW + n + 1, :] = (
            jnp.sum(acc_ref[n], axis=0, keepdims=True) * rate_ref[n : n + 1, :] * LN2
        )
    for n in range(TAPS + 1):
        rows_grad[TAP_ROW + n : TAP_ROW + n + 1, :] = jnp.sum(sums[n], axis=0, keepdims=True)
    for r in range(reps):
        state_part[r] = state_all[r * cols : (r + 1) * cols, :]
        rows_part[r] = rows_grad[:, r * cols : (r + 1) * cols]
    for r in range(reps):
        state_low[r] = state_part[r].astype(bf16)
        rows_low[r] = rows_part[r].astype(bf16)
    for d in range(1, reps):
        net.copy(state_low.at[net.y_at(d)], state_theirs.at[d - 1], net.along_y(d))
        net.copy(rows_low.at[net.y_at(d)], rows_theirs.at[d - 1], net.along_y(d))
    net.save(state_part.at[yi], state_mine)
    net.save(rows_part.at[yi], rows_mine)
    gain_end(0, cs)
    cs = gain_start(1)
    gx_first.wait_recv()
    part_x = mm_tn(gx[0], normed[0, :, half_cols]) + mm_tn(gx[1], normed[1, :, half_cols])
    part_x = part_x + mm_tn(gx_in[0], normed[0, :, half_cols]) + mm_tn(gx_in[1], normed[1, :, half_cols])
    for r in range(reps):
        wx_low[r] = part_x[r * cols : (r + 1) * cols].astype(bf16)
    for d in range(1, reps):
        net.copy(wx_low.at[net.y_at(d)], wx_theirs.at[d - 1], net.along_y(d))
    net.save(wx_low.at[yi], wx_mine)
    gain_end(1, cs)
    cs = gain_start(2)
    for c in out_zs:
        c.wait_recv()
    net.copy(out_all.at[pl.ds(gh * ZS, ZS)], out_theirs, net.over_x())
    net.save(out_all.at[pl.ds(s * ZS, ZS)], out_mine)
    gain_end(2, cs)
    cs = gain_start(3)
    x = tok[s, z, i].astype(f32)
    inv = lax.rsqrt(jnp.mean(x * x, axis=1, keepdims=True) + EPS)
    unit = x * inv
    gain_end(3, cs)
    cs = gain_start(4)
    to_core.wait_recv()
    grad = tok[gh, z, i].astype(f32) + mixed_core[z].astype(f32)
    for c in to_z:
        c.wait_recv()
    for m in range(1, ZS):
        grad = grad + mixed_z[m - 1].astype(f32)
    scaled = grad * gain[...]
    mean = jnp.mean(scaled * unit, axis=1, keepdims=True)
    grad_tokens[...] = inv * (scaled - unit * mean) + cot_own[...].astype(f32)
    gain_end(4, cs)
    grad_gain[...] = gain_acc[5]
    net.finish()


def block(reps, grids, gain, wstep, taps, bias, step, skip, decay, wstate, wout, cot, tokens, wx, wz):
    cols, width = wx.shape
    ch = reps * cols
    rows = TP * PACK
    half = rows // 2
    piece = wout.shape[0]
    hp = piece // 2 if piece % 32 == 0 else piece
    size = CHUNK * 8
    sds = jax.ShapeDtypeStruct
    V, H = pltpu.VMEM, pl.ANY
    args = [(grids, pltpu.SMEM)]
    args += [(a, V) for a in (gain, wstep, taps, bias, step, skip, decay, wstate)]
    args += [(a, H) for a in (wout, cot, tokens, wx, wz)]
    outs = (
        (sds((HALF, width), bf16), H),
        (sds((HALF, width), f32), V),
        (sds((cols, width // 2), bf16), H),
        (sds((reps - 1, cols, width // 2), bf16), H),
        (sds((cols, width // 2), bf16), H),
        (sds((reps - 1, cols, width // 2), bf16), H),
        (sds((ZS, hp, ch), bf16), H),
        (sds((ZS, hp, ch), bf16), H),
        (sds((SMALL_ROWS, cols), f32), H),
        (sds((reps - 1, SMALL_ROWS, cols), bf16), H),
        (sds((cols, 128), f32), H),
        (sds((reps - 1, cols, 128), bf16), H),
        (sds((1, width), f32), V),
    )
    big = V((rows, ch), f32)
    padded = V((rows + 2 * PAD, ch), f32)
    part = V((rows, 128), f32)
    low = V((half, ch), bf16)
    round_rows = V((size, ch), f32)
    state = V((STATE, 8, ch), f32)
    scratch = (
        V((reps, TP, 16, 128), bf16),
        V((1, width), f32),
        V((2, 8, 128), f32),
        V((reps, cols, width), bf16),
        V((ch, width), bf16),
        V((reps, cols, width), bf16),
        V((ch, width), bf16),
        V((reps, SMALL_ROWS, cols), bf16),
        V((SMALL_ROWS, ch), bf16),
        V((reps, cols, 128), bf16),
        V((ch, 128), bf16),
        V((TP, piece, ch), bf16),
        V((TP, piece, ch), bf16),
        V((reps, TP, piece, ch), bf16),
        V((width, ch), bf16),
        V((2, ZS, 2, HALF, width), bf16),
        V((2, half, width), bf16),
        V((half, ch), f32),
        padded,
        padded,
        big,
        V((half, ch), f32),
        part,
        V((rows, 128), bf16),
        part,
        V((PACK, STATE // 2, 16, ch), bf16),
        big,
        round_rows,
        round_rows,
        state,
        state,
        V((STATE, ch), f32),
        round_rows,
        round_rows,
        V((size, STATE * 128), f32),
        V((size, STATE * 128), f32),
        V((STATE * 128, 128), bf16),
        V((8, ch), f32),
        V((8, ch), f32),
        big,
        low,
        low,
        low,
        low,
        low,
        V((2, half, ch), bf16),
        V((half, width), bf16),
        V((ZS, HALF, width), bf16),
        V((ZS, HALF, width), bf16),
        V((ZS - 1, HALF, width), bf16),
        V((HALF, width), bf16),
        V((HALF, width), bf16),
        V((piece, TP * ch), bf16),
        V((HALF, width), bf16),
        V((reps, TP * piece, ch), bf16),
        V((reps - 1, TP * piece, ch), bf16),
        V((TP, piece, ch), bf16),
        V((TP, hp, ch), bf16),
        V((TP, hp, ch), bf16),
        V((reps, cols, width // 2), bf16),
        part,
        V((rows, 128), bf16),
        V((TAPS + 1, 8, ch), f32),
        V((2, half, ch), bf16),
        V((2, half, ch), bf16),
        V((reps, cols, width // 2), bf16),
        V((SMALL_ROWS, ch), f32),
        V((reps, SMALL_ROWS, cols), f32),
        V((reps, cols, 128), f32),
        V((reps, SMALL_ROWS, cols), bf16),
        V((reps, cols, 128), bf16),
        V((6, 1, width), f32),
        V((3 + reps, 1, width), f32),
    ) + REDUCE_SCRATCH * 4
    copies = 160 + 12 * (reps - 1)
    return fused(partial(block_kernel, reps), 1, copies, 16, outs, args, scratch)


def place_kernel(
    reps, mixed_in, tokens_in, wx_mine, wx_theirs, wz_mine, wz_theirs, out_mine, out_theirs,
    rows_mine, rows_theirs, state_mine, state_theirs, gain_in,
    mixed, grad_tokens, gain, wx, wz, wout, taps, bias, wstate, wstep, step, decay, skip,
):
    mixed[...] = mixed_in[...]
    grad_tokens[...] = tokens_in[...]
    width, n = gain_in.shape[1], gain.shape[1]
    s = lax.axis_index("dir")
    index = s * (TP * reps) + lax.axis_index("dp")
    moved = pltpu.roll(jnp.broadcast_to(gain_in[...], (8, width)), width - index * n, 1)
    gain[...] = moved[0:1, 0:n]

    def total(mine, theirs):
        value = mine[...].astype(f32)
        for d in range(reps - 1):
            value = value + theirs[d].astype(f32)
        return value

    wx[...] = total(wx_mine, wx_theirs)
    wz[...] = total(wz_mine, wz_theirs)
    cols = wx.shape[0]
    hp = out_mine.shape[1]
    share = hp < wout.shape[0]
    for q in range(ZS):
        parts = [(out_mine[q].astype(f32), s), (out_theirs[q].astype(f32), 1 - s)]
        if not share:
            parts = [(parts[0][0] + parts[1][0], 0)]
        for value, place in parts:
            for r in range(reps):
                at = ((q // 2) * reps + r) * 2 + q % 2
                rows = pl.ds(pl.multiple_of(place * hp, hp), hp) if share else pl.ds(0, hp)
                wout[rows, at * cols : (at + 1) * cols] = value[:, r * cols : (r + 1) * cols]
    rows = total(rows_mine, rows_theirs)
    wstep[...] = rows[0:DT_RANK]
    taps[...] = rows[TAP_ROW : TAP_ROW + TAPS]
    bias[...] = rows[BIAS_ROW : BIAS_ROW + 1]
    step[...] = rows[STEP_ROW : STEP_ROW + 1]
    skip[...] = rows[SKIP_ROW : SKIP_ROW + 1]
    decay[...] = rows[DECAY_ROW : DECAY_ROW + STATE]
    wstate[...] = total(state_mine, state_theirs)


def place(reps, results):
    mixed, grad_tokens, wx = results[0], results[1], results[2]
    ch = results[6].shape[2]
    cols = wx.shape[0]
    width = mixed.shape[1]
    piece = width // (TP * reps)
    sds = jax.ShapeDtypeStruct
    V = pl.BlockSpec(memory_space=pltpu.VMEM)
    outs = (
        sds(mixed.shape, bf16),
        sds(grad_tokens.shape, f32),
        sds((1, width // (2 * TP * reps)), f32),
        sds(wx.shape, f32),
        sds(wx.shape, f32),
        sds((piece, ZS * ch), f32),
        sds((TAPS, cols), f32),
        sds((1, cols), f32),
        sds((cols, 128), f32),
        sds((DT_RANK, cols), f32),
        sds((1, cols), f32),
        sds((STATE, cols), f32),
        sds((1, cols), f32),
    )
    return pl.pallas_call(
        partial(place_kernel, reps),
        out_shape=outs,
        in_specs=[V] * len(results),
        out_specs=tuple([V] * len(outs)),
        compiler_params=pltpu.CompilerParams(vmem_limit_bytes=63 << 20),
    )(*results)


def local(
    reps, tokens, item_grids, norm_gain, proj_in_x, proj_in_z, proj_out, conv_weight, conv_bias,
    proj_state, proj_step, step_bias, decay_log, skip_gain, grad_out,
):
    width = tokens.shape[1]
    results = block(
        reps, item_grids, norm_gain[None], proj_step[0], conv_weight[0], conv_bias, step_bias, skip_gain,
        decay_log[0], proj_state[0], proj_out.T, grad_out.reshape(HALF, width), tokens, proj_in_x.T,
        proj_in_z.T,
    )
    (
        mixed, grad_tokens, grad_gain, grad_wx, grad_wz, grad_wout, grad_taps, grad_bias, grad_wstate,
        grad_wstep, grad_step, grad_decay, grad_skip,
    ) = place(reps, results)
    return (
        mixed.reshape(1, 1, HALF, width),
        grad_tokens.reshape(1, 1, HALF, width),
        grad_gain[0],
        grad_wx.T,
        grad_wz.T,
        grad_wout.T,
        grad_taps[None],
        grad_bias,
        grad_wstate[None],
        grad_wstep[None],
        grad_step,
        grad_decay[None],
        grad_skip,
    )


def solution(mesh):
    reps = mesh.shape["dp"] // TP
    return jax.shard_map(
        partial(local, reps),
        mesh=mesh,
        in_specs=(
            P("dp", None),
            P("dp", None),
            P("dp"),
            P(None, "dp"),
            P(None, "dp"),
            P(None, "dp"),
            P("dir", None, "dp"),
            P("dir", "dp"),
            P("dir", "dp", None),
            P("dir", None, "dp"),
            P("dir", "dp"),
            P("dir", None, "dp"),
            P("dir", "dp"),
            P("dp", "dir", None, None),
        ),
        out_specs=(
            P("dp", "dir", None, None),
            P("dp", "dir", None, None),
            P(("dir", "dp")),
            P("dir", "dp"),
            P("dir", "dp"),
            P("dir", "dp"),
            P("dir", None, "dp"),
            P("dir", "dp"),
            P("dir", "dp", None),
            P("dir", None, "dp"),
            P("dir", "dp"),
            P("dir", None, "dp"),
            P("dir", "dp"),
        ),
        check_vma=False,
    )
```

```python
from functools import partial

import jax
import jax.numpy as jnp
from jax import lax
from jax.experimental import pallas as pl
from jax.experimental.pallas import tpu as pltpu
from jax.sharding import PartitionSpec as P

f32 = jnp.float32
bf16 = jnp.bfloat16
EPS = 1e-05
DT_RANK = 96
STATE = 16
TAPS = 4
ZS = 4
TP = 8
PACK = 128
HALF = 64
CHUNK = 16
NSTEP = 4
LOG2E = 1.4426950408889634
LN2 = 0.6931471805599453
BIG = 1e9
PAD = 24
TAP_ROW, BIAS_ROW, STEP_ROW, SKIP_ROW, DECAY_ROW, SMALL_ROWS = 96, 100, 101, 102, 103, 128


def mm(left, right):
    return jnp.dot(left, right, preferred_element_type=f32)


def mm_nt(left, right):
    return lax.dot_general(left, right, (((1,), (1,)), ((), ())), preferred_element_type=f32)


def mm_tn(left, right):
    return lax.dot_general(left, right, (((0,), (0,)), ((), ())), preferred_element_type=f32)


def segment_of(t, ends):
    t = t.astype(f32) if hasattr(t, "astype") else float(t)
    return (t >= ends[0]).astype(f32) + (t >= ends[1]).astype(f32)


def rows8(t):
    return pl.ds(pl.multiple_of(t * 8, 8), 8)


def span(start, size):
    return pl.ds(pl.multiple_of(start * size, size), size)


def sigmoid(v):
    return 1.0 / (1.0 + jnp.exp(-v))


def softplus(v):
    return jnp.maximum(v, 0.0) + jnp.log1p(jnp.exp(-jnp.abs(v)))


def wide(mask, ch):
    return jnp.concatenate([mask] * (ch // 128), axis=1)


def tiles(v):
    total = v[:, 0:128]
    for at in range(128, v.shape[1], 128):
        total = total + v[:, at : at + 128]
    return total


class Copy:
    def __init__(self, copy):
        self.copy, self.sent, self.got = copy, False, False
        copy.start()

    def wait_send(self):
        if not self.sent:
            self.copy.wait_send()
            self.sent = True

    def wait_recv(self):
        if not self.got:
            self.copy.wait_recv()
            self.got = True


class Net:
    def __init__(self, reps, send, recv, local):
        self.reps, self.send, self.recv, self.local = reps, send, recv, local
        self.s = lax.axis_index("dir")
        p = lax.axis_index("dp")
        self.i = lax.rem(p, 2)
        self.y = lax.rem(p // 2, reps)
        self.z = p // (2 * reps)
        self.used = 0
        self.moved = 0
        self.copies = []
        self.saves = []

    def place(self, s, z, y, i):
        return (s, (z * self.reps + y) * 2 + i)

    def flip(self, m):
        if m == 1:
            return self.z + 1 - 2 * lax.rem(self.z, 2)
        if m == 2:
            return lax.rem(self.z + 2, ZS)
        return ZS - 1 - self.z

    def over_x(self):
        return self.place(1 - self.s, self.z, self.y, self.i)

    def sibling(self):
        return self.place(self.s, self.z, self.y, 1 - self.i)

    def along_z(self, m):
        return self.place(self.s, self.flip(m), self.y, self.i)

    def shared(self, m):
        z = self.flip(m // 2) if m // 2 else self.z
        i = 1 - self.i if m % 2 else self.i
        return z, i

    def to_shared(self, m):
        z, i = self.shared(m)
        return self.place(self.s, z, self.y, i)

    def y_at(self, d):
        return lax.rem(self.y + d, self.reps)

    def along_y(self, d):
        return self.place(self.s, self.z, self.y_at(d), self.i)

    def greet(self):
        self.peers = [self.over_x()] + [self.to_shared(m) for m in range(1, TP)]
        self.peers += [self.along_y(d) for d in range(1, self.reps)]
        barrier = pltpu.get_barrier_semaphore()
        for peer in self.peers:
            pl.semaphore_signal(barrier, inc=1, device_id=peer, device_id_type=pl.DeviceIdType.MESH)

    def met(self):
        pl.semaphore_wait(pltpu.get_barrier_semaphore(), len(self.peers))

    def copy(self, source, target, peer):
        k = self.used
        self.used += 1
        c = Copy(
            pltpu.make_async_remote_copy(
                src_ref=source,
                dst_ref=target,
                send_sem=self.send.at[k],
                recv_sem=self.recv.at[k],
                device_id=peer,
                device_id_type=pl.DeviceIdType.MESH,
            )
        )
        self.copies.append(c)
        return c

    def gather_z(self, source, at):
        c = ZGather(self, source, at)
        self.copies.append(c)
        return c

    def load(self, source, target):
        c = pltpu.make_async_copy(source, target, self.local.at[self.moved])
        self.moved += 1
        c.start()
        return c

    def save(self, source, target):
        self.saves.append(self.load(source, target))

    def finish(self):
        for c in self.copies:
            c.wait_recv()
            c.wait_send()
        for c in self.saves:
            c.wait()


class ZGather:
    def __init__(self, net, source, at):
        self.net, self.at = net, at
        self.near = [net.copy(source, at(net.z), net.along_z(m)) for m in (1, 2)]
        self.inner = lax.rem(net.z + 1, ZS) >= 2
        k = net.used
        net.used += 2
        self.direct = self.make(source, at(net.z), k, k, 3)
        far = at(net.flip(2))
        self.onward = self.make(far, far, k + 1, k, 1)
        self.got = False

        @pl.when(self.inner)
        def _():
            self.direct.start()

    def make(self, source, target, out, arrival, m):
        return pltpu.make_async_remote_copy(
            src_ref=source,
            dst_ref=target,
            send_sem=self.net.send.at[out],
            recv_sem=self.net.recv.at[arrival],
            device_id=self.net.along_z(m),
            device_id_type=pl.DeviceIdType.MESH,
        )

    def wait(self, m):
        if m < 3:
            self.near[m - 1].wait_recv()
            if m == 2:

                @pl.when(self.inner)
                def _():
                    self.onward.start()

        elif not self.got:
            self.direct.wait_recv()
            self.got = True
        return self.at(self.net.flip(m))

    def wait_recv(self):
        pass

    def wait_send(self):
        @pl.when(self.inner)
        def _():
            self.direct.wait_send()
            self.onward.wait_send()


class Reduce:
    def __init__(self, net, part, base, size, fold, out_low, in_low, total):
        self.net, self.part, self.base = net, part, base
        self.fold, self.out_low, self.in_low, self.total = fold, out_low, in_low, total
        self.rows = size // 2
        self.block = self.rows // ZS
        self.first = net.copy(part.at[self.at(1 - net.i, self.rows)], fold, net.sibling())

    def at(self, n, size):
        return pl.ds(pl.multiple_of(self.base + n * size, size), size)

    def across_z(self):
        net, fold = self.net, self.fold
        self.first.wait_recv()
        fold[...] = self.part[self.at(net.i, self.rows), :] + fold[...]
        self.out_low[...] = fold[...].astype(bf16).reshape(ZS, self.block, 128)
        self.cs = [
            net.copy(self.out_low.at[net.flip(m)], self.in_low.at[m - 1], net.along_z(m))
            for m in range(1, ZS)
        ]

    def give(self):
        net, total = self.net, self.total
        mine = self.at(net.i * ZS + net.z, self.block)
        value = self.fold[span(net.z, self.block), :]
        for m in range(1, ZS):
            self.cs[m - 1].wait_recv()
            value = value + self.in_low[m - 1].astype(f32)
        total[mine, :] = value.astype(bf16)
        self.cs = [net.copy(total.at[mine], total.at[mine], net.along_z(m)) for m in range(1, ZS)]
        self.ds = [net.copy(total.at[mine], total.at[mine], net.sibling())]

    def end(self):
        net, total = self.net, self.total
        for m in range(1, ZS):
            self.cs[m - 1].wait_recv()
            there = self.at(net.i * ZS + net.flip(m), self.block)
            self.ds.append(net.copy(total.at[there], total.at[there], net.sibling()))
        for d in self.ds:
            d.wait_recv()


REDUCE_ROWS = TP * HALF
REDUCE_SCRATCH = (
    pltpu.VMEM((REDUCE_ROWS // 2, 128), f32),
    pltpu.VMEM((ZS, REDUCE_ROWS // 2 // ZS, 128), bf16),
    pltpu.VMEM((ZS - 1, REDUCE_ROWS // 2 // ZS, 128), bf16),
)


def fused(kernel, name_id, copies, moves, outs, args, scratch):
    return pl.pallas_call(
        kernel,
        out_shape=tuple(o for o, _ in outs),
        in_specs=[pl.BlockSpec(memory_space=m) for _, m in args],
        out_specs=tuple(pl.BlockSpec(memory_space=m) for _, m in outs),
        scratch_shapes=list(scratch)
        + [pltpu.SemaphoreType.DMA((n,)) for n in (copies, copies, moves)],
        compiler_params=pltpu.CompilerParams(
            collective_id=name_id, has_side_effects=True, vmem_limit_bytes=63 << 20
        ),
    )(*(a for a, _ in args))


def block_kernel(reps, *refs):
    refs = list(refs)

    def take_refs(n):
        out = refs[:n]
        del refs[:n]
        return out

    (
        grids, gain_own, wstep_own, taps_own, bias_own, step_own, skip_own, decay_own, wstate_own, wout_hbm,
        cot_hbm, tokens, wx_own, wz_own,
    ) = take_refs(14)
    (
        mixed, grad_tokens, wx_mine, wx_theirs, wz_mine, wz_theirs, out_mine, out_theirs, rows_mine,
        rows_theirs, state_mine, state_theirs, grad_gain,
    ) = take_refs(13)
    (
        meta_all, gain, ends_ref, wx_all, wx, wz_all, wz, small_all, small, wstate_all, wstate,
        wout_send, wout_in, wout_all, wout,
    ) = take_refs(15)
    (tok, normed, raw, conv_in, conv_pre, conv_out, gate_in, part, proj_low, proj) = take_refs(10)
    (
        hprev, step, decay_step, u, state, acc_ref, rate_ref, s1, s2, pb, pc, ones, bias_acc, skip_acc, g,
    ) = take_refs(15)
    (y_send, y_in, g_send, g_in, gated, gate_both, cot, mixed_core, mixed_low, mixed_z, mixed_sum, tok_last, wout_own, cot_own) = take_refs(14)
    (out_send, out_y, out_low, out_x_in, out_all, wz_low, part_back, grad_proj, sums, gx, gx_in) = take_refs(11)
    (wx_low, rows_grad, rows_part, state_part, rows_low, state_low, gain_acc, gain_in) = take_refs(8)
    reduces = [take_refs(3) for _ in range(4)]
    send, recv, local_sems = refs
    net = Net(reps, send, recv, local_sems)
    net.greet()
    s, z, yi, i = net.s, net.z, net.y, net.i
    sgn = 1 - 2 * s
    gh = 1 - s
    j = z * 2 + i
    cols, width = wx_own.shape
    ch = reps * cols
    piece = wout_hbm.shape[0]
    half = TP * HALF
    rounds = HALF // CHUNK
    size = CHUNK * 8
    share = piece % 32 == 0
    hp = piece // 2 if share else piece
    own_part = pl.ds(pl.multiple_of(s * hp, hp), hp) if share else pl.ds(0, piece)
    half_cols = pl.ds(pl.multiple_of(s * (width // 2), 128), width // 2)

    own_loads = [net.load(tokens.at[pl.ds(h * HALF, HALF)], tok.at[h, z, i]) for h in range(2)]
    own_loads += [net.load(wx_own, wx_all.at[yi]), net.load(wz_own, wz_all.at[yi])]
    own_loads += [net.load(wout_hbm, wout_own), net.load(cot_hbm, cot_own)]
    own_loads += [net.load(tokens.at[pl.ds(pl.multiple_of(gh * HALF, HALF), HALF)], tok_last)]
    first_end = (grids[0, 0] * grids[0, 1]).astype(f32)
    second_end = first_end + (grids[1, 0] * grids[1, 1]).astype(f32)
    row = lax.broadcasted_iota(jnp.int32, (16, 128), 0)
    gain_row = jnp.concatenate([gain_own[...].astype(f32), jnp.zeros((1, 128 - piece), f32)], axis=1)
    meta = jnp.where(row == 0, gain_row, jnp.where(row == 1, first_end, second_end))
    meta_all[yi, j] = meta.astype(bf16)
    small_rows = [ref[...].astype(f32) for ref in (wstep_own, taps_own, bias_own, step_own, skip_own, decay_own)]
    small_rows.append(jnp.zeros((SMALL_ROWS - DECAY_ROW - STATE, cols), f32))
    small_all[yi] = jnp.concatenate(small_rows, axis=0).astype(bf16)
    wstate_all[yi] = wstate_own[...]
    net.met()
    own_first = tokens.at[pl.ds(pl.multiple_of(s * HALF, HALF), HALF)]
    own_last = tokens.at[pl.ds(pl.multiple_of(gh * HALF, HALF), HALF)]
    from_z = net.gather_z(own_first, lambda zz: tok.at[s, zz, i])
    core_first = [net.copy(own_first, tok.at[s, z, i], net.sibling())]
    core_last = [net.copy(own_last, tok.at[gh, z, i], net.sibling())]
    metas = [net.copy(meta_all.at[yi, j], meta_all.at[yi, j], net.to_shared(m)) for m in range(1, TP)]
    first_y = []
    for d in range(1, reps):
        first_y.append(net.copy(wx_own, wx_all.at[yi], net.along_y(d)))
        for ref in (small_all, wstate_all):
            first_y.append(net.copy(ref.at[yi], ref.at[yi], net.along_y(d)))
    cot_mine = span(j, HALF)
    cot_x = net.copy(cot_hbm, cot.at[cot_mine], net.over_x())
    for c in metas:
        c.wait_recv()
    meta_y = [net.copy(meta_all.at[yi], meta_all.at[yi], net.along_y(d)) for d in range(1, reps)]
    late_y = [net.copy(wz_own, wz_all.at[yi], net.along_y(d)) for d in range(1, reps)]

    for ref in (conv_in, conv_pre):
        ref[0:PAD, :] = jnp.zeros((PAD, ch), f32)
        ref[PAD + 8 * PACK :, :] = jnp.zeros((PAD, ch), f32)
    for b in range(TP):
        both = meta_all[yi, b].astype(f32)
        ends_ref[0, b : b + 1, :] = both[1:2, :]
        ends_ref[1, b : b + 1, :] = both[2:3, :]
    source = lax.broadcasted_iota(jnp.int32, (STATE * 128, 128), 0) // 128
    target = lax.broadcasted_iota(jnp.int32, (STATE * 128, 128), 1)
    ones[...] = (target == DT_RANK + source).astype(f32).astype(bf16)
    rows_grad[...] = jnp.zeros_like(rows_grad)
    state[...] = jnp.zeros_like(state)
    for c in own_loads:
        c.wait()
    for p in range(TP * reps):
        zp, yp, ip = p // (2 * reps), (p // 2) % reps, p % 2
        wout_send[zp * 2 + ip, :, yp * cols : (yp + 1) * cols] = wout_own[:, p * cols : (p + 1) * cols]
    wout_in[j, own_part] = wout_send[j, own_part]

    from_x = []
    for m in range(1, ZS):
        there = from_z.wait(m)
        core_first.append(net.copy(there, there, net.sibling()))
        from_x.append(net.copy(there, there, net.over_x()))
    wout_z = []
    for m in range(1, TP):
        zm, im = net.shared(m)
        wout_z.append(net.copy(wout_send.at[zm * 2 + im, own_part], wout_in.at[j, own_part], net.to_shared(m)))
    cot_x.wait_recv()

    def gather_cot(part):
        rows = lambda zz: cot.at[span((zz * 2 + i) * 2 + part, HALF // 2)]
        return net.gather_z(rows(z), rows)

    def pass_cot(part, m):
        there = cot_zs[part].wait(m)
        cot_core.append(net.copy(there, there, net.sibling()))

    cot_zs = [gather_cot(0)]
    cot_core = [net.copy(cot.at[cot_mine], cot.at[cot_mine], net.sibling())]
    for c in meta_y + first_y:
        c.wait_recv()
    for p in range(TP * reps):
        zp, yp, ip = p // (2 * reps), (p // 2) % reps, p % 2
        gain[:, p * piece : (p + 1) * piece] = meta_all[yp, zp * 2 + ip].astype(f32)[0:1, 0:piece]
    for r in range(reps):
        wx[r * cols : (r + 1) * cols, :] = wx_all[r]
        small[:, r * cols : (r + 1) * cols] = small_all[r]
        wstate[r * cols : (r + 1) * cols, :] = wstate_all[r]
    for c in core_first:
        c.wait_recv()

    ends = (ends_ref[0], ends_ref[1])
    vectors = small[DT_RANK : DT_RANK + 16, :].astype(f32)
    taps = vectors[0 : TAPS + 1, :]
    step_bias = vectors[STEP_ROW - DT_RANK : STEP_ROW - DT_RANK + 1, :]
    skip = vectors[SKIP_ROW - DT_RANK : SKIP_ROW - DT_RANK + 1, :]

    def take(h):
        def one(q, carry):
            rows = span(q, PACK)
            x = tok[h, q].astype(f32).reshape(PACK, width)
            inv = lax.rsqrt(jnp.mean(x * x, axis=1, keepdims=True) + EPS)
            low = (x * inv * gain[...]).astype(bf16)
            normed[h, rows, :] = low
            raw[rows, :] = mm_nt(low, wx[...])
            return carry

        lax.fori_loop(0, ZS, one, 0)
        x = jnp.swapaxes(raw[...].reshape(8, HALF, ch), 0, 1).reshape(half, ch)
        conv_in[pl.ds(pl.multiple_of(PAD + h * half, 8), half), :] = x

    def convolve(h, sums):
        def one(k, carry):
            t = h * HALF + k
            seg = segment_of(t, ends)
            total = taps[4:5, :] + taps[3:4, :] * conv_in[rows8(t + 3), :]
            for n in range(1, TAPS):
                there = t - n * sgn
                same = wide((segment_of(there, ends) == seg).astype(f32), ch)
                total = total + taps[3 - n : 4 - n, :] * (conv_in[rows8(there + 3), :] * same)
            conv_pre[rows8(t + 3), :] = total
            act = total * sigmoid(total)
            conv_out[rows8(t), :] = act.astype(bf16).astype(f32)
            return carry

        lax.fori_loop(0, HALF, one, 0, unroll=4)
        rows = span(h, half)
        part[rows, :] = mm(conv_out[rows, :].astype(bf16), wstate[...])
        return Reduce(net, part, h * half, half, *sums, proj_low)

    take(s)
    sum_first = convolve(s, reduces[0])

    def last_tokens(m):
        from_x[m - 1].wait_recv()
        there = tok.at[gh, net.flip(m), i]
        core_last.append(net.copy(there, there, net.sibling()))

    last_tokens(1)
    sum_first.across_z()
    last_tokens(2)
    sum_first.give()
    cot_zs.append(gather_cot(1))
    last_tokens(3)
    for c in wout_z:
        c.wait_recv()
    wout_x = [net.copy(wout_in.at[:, own_part], wout_in.at[:, own_part], net.over_x())] if share else []
    pass_cot(0, 1)
    pass_cot(0, 2)
    for c in core_last:
        c.wait_recv()
    take(gh)
    sum_last = convolve(gh, reduces[1])
    sum_first.end()
    first_rows = span(s, half)
    last_rows = span(gh, half)
    proj[first_rows, :] = proj_low[first_rows, :].astype(f32)

    wstep = jnp.where(lax.broadcasted_iota(jnp.int32, (128, ch), 0) < DT_RANK, small[...], 0.0).astype(bf16)
    rate_ref[...] = -LOG2E * jnp.exp(small[DT_RANK:, :].astype(f32)[DECAY_ROW - DT_RANK : DECAY_ROW - DT_RANK + STATE, :])
    y = g

    def prepare(block, first):
        rows = span(block, size)
        pre = mm(proj_low[rows, :], wstep) + step_bias
        if first:
            step[rows, :] = softplus(pre)
        step_all = step[rows, :]
        values = conv_out[rows, :]
        u[...] = step_all * values
        for k in range(CHUNK):
            t = block * CHUNK + k
            fresh = segment_of(t, ends) != segment_of(t - sgn, ends)
            decay_step[8 * k : 8 * k + 8, :] = jnp.where(
                wide(fresh, ch), BIG, step_all[8 * k : 8 * k + 8, :]
            )
        return rows, pre, values

    def rates(n0):
        return [jnp.broadcast_to(rate_ref[n : n + 1, :], (8, ch)) for n in range(n0, n0 + NSTEP)]

    def forward(c, carry):
        block = c + s * (2 * rounds - 1 - 2 * c)
        rows, _, values = prepare(block, True)
        y[rows, :] = skip * values
        for n0 in range(0, STATE, NSTEP):
            rate = rates(n0)

            def body(k, hs):
                r = s * (CHUNK - 1 - k) + (1 - s) * k
                t = block * CHUNK + r
                pv = proj[rows8(t), :]
                st = decay_step[rows8(r), :]
                uv = u[rows8(r), :]
                total = y[rows8(t), :]
                new = []
                for m in range(NSTEP):
                    n = n0 + m
                    if m % 2 == 0:
                        hprev[t, n // 2] = jnp.concatenate([hs[m], hs[m + 1]], axis=0).astype(bf16)
                    h = jnp.exp2(st * rate[m]) * hs[m] + uv * pv[:, DT_RANK + n : DT_RANK + n + 1]
                    total = total + h * pv[:, DT_RANK + STATE + n : DT_RANK + STATE + n + 1]
                    new.append(h)
                y[rows8(t), :] = total
                return tuple(new)

            hs = lax.fori_loop(0, CHUNK, body, tuple(state[n] for n in range(n0, n0 + NSTEP)), unroll=CHUNK)
            for m in range(NSTEP):
                state[n0 + m] = hs[m]
        return carry

    def send_readout(n):
        at = n + s * (rounds - 1 - 2 * n)
        rows = span(at, size)
        y_send[rows, :] = y[span(s * rounds + at, size), :].astype(bf16)
        return net.copy(y_send.at[rows], y_in.at[rows], net.over_x())

    sum_last.across_z()
    for c in wout_x:
        c.wait_recv()
    wout_y = [net.copy(wout_in, wout_all.at[yi], net.along_y(d)) for d in range(1, reps)]
    wout_all[yi] = wout_in[...]
    lax.fori_loop(0, rounds // 2, forward, 0)
    sum_last.give()
    y_copies = [send_readout(n) for n in range(rounds // 2)]
    lax.fori_loop(rounds // 2, rounds, forward, 0)
    y_copies += [send_readout(n) for n in (rounds // 2, rounds - 1)]
    pass_cot(0, 3)
    sum_last.end()
    pass_cot(1, 1)
    pass_cot(1, 2)
    proj[last_rows, :] = proj_low[last_rows, :].astype(f32)
    for c in late_y:
        c.wait_recv()
    for r in range(reps):
        wz[r * cols : (r + 1) * cols, :] = wz_all[r]
    gate_in[...] = mm_nt(normed[gh], wz[...])
    lax.fori_loop(rounds, 2 * rounds - 1, forward, 0)
    lax.fori_loop(2 * rounds - 1, 2 * rounds, forward, 0)
    for c in wout_y:
        c.wait_recv()
    for p in range(TP * reps):
        zp, yp, ip = p // (2 * reps), (p // 2) % reps, p % 2
        wout[p * piece : (p + 1) * piece, :] = wout_all[yp, zp * 2 + ip]
    for c in y_copies:
        c.wait_recv()

    summed = y[last_rows, :] + y_in[...].astype(f32)
    raw[...] = jnp.swapaxes(summed.reshape(HALF, 8, ch), 0, 1).reshape(half, ch)

    def gate_rows(q, carry):
        rows = span(q, PACK)
        gate = gate_in[rows, :]
        low = (raw[rows, :] * (gate * sigmoid(gate))).astype(bf16)
        gated[rows, :] = low
        tok[gh, q] = mm_nt(low, wout[...]).astype(bf16).reshape(2, HALF, width)
        return carry

    def grad_rows(q, carry):
        rows = span(q, PACK)
        gate = gate_in[rows, :]
        sig = sigmoid(gate)
        grad_gated = mm(cot[rows, :], wout[...])
        gate_both[gh, rows, :] = (grad_gated * raw[rows, :] * sig * (1.0 + gate * (1.0 - sig))).astype(bf16)
        gate_in[rows, :] = grad_gated * (gate * sig)
        return carry

    for c in core_last:
        c.wait_send()
    lax.fori_loop(0, ZS, gate_rows, 0)
    mixed_copy = net.copy(tok.at[gh, :, 1 - i], mixed_core, net.sibling())
    pass_cot(1, 3)
    for c in cot_core:
        c.wait_recv()
    lax.fori_loop(0, ZS, grad_rows, 0)
    back = jnp.swapaxes(gate_in[...].reshape(8, HALF, ch), 0, 1).reshape(half, ch)
    g[last_rows, :] = back
    g_send[...] = back.astype(bf16)
    g_copy = net.copy(g_send, g_in, net.over_x())
    gate_copy = net.copy(gate_both.at[gh], gate_both.at[gh], net.over_x())
    mixed_copy.wait_recv()
    for q in range(ZS):
        mixed_low[q] = (tok[gh, q, i].astype(f32) + mixed_core[q].astype(f32)).astype(bf16)
    mixed_zs = [net.copy(mixed_low.at[net.flip(m)], mixed_z.at[m - 1], net.along_z(m)) for m in range(1, ZS)]

    state[...] = jnp.zeros_like(state)
    acc_ref[...] = jnp.zeros_like(acc_ref)
    bias_acc[...] = jnp.zeros_like(bias_acc)
    skip_acc[...] = jnp.zeros_like(skip_acc)

    def backward(c, carry):
        block = (1 - s) * (2 * rounds - 1 - c) + s * c
        rows, pre, values = prepare(block, False)
        s1[...] = jnp.zeros_like(s1)
        s2[...] = jnp.zeros_like(s2)
        for n0 in range(0, STATE, NSTEP):
            rate = rates(n0)

            def body(k, both):
                lams, accs = both
                r = s * k + (1 - s) * (CHUNK - 1 - k)
                t = block * CHUNK + r
                here = rows8(r)
                pv = proj[rows8(t), :]
                gv = g[rows8(t), :]
                uv = u[here, :]
                stv = step[rows8(t), :]
                st = decay_step[here, :]
                one = s1[here, :]
                two = s2[here, :]
                new_lams, new_accs = [], []
                for m in range(NSTEP):
                    n = n0 + m
                    if m % 2 == 0:
                        pair = hprev[t, n // 2].astype(f32)
                    a = jnp.exp2(st * rate[m])
                    ah = a * pair[8 * (m % 2) : 8 * (m % 2) + 8]
                    lam = gv * pv[:, DT_RANK + STATE + n : DT_RANK + STATE + n + 1] + lams[m]
                    w = lam * ah
                    new_lams.append(a * lam)
                    two = two + rate[m] * w
                    new_accs.append(accs[m] + stv * w)
                    one = one + lam * pv[:, DT_RANK + n : DT_RANK + n + 1]
                    pb[here, 128 * n : 128 * n + 128] = tiles(lam * uv)
                    pc[here, 128 * n : 128 * n + 128] = tiles(gv * ah)
                s1[here, :] = one
                s2[here, :] = two
                return tuple(new_lams), tuple(new_accs)

            first = (
                tuple(state[n] for n in range(n0, n0 + NSTEP)),
                tuple(acc_ref[n] for n in range(n0, n0 + NSTEP)),
            )
            lams, accs = lax.fori_loop(0, CHUNK, body, first, unroll=CHUNK)
            for m in range(NSTEP):
                state[n0 + m] = lams[m]
                acc_ref[n0 + m] = accs[m]
        gv = g[rows, :]
        one = s1[...]
        q = (LN2 * s2[...] + values * one) * sigmoid(pre)
        q_low = q.astype(bf16)
        bias_acc[...] += jnp.sum(q.reshape(CHUNK, 8, ch), axis=0)
        skip_acc[...] += jnp.sum((gv * values).reshape(CHUNK, 8, ch), axis=0)
        rows_grad[0:DT_RANK, :] += mm_tn(proj_low[rows, :], q_low)[0:DT_RANK, :]
        gu = jnp.sum(gv * u[...], axis=1, keepdims=True)
        lane = lax.broadcasted_iota(jnp.int32, (size, 128), 1)
        read_part = mm(pc[...].astype(bf16), ones[...]) + gu * jnp.where(
            lane < DT_RANK + STATE, proj[rows, :], 0.0
        )
        read_part = jnp.where(lane >= DT_RANK + STATE, pltpu.roll(read_part, STATE, 1), 0.0)
        part_back[rows, :] = mm_nt(q_low, wstep) + mm(pb[...].astype(bf16), ones[...]) + read_part
        g[rows, :] = gv * skip + step[rows, :] * one
        return carry

    lax.fori_loop(0, 1, backward, 0)
    quarter = width // ZS
    for q in range(ZS):
        value = mm_tn(cot[:, q * quarter : (q + 1) * quarter], gated[...]).astype(bf16)
        for r in range(reps):
            out_send[r, q * 2 * piece : (q + 1) * 2 * piece, :] = value[r * 2 * piece : (r + 1) * 2 * piece, :]
    out_copies = [
        net.copy(out_send.at[net.y_at(d)], out_y.at[d - 1], net.along_y(d)) for d in range(1, reps)
    ]
    lax.fori_loop(1, rounds, backward, 0)
    back_last = Reduce(net, part_back, gh * half, half, *reduces[2], grad_proj)
    g_copy.wait_recv()
    g[first_rows, :] = g_in[...].astype(f32)
    lax.fori_loop(rounds, rounds + 1, backward, 0)
    for c in out_copies:
        c.wait_recv()
    total = out_send[yi].astype(f32)
    for d in range(1, reps):
        total = total + out_y[d - 1].astype(f32)
    total = total.astype(bf16)
    for q in range(TP):
        out_low[q] = total[q * piece : (q + 1) * piece]
    if share:
        other_part = pl.ds(pl.multiple_of(gh * hp, hp), hp)
        out_x = net.copy(out_low.at[:, other_part], out_x_in, net.over_x())
    back_last.across_z()
    lax.fori_loop(rounds + 1, 2 * rounds - 1, backward, 0)
    back_last.give()
    lax.fori_loop(2 * rounds - 1, 2 * rounds, backward, 0)
    back_first = Reduce(net, part_back, s * half, half, *reduces[3], grad_proj)
    back_last.end()

    w = conv_pre
    sums[...] = jnp.zeros_like(sums)

    def pull(h):
        def one(b, carry):
            at = h * half + b * PACK
            rows = pl.ds(pl.multiple_of(PAD + at, 8), PACK)
            at = pl.ds(pl.multiple_of(at, PACK), PACK)
            c = conv_pre[rows, :]
            sig = sigmoid(c)
            w[rows, :] = (g[at, :] + mm_nt(grad_proj[at, :], wstate[...])) * (sig * (1.0 + c * (1.0 - sig)))
            return carry

        lax.fori_loop(0, half // PACK, one, 0)

    def convolve_back(h):
        def one(k, carry):
            t = h * HALF + k
            seg = segment_of(t, ends)
            here = w[rows8(t + 3), :]
            total = taps[3:4, :] * here
            new = [carry[3] + here * conv_in[rows8(t + 3), :], carry[4] + here]
            first = []
            for n in range(1, TAPS):
                back = t - n * sgn
                ahead = t + n * sgn
                same_back = wide((segment_of(back, ends) == seg).astype(f32), ch)
                same_ahead = wide((segment_of(ahead, ends) == seg).astype(f32), ch)
                first.insert(0, carry[3 - n] + here * (conv_in[rows8(back + 3), :] * same_back))
                total = total + taps[3 - n : 4 - n, :] * (w[rows8(ahead + 3), :] * same_ahead)
            raw[rows8(k), :] = total
            return tuple(first + new)

        carry = lax.fori_loop(0, HALF, one, tuple(sums[n] for n in range(TAPS + 1)), unroll=4)
        for n in range(TAPS + 1):
            sums[n] = carry[n]
        gx[h] = jnp.swapaxes(raw[...].reshape(HALF, 8, ch), 0, 1).reshape(half, ch).astype(bf16)
        return net.copy(gx.at[h], gx_in.at[h], net.over_x())

    pull(gh)
    back_first.across_z()
    gx_last = convolve_back(gh)
    for c in mixed_zs:
        c.wait_recv()
    total = tok[gh, z, i].astype(f32) + mixed_core[z].astype(f32)
    for m in range(1, ZS):
        total = total + mixed_z[m - 1].astype(f32)
    mixed_sum[...] = (total + tok_last[...].astype(f32)).astype(bf16)
    net.copy(mixed_sum, mixed, net.over_x())
    back_first.give()
    out_half = out_low
    if share:
        out_x.wait_recv()
        out_half = out_x_in
        out_half[...] = (out_low[:, own_part].astype(f32) + out_x_in[...].astype(f32)).astype(bf16)
    out_all[j] = out_half[j]
    out_zs = []
    for m in range(1, TP):
        zm, im = net.shared(m)
        out_zs.append(net.copy(out_half.at[zm * 2 + im], out_all.at[j], net.to_shared(m)))
    gate_copy.wait_recv()
    part_z = mm_tn(gate_both[0], normed[0, :, half_cols]) + mm_tn(gate_both[1], normed[1, :, half_cols])
    for r in range(reps):
        wz_low[r] = part_z[r * cols : (r + 1) * cols].astype(bf16)
    for d in range(1, reps):
        net.copy(wz_low.at[net.y_at(d)], wz_theirs.at[d - 1], net.along_y(d))
    net.save(wz_low.at[yi], wz_mine)
    back_first.end()
    pull(s)
    gx_first = convolve_back(s)

    def rows_of(q):
        rows = span(q, PACK)
        both = gx[s, rows, :].astype(f32) + gx_in[s, rows, :].astype(f32)
        value = (
            mm(both.astype(bf16), wx[...]) + mm(gate_both[s, rows, :], wz[...])
        )
        tok[gh, q] = value.astype(bf16).reshape(2, HALF, width)
        return net.copy(tok.at[gh, q, 1 - i], mixed_core.at[q], net.sibling())

    def send_on(m, c):
        q = net.flip(m)
        c.wait_recv()
        mixed_low[q] = (tok[gh, q, i].astype(f32) + mixed_core[q].astype(f32)).astype(bf16)
        to_z.append(net.copy(mixed_low.at[q], mixed_z.at[m - 1], net.along_z(m)))

    mixed_copy.wait_send()
    for c in mixed_zs:
        c.wait_send()
    gx_last.wait_recv()
    to_z = []
    far = rows_of(net.flip(2))
    middle = rows_of(net.flip(3))
    send_on(2, far)
    near = rows_of(net.flip(1))
    send_on(3, middle)
    to_core = rows_of(z)
    send_on(1, near)
    def gain_terms(q, carry):
        x = tok[s, q].astype(f32).reshape(PACK, width)
        inv = lax.rsqrt(jnp.mean(x * x, axis=1, keepdims=True) + EPS)
        terms = tok[gh, q].astype(f32).reshape(PACK, width) * (x * inv)
        return carry + jnp.sum(terms.reshape(PACK // 8, 8, width), axis=0)

    gain_acc[0] = jnp.sum(lax.fori_loop(0, ZS, gain_terms, jnp.zeros((8, width), f32)), axis=0, keepdims=True)
    stages = [
        [net.along_y(d) for d in range(1, reps)],
        [net.sibling()],
        [net.over_x()],
        [net.along_z(1)],
        [net.along_z(2)],
    ]
    slot = [0]

    def gain_start(k):
        cs = []
        for peer in stages[k]:
            cs.append((slot[0], net.copy(gain_acc.at[k], gain_in.at[slot[0]], peer)))
            slot[0] += 1
        return cs

    def gain_end(k, cs):
        total = gain_acc[k]
        for at, c in cs:
            c.wait_recv()
            total = total + gain_in[at]
        gain_acc[k + 1] = total

    cs = gain_start(0)
    state_all = mm_tn(conv_out[...].astype(bf16), grad_proj[...])
    rows_grad[STEP_ROW : STEP_ROW + 1, :] = jnp.sum(bias_acc[...], axis=0, keepdims=True)
    rows_grad[SKIP_ROW : SKIP_ROW + 1, :] = jnp.sum(skip_acc[...], axis=0, keepdims=True)
    for n in range(STATE):
        rows_grad[DECAY_ROW + n : DECAY_ROW + n + 1, :] = (
            jnp.sum(acc_ref[n], axis=0, keepdims=True) * rate_ref[n : n + 1, :] * LN2
        )
    for n in range(TAPS + 1):
        rows_grad[TAP_ROW + n : TAP_ROW + n + 1, :] = jnp.sum(sums[n], axis=0, keepdims=True)
    for r in range(reps):
        state_part[r] = state_all[r * cols : (r + 1) * cols, :]
        rows_part[r] = rows_grad[:, r * cols : (r + 1) * cols]
    for r in range(reps):
        state_low[r] = state_part[r].astype(bf16)
        rows_low[r] = rows_part[r].astype(bf16)
    for d in range(1, reps):
        net.copy(state_low.at[net.y_at(d)], state_theirs.at[d - 1], net.along_y(d))
        net.copy(rows_low.at[net.y_at(d)], rows_theirs.at[d - 1], net.along_y(d))
    net.save(state_part.at[yi], state_mine)
    net.save(rows_part.at[yi], rows_mine)
    gain_end(0, cs)
    cs = gain_start(1)
    gx_first.wait_recv()
    part_x = mm_tn(gx[0], normed[0, :, half_cols]) + mm_tn(gx[1], normed[1, :, half_cols])
    part_x = part_x + mm_tn(gx_in[0], normed[0, :, half_cols]) + mm_tn(gx_in[1], normed[1, :, half_cols])
    for r in range(reps):
        wx_low[r] = part_x[r * cols : (r + 1) * cols].astype(bf16)
    for d in range(1, reps):
        net.copy(wx_low.at[net.y_at(d)], wx_theirs.at[d - 1], net.along_y(d))
    net.save(wx_low.at[yi], wx_mine)
    gain_end(1, cs)
    cs = gain_start(2)
    for c in out_zs:
        c.wait_recv()
    net.copy(out_all.at[pl.ds(gh * ZS, ZS)], out_theirs, net.over_x())
    net.save(out_all.at[pl.ds(s * ZS, ZS)], out_mine)
    gain_end(2, cs)
    cs = gain_start(3)
    x = tok[s, z, i].astype(f32)
    inv = lax.rsqrt(jnp.mean(x * x, axis=1, keepdims=True) + EPS)
    unit = x * inv
    gain_end(3, cs)
    cs = gain_start(4)
    to_core.wait_recv()
    grad = tok[gh, z, i].astype(f32) + mixed_core[z].astype(f32)
    for c in to_z:
        c.wait_recv()
    for m in range(1, ZS):
        grad = grad + mixed_z[m - 1].astype(f32)
    scaled = grad * gain[...]
    mean = jnp.mean(scaled * unit, axis=1, keepdims=True)
    grad_tokens[...] = inv * (scaled - unit * mean) + cot_own[...].astype(f32)
    gain_end(4, cs)
    grad_gain[...] = gain_acc[5]
    net.finish()


def block(reps, grids, gain, wstep, taps, bias, step, skip, decay, wstate, wout, cot, tokens, wx, wz):
    cols, width = wx.shape
    ch = reps * cols
    rows = TP * PACK
    half = rows // 2
    piece = wout.shape[0]
    hp = piece // 2 if piece % 32 == 0 else piece
    size = CHUNK * 8
    sds = jax.ShapeDtypeStruct
    V, H = pltpu.VMEM, pl.ANY
    args = [(grids, pltpu.SMEM)]
    args += [(a, V) for a in (gain, wstep, taps, bias, step, skip, decay, wstate)]
    args += [(a, H) for a in (wout, cot, tokens, wx, wz)]
    outs = (
        (sds((HALF, width), bf16), H),
        (sds((HALF, width), f32), V),
        (sds((cols, width // 2), bf16), H),
        (sds((reps - 1, cols, width // 2), bf16), H),
        (sds((cols, width // 2), bf16), H),
        (sds((reps - 1, cols, width // 2), bf16), H),
        (sds((ZS, hp, ch), bf16), H),
        (sds((ZS, hp, ch), bf16), H),
        (sds((SMALL_ROWS, cols), f32), H),
        (sds((reps - 1, SMALL_ROWS, cols), bf16), H),
        (sds((cols, 128), f32), H),
        (sds((reps - 1, cols, 128), bf16), H),
        (sds((1, width), f32), V),
    )
    big = V((rows, ch), f32)
    padded = V((rows + 2 * PAD, ch), f32)
    part = V((rows, 128), f32)
    low = V((half, ch), bf16)
    round_rows = V((size, ch), f32)
    state = V((STATE, 8, ch), f32)
    scratch = (
        V((reps, TP, 16, 128), bf16),
        V((1, width), f32),
        V((2, 8, 128), f32),
        V((reps, cols, width), bf16),
        V((ch, width), bf16),
        V((reps, cols, width), bf16),
        V((ch, width), bf16),
        V((reps, SMALL_ROWS, cols), bf16),
        V((SMALL_ROWS, ch), bf16),
        V((reps, cols, 128), bf16),
        V((ch, 128), bf16),
        V((TP, piece, ch), bf16),
        V((TP, piece, ch), bf16),
        V((reps, TP, piece, ch), bf16),
        V((width, ch), bf16),
        V((2, ZS, 2, HALF, width), bf16),
        V((2, half, width), bf16),
        V((half, ch), f32),
        padded,
        padded,
        big,
        V((half, ch), f32),
        part,
        V((rows, 128), bf16),
        part,
        V((PACK, STATE // 2, 16, ch), bf16),
        big,
        round_rows,
        round_rows,
        state,
        state,
        V((STATE, ch), f32),
        round_rows,
        round_rows,
        V((size, STATE * 128), f32),
        V((size, STATE * 128), f32),
        V((STATE * 128, 128), bf16),
        V((8, ch), f32),
        V((8, ch), f32),
        big,
        low,
        low,
        low,
        low,
        low,
        V((2, half, ch), bf16),
        V((half, width), bf16),
        V((ZS, HALF, width), bf16),
        V((ZS, HALF, width), bf16),
        V((ZS - 1, HALF, width), bf16),
        V((HALF, width), bf16),
        V((HALF, width), bf16),
        V((piece, TP * ch), bf16),
        V((HALF, width), bf16),
        V((reps, TP * piece, ch), bf16),
        V((reps - 1, TP * piece, ch), bf16),
        V((TP, piece, ch), bf16),
        V((TP, hp, ch), bf16),
        V((TP, hp, ch), bf16),
        V((reps, cols, width // 2), bf16),
        part,
        V((rows, 128), bf16),
        V((TAPS + 1, 8, ch), f32),
        V((2, half, ch), bf16),
        V((2, half, ch), bf16),
        V((reps, cols, width // 2), bf16),
        V((SMALL_ROWS, ch), f32),
        V((reps, SMALL_ROWS, cols), f32),
        V((reps, cols, 128), f32),
        V((reps, SMALL_ROWS, cols), bf16),
        V((reps, cols, 128), bf16),
        V((6, 1, width), f32),
        V((3 + reps, 1, width), f32),
    ) + REDUCE_SCRATCH * 4
    copies = 160 + 12 * (reps - 1)
    return fused(partial(block_kernel, reps), 1, copies, 16, outs, args, scratch)


def place_kernel(
    reps, mixed_in, tokens_in, wx_mine, wx_theirs, wz_mine, wz_theirs, out_mine, out_theirs,
    rows_mine, rows_theirs, state_mine, state_theirs, gain_in,
    mixed, grad_tokens, gain, wx, wz, wout, taps, bias, wstate, wstep, step, decay, skip,
):
    mixed[...] = mixed_in[...]
    grad_tokens[...] = tokens_in[...]
    width, n = gain_in.shape[1], gain.shape[1]
    s = lax.axis_index("dir")
    index = s * (TP * reps) + lax.axis_index("dp")
    moved = pltpu.roll(jnp.broadcast_to(gain_in[...], (8, width)), width - index * n, 1)
    gain[...] = moved[0:1, 0:n]

    def total(mine, theirs):
        value = mine[...].astype(f32)
        for d in range(reps - 1):
            value = value + theirs[d].astype(f32)
        return value

    wx[...] = total(wx_mine, wx_theirs)
    wz[...] = total(wz_mine, wz_theirs)
    cols = wx.shape[0]
    hp = out_mine.shape[1]
    share = hp < wout.shape[0]
    for q in range(ZS):
        parts = [(out_mine[q].astype(f32), s), (out_theirs[q].astype(f32), 1 - s)]
        if not share:
            parts = [(parts[0][0] + parts[1][0], 0)]
        for value, place in parts:
            for r in range(reps):
                at = ((q // 2) * reps + r) * 2 + q % 2
                rows = pl.ds(pl.multiple_of(place * hp, hp), hp) if share else pl.ds(0, hp)
                wout[rows, at * cols : (at + 1) * cols] = value[:, r * cols : (r + 1) * cols]
    rows = total(rows_mine, rows_theirs)
    wstep[...] = rows[0:DT_RANK]
    taps[...] = rows[TAP_ROW : TAP_ROW + TAPS]
    bias[...] = rows[BIAS_ROW : BIAS_ROW + 1]
    step[...] = rows[STEP_ROW : STEP_ROW + 1]
    skip[...] = rows[SKIP_ROW : SKIP_ROW + 1]
    decay[...] = rows[DECAY_ROW : DECAY_ROW + STATE]
    wstate[...] = total(state_mine, state_theirs)


def place(reps, results):
    mixed, grad_tokens, wx = results[0], results[1], results[2]
    ch = results[6].shape[2]
    cols = wx.shape[0]
    width = mixed.shape[1]
    piece = width // (TP * reps)
    sds = jax.ShapeDtypeStruct
    V = pl.BlockSpec(memory_space=pltpu.VMEM)
    outs = (
        sds(mixed.shape, bf16),
        sds(grad_tokens.shape, f32),
        sds((1, width // (2 * TP * reps)), f32),
        sds(wx.shape, f32),
        sds(wx.shape, f32),
        sds((piece, ZS * ch), f32),
        sds((TAPS, cols), f32),
        sds((1, cols), f32),
        sds((cols, 128), f32),
        sds((DT_RANK, cols), f32),
        sds((1, cols), f32),
        sds((STATE, cols), f32),
        sds((1, cols), f32),
    )
    return pl.pallas_call(
        partial(place_kernel, reps),
        out_shape=outs,
        in_specs=[V] * len(results),
        out_specs=tuple([V] * len(outs)),
        compiler_params=pltpu.CompilerParams(vmem_limit_bytes=63 << 20),
    )(*results)


def local(
    reps, tokens, item_grids, norm_gain, proj_in_x, proj_in_z, proj_out, conv_weight, conv_bias,
    proj_state, proj_step, step_bias, decay_log, skip_gain, grad_out,
):
    width = tokens.shape[1]
    results = block(
        reps, item_grids, norm_gain[None], proj_step[0], conv_weight[0], conv_bias, step_bias, skip_gain,
        decay_log[0], proj_state[0], proj_out.T, grad_out.reshape(HALF, width), tokens, proj_in_x.T,
        proj_in_z.T,
    )
    (
        mixed, grad_tokens, grad_gain, grad_wx, grad_wz, grad_wout, grad_taps, grad_bias, grad_wstate,
        grad_wstep, grad_step, grad_decay, grad_skip,
    ) = place(reps, results)
    return (
        mixed.reshape(1, 1, HALF, width),
        grad_tokens.reshape(1, 1, HALF, width),
        grad_gain[0],
        grad_wx.T,
        grad_wz.T,
        grad_wout.T,
        grad_taps[None],
        grad_bias,
        grad_wstate[None],
        grad_wstep[None],
        grad_step,
        grad_decay[None],
        grad_skip,
    )


def solution(mesh):
    reps = mesh.shape["dp"] // TP
    return jax.shard_map(
        partial(local, reps),
        mesh=mesh,
        in_specs=(
            P("dp", None),
            P("dp", None),
            P("dp"),
            P(None, "dp"),
            P(None, "dp"),
            P(None, "dp"),
            P("dir", None, "dp"),
            P("dir", "dp"),
            P("dir", "dp", None),
            P("dir", None, "dp"),
            P("dir", "dp"),
            P("dir", None, "dp"),
            P("dir", "dp"),
            P("dp", "dir", None, None),
        ),
        out_specs=(
            P("dp", "dir", None, None),
            P("dp", "dir", None, None),
            P(("dir", "dp")),
            P("dir", "dp"),
            P("dir", "dp"),
            P("dir", "dp"),
            P("dir", None, "dp"),
            P("dir", "dp"),
            P("dir", "dp", None),
            P("dir", None, "dp"),
            P("dir", "dp"),
            P("dir", None, "dp"),
            P("dir", "dp"),
        ),
        check_vma=False,
    )
```
